256 devices in a mesh: gx: 64 (over y, x, z_lo, core), gy: 4 (over z_hi).
Axes of the slice: x: 4, y: 4, z: 8 (z_hi: 4, z_lo: 2; z = z_hi * 2 + z_lo), core: 2. Of those that a mesh axis runs over, the one named last changes fastest.
Arguments:
- fractions: float32 [3, 64, 8, 128], P(None, 'gx', 'gy'), may hold values from 0 to 1
- species: int32 [64, 8, 128], P('gx', 'gy'), may hold values from 0 to 89, as said below
- neighbours: int32 [64, 8, 16, 128], P('gx', 'gy'), may hold values from 0 to 1151, as said below
- embedding: float32 [89, 128], replicated, may hold values from -6 to 6
- up_weight: float32 [2, 128, 128], replicated, may hold values from -0.5 to 0.5
- radial_in: float32 [2, 8, 64], replicated, may hold values from -2 to 2
- radial_out: float32 [2, 64, 384], replicated, may hold values from -0.75 to 0.75
- self_weight: float32 [2, 128, 128], replicated, may hold values from -0.5 to 0.5
- product_weight: float32 [2, 384, 128], replicated, may hold values from -0.3125 to 0.3125
- readout: float32 [2, 128], replicated, may hold values from -0.5 to 0.5
Outputs:
- forces: float32 [3, 64, 8, 128], P(None, 'gx', 'gy')
- atom_energy: float32 [64, 8, 128], P('gx', 'gy')
- total_energy: float32 [], replicated
The draws below stay inside these ranges and needn't reach their ends.
Inputs may be any that keep to these rules, and one draw needn't show every extreme that they name: `species`: 0 marks an empty slot, other values name an element 1 .. 89; the share of filled slots grows from about 0.4 to 1 along the first bin dimension. `neighbours`: a code names a slot of one of the 3 x 3 bins around the atom's own bin as described in the reference program; codes may repeat; no atom names itself.
All inputs are finite; a program needn't handle non-finite values.
Results may differ from the reference program's by a relative error of at most 0.0003.
Values sent between devices are 32-bit elements; how exact they have to be, the bound alone decides.
A program may use at most 128 MiB of HBM per device.

```python
import math
import jax
import jax.numpy as jnp
from jax import lax

C = 128
NB = 8
HR = 64
NSPEC = 89
S = 128
K = 16
LAYERS = 2
NBX = 64
NBY = 8


def draw_species(key, part):
    key = jax.random.fold_in(key, 5)
    first_key, second_key = jax.random.split(key)
    shape_all = (NBX, NBY, S)
    bin_row = lax.broadcasted_iota(jnp.int32, shape_all, 0)
    percent = 40 + 60 * bin_row // NBX
    rolled = jax.random.randint(first_key, shape_all, 0, 100)
    element = jax.random.randint(second_key, shape_all, 1, NSPEC + 1)
    return jnp.where(rolled < percent, element, 0).astype(jnp.int32)


def draw_neighbours(key, part):
    key = jax.random.fold_in(key, 11)
    first_key, second_key = jax.random.split(key)
    shape_all = (NBX, NBY, K, S)
    bin_pick = jax.random.randint(first_key, shape_all, 0, 9)
    slot_pick = jax.random.randint(second_key, shape_all, 0, S)
    own_slot = lax.broadcasted_iota(jnp.int32, shape_all, 3)
    clash = (bin_pick == 4) & (slot_pick == own_slot)
    slot_pick = jnp.where(clash, (slot_pick + 1) % S, slot_pick)
    return (bin_pick * S + slot_pick).astype(jnp.int32)


def level_of(stream_key, shape, shards, least, high):
    gain = 1.0
    for position, shards_of in shards:
        draws = jax.random.uniform(jax.random.fold_in(jax.random.fold_in(stream_key, 6), position), (shards_of,), jnp.float32, least / len(shards), high / len(shards))
        gain = gain * jnp.repeat(jnp.exp(draws), shape[position] // shards_of).reshape((-1,) + (1,) * (len(shape) - 1 - position))
    return gain


def scatter_about(key, dims, spread, reach, held_as=jnp.bfloat16):
    values = spread * jax.random.normal(key, dims, jnp.float32)
    return jnp.clip(values, min=-reach, max=reach).astype(held_as)


def setup_inputs(seed: int = 0) -> dict:
    splits = jax.random.split(jax.random.key(seed), 11)
    fractions = jnp.clip(1.0 * jax.random.uniform(splits[0], (3, NBX, NBY, S), jnp.float32) ** level_of(splits[0], (3, NBX, NBY, S), ((1, 64), (2, 4)), -0.2, 0.2), 0.0, 1.0)
    species = draw_species(jax.random.fold_in(splits[10], 71), 0)
    neighbours = draw_neighbours(jax.random.fold_in(splits[10], 71), 0)
    embedding = scatter_about(splits[3], (NSPEC, C), 1.0, 6.0, jnp.float32)
    up_weight = scatter_about(splits[4], (LAYERS, C, C), C ** -0.5, 0.5, jnp.float32)
    radial_in = scatter_about(splits[5], (LAYERS, NB, HR), NB ** -0.5, 2.0, jnp.float32)
    radial_out = scatter_about(splits[6], (LAYERS, HR, 3 * C), HR ** -0.5, 0.75, jnp.float32)
    self_weight = scatter_about(splits[7], (LAYERS, C, C), C ** -0.5, 0.5, jnp.float32)
    product_weight = scatter_about(splits[8], (LAYERS, 3 * C, C), (3 * C) ** -0.5, 0.3125, jnp.float32)
    readout = scatter_about(splits[9], (LAYERS, C), C ** -0.5, 0.5, jnp.float32)
    return dict(fractions=fractions, species=species, neighbours=neighbours, embedding=embedding, up_weight=up_weight, radial_in=radial_in, radial_out=radial_out, self_weight=self_weight, product_weight=product_weight, readout=readout)


bin_width = 6.0
slab_height = 12.0
cutoff = 6.0
softening = 0.25
spread_width = 0.75
message_scale = 1.5

def bin_terms(bin_codes, hood_up, hood_frac, own_features, filled, radial_in, radial_out, self_weight, product_weight, readout):
    slot_count = bin_codes.shape[1]
    channels = hood_up.shape[1]
    bin_pick = bin_codes // slot_count
    step_x = (bin_pick // 3 - 1).astype(jnp.float32)
    step_y = (bin_pick % 3 - 1).astype(jnp.float32)
    flat_frac = jnp.transpose(hood_frac, (1, 0, 2)).reshape(3, 9 * slot_count)
    far_frac = flat_frac[:, bin_codes]
    near_frac = hood_frac[4]
    delta_x = (step_x + far_frac[0] - near_frac[0][None, :]) * bin_width
    delta_y = (step_y + far_frac[1] - near_frac[1][None, :]) * bin_width
    delta_z = (far_frac[2] - near_frac[2][None, :]) * slab_height
    distance = jnp.sqrt(delta_x * delta_x + delta_y * delta_y + delta_z * delta_z + softening)
    unit_x = delta_x / distance
    unit_y = delta_y / distance
    unit_z = delta_z / distance
    basis_count = radial_in.shape[0]
    centers = jnp.arange(basis_count, dtype=jnp.float32) * (cutoff / (basis_count - 1))
    basis = jnp.exp(-jnp.square((distance[..., None] - centers) / spread_width))
    scaled = distance / cutoff
    quint = scaled * scaled * scaled * scaled * scaled
    envelope = jnp.where(scaled < 1.0, 1.0 - 21.0 * quint + 35.0 * quint * scaled - 15.0 * quint * scaled * scaled, 0.0)
    hidden = jax.nn.silu(jnp.einsum('ksn,nm->ksm', basis, radial_in, precision=lax.Precision.HIGHEST))
    radial = jnp.einsum('ksm,mc->ksc', hidden, radial_out, precision=lax.Precision.HIGHEST) * envelope[..., None]
    far_up = hood_up[bin_codes]
    message_zero = radial[..., :channels] * far_up
    message_one = radial[..., channels:2 * channels] * far_up
    message_two = radial[..., 2 * channels:] * far_up
    root_three = math.sqrt(3.0)
    root_five = math.sqrt(5.0)
    root_fifteen = math.sqrt(15.0)
    length_sq = unit_x * unit_x + unit_y * unit_y + unit_z * unit_z
    harm_one = jnp.stack([unit_x, unit_y, unit_z]) * root_three
    harm_two = jnp.stack([root_fifteen * unit_x * unit_y, root_fifteen * unit_y * unit_z, 0.5 * root_five * (3.0 * unit_z * unit_z - length_sq), root_fifteen * unit_x * unit_z, 0.5 * root_fifteen * (unit_x * unit_x - unit_y * unit_y)])
    moment_zero = message_scale * lax.optimization_barrier(jnp.sum(message_zero, axis=0))
    moment_one = message_scale * jnp.einsum('mks,ksc->msc', harm_one, message_one, precision=lax.Precision.HIGHEST)
    moment_two = message_scale * jnp.einsum('mks,ksc->msc', harm_two, message_two, precision=lax.Precision.HIGHEST)
    invariants = jnp.concatenate([moment_zero, lax.optimization_barrier(jnp.sum(moment_one * moment_one, axis=0)), lax.optimization_barrier(jnp.sum(moment_two * moment_two, axis=0))], axis=-1)
    mixed = jnp.dot(own_features, self_weight, precision=lax.Precision.HIGHEST) + jnp.dot(invariants, product_weight, precision=lax.Precision.HIGHEST)
    updated = filled[:, None] * mixed
    energy = jnp.dot(updated, readout, precision=lax.Precision.HIGHEST)
    return (updated, energy)

def neighbourhood(source, row_count, col_count):
    return jnp.stack([source[row_off:row_off + row_count, col_off:col_off + col_count] for row_off in range(3) for col_off in range(3)], axis=2)

def interaction(own_features, rim_features, rim_fractions, filled, neighbours, up_weight, radial_in, radial_out, self_weight, product_weight, readout):
    row_count, col_count, slot_count, channels = own_features.shape
    edge_count = neighbours.shape[2]
    rim_up = jnp.einsum('absc,cd->absd', rim_features, up_weight, precision=lax.Precision.HIGHEST)
    hood_up = neighbourhood(rim_up, row_count, col_count).reshape(row_count * col_count, 9 * slot_count, channels)
    hood_frac = neighbourhood(rim_fractions, row_count, col_count).reshape(row_count * col_count, 9, 3, slot_count)

    def one_bin(bin_items):
        return bin_terms(bin_items[0], bin_items[1], bin_items[2], bin_items[3], bin_items[4], radial_in, radial_out, self_weight, product_weight, readout)
    updated, energy = lax.map(jax.checkpoint(one_bin), (neighbours.reshape(row_count * col_count, edge_count, slot_count), hood_up, hood_frac, own_features.reshape(row_count * col_count, slot_count, channels), filled.reshape(row_count * col_count, slot_count)))
    return (updated.reshape(row_count, col_count, slot_count, channels), energy.reshape(row_count, col_count, slot_count))

def extend(source):
    padding = [(1, 1), (1, 1)] + [(0, 0)] * (source.ndim - 2)
    return jnp.pad(source, padding, mode='wrap')

def reference(fractions, species, neighbours, embedding, up_weight, radial_in, radial_out, self_weight, product_weight, readout):
    filled = (species > 0).astype(jnp.float32)
    one_hot = (species[..., None] == jnp.arange(1, NSPEC + 1, dtype=jnp.int32)).astype(jnp.float32)
    start = jnp.einsum('xysn,nc->xysc', one_hot, embedding, precision=lax.Precision.HIGHEST) * filled[..., None]
    own_fractions = jnp.transpose(fractions, (1, 2, 0, 3))

    def total(own_in):
        rim_fractions = extend(own_in)
        first_feat, first_energy = interaction(start, extend(start), rim_fractions, filled, neighbours, up_weight[0], radial_in[0], radial_out[0], self_weight[0], product_weight[0], readout[0])
        second_feat, second_energy = interaction(first_feat, extend(first_feat), rim_fractions, filled, neighbours, up_weight[1], radial_in[1], radial_out[1], self_weight[1], product_weight[1], readout[1])
        atom_sum = first_energy + second_energy
        return (jnp.sum(atom_sum), atom_sum)
    (total_energy, atom_energy), gradient = jax.value_and_grad(total, has_aux=True)(own_fractions)
    scales = jnp.array([bin_width, bin_width, slab_height], dtype=jnp.float32)
    forces = -jnp.transpose(gradient, (2, 0, 1, 3)) / scales[:, None, None, None]
    return (forces, atom_energy, total_energy)
```

```python
import functools
import math

import jax
import jax.numpy as jnp
from jax import lax
from jax.experimental import pallas as pl
from jax.experimental.pallas import tpu as pltpu
from jax.sharding import PartitionSpec as P

bin_width = 6.0
slab_height = 12.0
cutoff = 6.0
softening = 0.25
spread_width = 0.75
message_scale = 1.5

S = 128
C = 128
K = 16
HR = 64
NB = 8
NSPEC = 89
Q = 16
W = 256
MESH = pl.DeviceIdType.MESH
F32 = jnp.float32
BF16 = jnp.bfloat16
HIGH = lax.Precision.HIGHEST
R3 = math.sqrt(3.0)
R5 = math.sqrt(5.0)
R15 = math.sqrt(15.0)


def exact(a, b):
    return jnp.dot(a, b, precision=HIGH, preferred_element_type=F32)


def pieces(x, count):
    parts = []
    for _ in range(count):
        part = x.astype(BF16).astype(F32)
        parts.append(part)
        x = x - part
    return parts


def nt(a, b):
    return lax.dot_general(a, b, (((1,), (1,)), ((), ())), preferred_element_type=F32)


def rows_iota(rows, cols):
    return lax.broadcasted_iota(jnp.int32, (rows, cols), 0)


def kernel(
    shape,
    frac_ref,
    spec_ref,
    nbr_ref,
    emb_ref,
    up_ref,
    rin_ref,
    rout_ref,
    self_ref,
    prod_ref,
    read_ref,
    force_ref,
    energy_ref,
    total_ref,
    pos,
    hot,
    yb,
    xs,
    rad,
    drad,
    hup,
    mom,
    gmom,
    rim,
    hl,
    dhl,
    rgrad,
    gx_in,
    gy_in,
    edge,
    pgrad,
    pg_in,
    wst,
    lin,
    tab,
    emb_t,
    pad,
    feat,
    ar_out,
    ar_in,
    send_sem,
    recv_sem,
):
    gxn, gyn = shape
    gx = lax.axis_index("gx")
    gy = lax.axis_index("gy")
    left = lax.rem(gx + gxn - 1, gxn)
    right = lax.rem(gx + 1, gxn)
    down = lax.rem(gy + gyn - 1, gyn)
    up = lax.rem(gy + 1, gyn)
    around = [
        (left, gy),
        (right, gy),
        (gx, down),
        (gx, up),
        (left, down),
        (left, up),
        (right, down),
        (right, up),
    ]
    digits = [
        gy,
        lax.rem(gx, 4),
        lax.rem(gx // 4, 4),
        gx // 16,
    ]

    def partner(phase, step):
        other = lax.rem(digits[phase] + step, 4)
        if phase == 0:
            return (gx, other)
        return (gx + (other - digits[phase]) * 4 ** (phase - 1), gy)

    barrier = pltpu.get_barrier_semaphore()
    greeted = around + [partner(phase, step) for phase in range(4) for step in (1, 2, 3)]
    for device in greeted:
        pl.semaphore_signal(barrier, inc=1, device_id=device, device_id_type=MESH)

    def remote(number, source, target, device):
        return pltpu.make_async_remote_copy(
            src_ref=source,
            dst_ref=target,
            send_sem=send_sem.at[number],
            recv_sem=recv_sem.at[number],
            device_id=device,
            device_id_type=MESH,
        )

    pos[5:7] = jnp.zeros((2, 8, S), F32)
    for b in range(2):
        for d in range(3):
            pos[5 + b, d : d + 1, :] = frac_ref[d, 0, b : b + 1, :]
        pos[5 + b, 3:4, :] = spec_ref[0, b : b + 1, :].astype(F32)
    pl.semaphore_wait(barrier, len(greeted))

    pos_copies = [
        remote(0, pos.at[pl.ds(5, 2)], pos.at[pl.ds(9, 2)], (left, gy)),
        remote(1, pos.at[pl.ds(5, 2)], pos.at[pl.ds(1, 2)], (right, gy)),
        remote(2, pos.at[5], pos.at[7], (gx, down)),
        remote(3, pos.at[6], pos.at[4], (gx, up)),
        remote(4, pos.at[5], pos.at[11], (left, down)),
        remote(5, pos.at[6], pos.at[8], (left, up)),
        remote(6, pos.at[5], pos.at[3], (right, down)),
        remote(7, pos.at[6], pos.at[0], (right, up)),
    ]
    for copy in pos_copies:
        copy.start()

    pad[...] = jnp.zeros_like(pad)
    pad[0:NSPEC, :] = emb_ref[...]
    table = exact(pad[...], up_ref[0])
    parts = pieces(table.T, 2)
    tab[...] = jnp.concatenate(parts, axis=0).astype(BF16)
    parts = pieces(pad[...].T, 3)
    emb_t[...] = jnp.concatenate(parts, axis=0).astype(BF16)
    for t in range(2):
        w1, w2, w3 = pieces(rin_ref[t], 3)
        stack = jnp.concatenate([w1, w1, w2, w1, w2, w3], axis=0)
        pad[...] = jnp.zeros_like(pad)
        pad[0 : 6 * NB, 0:HR] = stack
        lin[t * HR : (t + 1) * HR, :] = pad[...].T[0:HR, 0 : 6 * NB].astype(BF16)
        w1, w2 = pieces(rout_ref[t], 2)
        wst[t] = jnp.concatenate([w1, w1, w2], axis=0).T.astype(BF16)

    for b in range(2):

        def hot_block(k, carry, b=b):
            code = nbr_ref[0, b, pl.ds(k, 1), :]
            lanes = pl.ds(pl.multiple_of((b * K + k) * S, S), S)
            for c in range(9):
                match = rows_iota(S, S) == jnp.broadcast_to(code - c * S, (S, S))
                hot[c * S : (c + 1) * S, lanes] = jnp.where(match, 1.0, 0.0).astype(BF16)
            return carry

        lax.fori_loop(0, K, hot_block, 0)

    mom[...] = jnp.zeros_like(mom)
    edge[...] = jnp.zeros_like(edge)

    for copy in pos_copies:
        copy.wait_recv()

    unit = []
    for b in range(2):
        codes = nbr_ref[0, b]
        which = lax.shift_right_logical(codes, 7)
        slot = lax.bitwise_and(codes, S - 1)
        step_x = lax.shift_right_logical(which * 11, 5)
        step_y = which - 3 * step_x
        far = [jnp.zeros((K, S), F32)] * 4
        for c in range(9):
            source = (c // 3) * 4 + b + c % 3
            chosen = which == c
            for d in range(4):
                row = jnp.broadcast_to(pos[source, d : d + 1, :], (K, S))
                taken = jnp.take_along_axis(row, slot, axis=1, mode="promise_in_bounds")
                far[d] = jnp.where(chosen, taken, far[d])
        near = [pos[5 + b, d : d + 1, :] for d in range(3)]
        delta_x = ((step_x - 1).astype(F32) + far[0] - near[0]) * bin_width
        delta_y = ((step_y - 1).astype(F32) + far[1] - near[1]) * bin_width
        delta_z = (far[2] - near[2]) * slab_height
        distance = jnp.sqrt(delta_x * delta_x + delta_y * delta_y + delta_z * delta_z + softening)
        ux = delta_x / distance
        uy = delta_y / distance
        uz = delta_z / distance
        unit.append((distance, ux, uy, uz, which, slot))
        q1 = distance * (1.0 / cutoff)
        q2 = q1 * q1
        q4 = q2 * q2
        inside = q1 < 1.0
        env = jnp.where(inside, 1.0 + q4 * q1 * (-21.0 + q1 * (35.0 - 15.0 * q1)), 0.0)
        denv = jnp.where(
            inside, q4 * (-105.0 + q1 * (210.0 - 105.0 * q1)) * (1.0 / cutoff), 0.0
        )
        values = [
            R3 * ux,
            R3 * uy,
            R3 * uz,
            R15 * ux * uy,
            R15 * uy * uz,
            0.5 * R5 * (2.0 * uz * uz - ux * ux - uy * uy),
            R15 * ux * uz,
            0.5 * R15 * (ux * ux - uy * uy),
            distance,
            env,
            denv,
            far[3],
        ]
        for m, value in enumerate(values):
            for k in range(K):
                yb[b * 8 + k // 2, m, :, (k % 2) * S : (k % 2 + 1) * S] = jnp.broadcast_to(
                    value[k : k + 1, :], (8, S)
                )

    centers = rows_iota(NB, W).astype(F32) * (cutoff / (NB - 1))

    def hidden_block(q, carry):
        offset = yb[q, 8] - centers
        scaled = offset * (1.0 / spread_width)
        basis = jnp.exp(-(scaled * scaled))
        slope = basis * (offset * (-2.0 / (spread_width * spread_width)))

        def stacked(value):
            b1, b2, b3 = pieces(value, 3)
            return jnp.concatenate([b1, b2, b1, b3, b2, b1], axis=0).astype(BF16)

        pre = jnp.dot(lin[...], stacked(basis), preferred_element_type=F32)
        dpre = jnp.dot(lin[...], stacked(slope), preferred_element_type=F32)
        env16 = jnp.concatenate([yb[q, 9], yb[q, 9]], axis=0)
        denv16 = jnp.concatenate([yb[q, 10], yb[q, 10]], axis=0)
        for t in range(2):
            for r in range(HR // 16):
                rows = slice(t * HR + r * 16, t * HR + (r + 1) * 16)
                x = pre[rows]
                sig = 1.0 / (1.0 + jnp.exp(-x))
                h = x * sig
                dh = (sig + h * (1.0 - sig)) * dpre[rows]
                for v, value in enumerate((env16 * h, denv16 * h + env16 * dh)):
                    high, low = pieces(value, 2)
                    high = high.astype(BF16)
                    xs[t, v, q, r * 16 : (r + 1) * 16, :] = high
                    xs[t, v, q, HR + r * 16 : HR + (r + 1) * 16, :] = low.astype(BF16)
                    xs[t, v, q, 2 * HR + r * 16 : 2 * HR + (r + 1) * 16, :] = high
        return carry

    lax.fori_loop(0, Q, hidden_block, 0)

    def radial_blocks(t, v, target):
        def block(q, carry):
            target[t, q] = jnp.dot(wst[t], xs[t, v, q], preferred_element_type=F32)
            return carry

        lax.fori_loop(0, Q, block, 0)

    def gather_blocks(t):
        def block(q, carry):
            if t == 0:
                element = yb[q, 11].astype(jnp.int32) - 1
                element = jnp.concatenate([element] * (S // 8), axis=0)
                choice = jnp.where(rows_iota(S, W) == element, 1.0, 0.0).astype(BF16)
                both = jnp.dot(tab[...], choice, preferred_element_type=F32)
            else:
                lanes = pl.ds(pl.multiple_of(q * W, W), W)
                both = jnp.dot(hl[q // 8], hot[:, lanes], preferred_element_type=F32)
            hup[t, q] = both[0:C] + both[C:]
            return carry

        lax.fori_loop(0, Q, block, 0)

    def moments(t):
        def block(q, carry):
            b = q // 8
            for ct in range(C // 8):
                rows = slice(ct * 8, ct * 8 + 8)
                sums = [mom[t, b, m, rows, :] for m in range(9)]
                for half in range(2):
                    lanes = slice(half * S, half * S + S)
                    h = hup[t, q, rows, lanes]
                    sums[0] = sums[0] + rad[t, q, rows, lanes] * h
                    h1 = rad[t, q, C + ct * 8 : C + ct * 8 + 8, lanes] * h
                    h2 = rad[t, q, 2 * C + ct * 8 : 2 * C + ct * 8 + 8, lanes] * h
                    for m in range(3):
                        sums[1 + m] = sums[1 + m] + yb[q, m, :, lanes] * h1
                    for m in range(3, 8):
                        sums[1 + m] = sums[1 + m] + yb[q, m, :, lanes] * h2
                for m in range(9):
                    mom[t, b, m, rows, :] = sums[m]
            return carry

        lax.fori_loop(0, Q, block, 0)

    filled = jnp.concatenate(
        [jnp.where(pos[5 + b, 3:4, :] > 0.0, 1.0, 0.0) for b in range(2)], axis=1
    )

    def features(t, own):
        inv0 = jnp.concatenate([mom[t, b, 0] for b in range(2)], axis=1) * message_scale
        inv1 = jnp.concatenate(
            [sum(mom[t, b, m] * mom[t, b, m] for m in range(1, 4)) for b in range(2)], axis=1
        )
        inv2 = jnp.concatenate(
            [sum(mom[t, b, m] * mom[t, b, m] for m in range(4, 9)) for b in range(2)], axis=1
        )
        scale = message_scale * message_scale
        inv = jnp.concatenate([inv0, inv1 * scale, inv2 * scale], axis=0)
        mixed = exact(self_ref[t].T, own) + exact(prod_ref[t].T, inv)
        return mixed * filled

    def read_column(t):
        return jnp.broadcast_to(read_ref[t : t + 1, :], (C, C)).T

    def energies(t, values):
        column = read_column(t)
        return jnp.concatenate(
            [
                jnp.sum(values[:, b * S : (b + 1) * S] * column, axis=0, keepdims=True)
                for b in range(2)
            ],
            axis=1,
        )

    def moment_grads(t, grad):
        inner = exact(prod_ref[t], grad)
        for b in range(2):
            lanes = slice(b * S, (b + 1) * S)
            gmom[b, 0] = inner[0:C, lanes] * message_scale
            scale = 2.0 * message_scale * message_scale
            for m in range(1, 9):
                rows = slice(C, 2 * C) if m < 4 else slice(2 * C, 3 * C)
                gmom[b, m] = inner[rows, lanes] * mom[t, b, m] * scale

    radial_blocks(0, 0, rad)
    gather_blocks(0)
    moments(0)
    own_element = jnp.concatenate([pos[5 + b, 3:4, :] for b in range(2)], axis=1)
    own_hot = jnp.where(
        rows_iota(S, 2 * S) == jnp.broadcast_to(own_element.astype(jnp.int32) - 1, (S, 2 * S)),
        1.0,
        0.0,
    ).astype(BF16)
    start = jnp.dot(emb_t[...], own_hot, preferred_element_type=F32)
    start = start[0:C] + start[C : 2 * C] + start[2 * C :]
    first = features(0, start)
    feat[0] = first
    own_up = exact(up_ref[1].T, first)
    rim[5] = own_up[:, 0:S]
    rim[6] = own_up[:, S:]
    up_copies = [
        remote(8, rim.at[5], rim.at[7], (gx, down)),
        remote(9, rim.at[6], rim.at[4], (gx, up)),
        remote(10, rim.at[pl.ds(5, 2)], rim.at[pl.ds(9, 2)], (left, gy)),
        remote(11, rim.at[pl.ds(5, 2)], rim.at[pl.ds(1, 2)], (right, gy)),
    ]
    for copy in up_copies:
        copy.start()
    first_energy = energies(0, first)

    radial_blocks(1, 0, rad)
    up_copies[0].wait_recv()
    up_copies[1].wait_recv()
    far_copies = [
        remote(12, rim.at[4], rim.at[8], (left, gy)),
        remote(13, rim.at[4], rim.at[0], (right, gy)),
        remote(14, rim.at[7], rim.at[11], (left, gy)),
        remote(15, rim.at[7], rim.at[3], (right, gy)),
    ]
    for copy in far_copies:
        copy.start()
    radial_blocks(0, 1, drad)
    radial_blocks(1, 1, drad)
    for copy in up_copies[2:] + far_copies:
        copy.wait_recv()

    for a in range(3):
        for r in range(4):
            high, low = pieces(rim[a * 4 + r], 2)
            value = jnp.concatenate([high, low], axis=0).astype(BF16)
            for b in range(2):
                if 0 <= r - b < 3:
                    c = a * 3 + r - b
                    hl[b, :, c * S : (c + 1) * S] = value

    gather_blocks(1)
    moments(1)
    second = features(1, feat[0])
    atom_energy = first_energy + energies(1, second)
    for b in range(2):
        energy_ref[0, b : b + 1, :] = atom_energy[:, b * S : (b + 1) * S]

    def reduce_send(phase, value):
        ar_out[phase] = value
        ar_in[phase, digits[phase]] = value
        copies = [
            remote(
                32 + phase * 3 + step - 1,
                ar_out.at[phase],
                ar_in.at[phase, digits[phase]],
                partner(phase, step),
            )
            for step in (1, 2, 3)
        ]
        for copy in copies:
            copy.start()
        return copies

    def reduce_wait(phase, copies):
        for copy in copies:
            copy.wait()
        return (ar_in[phase, 0] + ar_in[phase, 1]) + (ar_in[phase, 2] + ar_in[phase, 3])

    pair = atom_energy[:, 0:S] + atom_energy[:, S:]
    reduced = reduce_send(0, jnp.broadcast_to(jnp.sum(pair, axis=1, keepdims=True), (8, S)))

    grad1 = jnp.concatenate([read_column(1)] * 2, axis=1) * filled
    moment_grads(1, grad1)

    def harmonics(q, half, rows, b, twice):
        lanes = slice(half * S, half * S + S)

        def spread(m):
            value = yb[q, m, :, lanes]
            return jnp.concatenate([value, value], axis=0) if twice else value

        a1 = sum(spread(m) * gmom[b, 1 + m, rows, :] for m in range(3))
        a2 = sum(spread(m) * gmom[b, 1 + m, rows, :] for m in range(3, 8))
        return a1, a2

    def feature_block(q, carry):
        b = q // 8
        for half in range(2):
            lanes = slice(half * S, half * S + S)
            for ct in range(C // 16):
                rows = slice(ct * 16, ct * 16 + 16)
                a1, a2 = harmonics(q, half, rows, b, True)
                value = (
                    rad[1, q, rows, lanes] * gmom[b, 0, rows, :]
                    + rad[1, q, C + ct * 16 : C + ct * 16 + 16, lanes] * a1
                    + rad[1, q, 2 * C + ct * 16 : 2 * C + ct * 16 + 16, lanes] * a2
                )
                high, low = pieces(value, 2)
                target = pl.ds(pl.multiple_of(q * W + half * S, S), S)
                dhl[rows, target] = high.astype(BF16)
                dhl[C + ct * 16 : C + ct * 16 + 16, target] = low.astype(BF16)
        return carry

    lax.fori_loop(0, Q, feature_block, 0)

    def scatter(a):
        half = []
        for b in range(2):
            lanes = slice(b * K * S, (b + 1) * K * S)
            both = nt(dhl[:, lanes], hot[a * 3 * S : (a + 1) * 3 * S, lanes])
            half.append(both[0:C] + both[C:])
        rgrad[a * 4] = half[0][:, 0:S]
        rgrad[a * 4 + 1] = half[0][:, S : 2 * S] + half[1][:, 0:S]
        rgrad[a * 4 + 2] = half[0][:, 2 * S :] + half[1][:, S : 2 * S]
        rgrad[a * 4 + 3] = half[1][:, 2 * S :]

    def column_copies(a, number, target, device):
        return [
            remote(number, rgrad.at[a * 4], gx_in.at[target, 0], device),
            remote(number + 1, rgrad.at[a * 4 + 3], gx_in.at[target, 3], device),
            remote(
                number + 2,
                rgrad.at[pl.ds(a * 4 + 1, 2)],
                gx_in.at[target, pl.ds(1, 2)],
                device,
            ),
        ]

    scatter(0)
    to_left = column_copies(0, 16, 0, (left, gy))
    for copy in to_left:
        copy.start()
    scatter(2)
    to_right = column_copies(2, 19, 1, (right, gy))
    for copy in to_right:
        copy.start()
    scatter(1)

    def position_block(t):
        def block(q, carry):
            b = q // 8
            for half in range(2):
                lanes = slice(half * S, half * S + S)
                sums = [jnp.zeros((8, S), F32)] * 9
                for ct in range(C // 8):
                    rows = slice(ct * 8, ct * 8 + 8)
                    rows1 = slice(C + ct * 8, C + ct * 8 + 8)
                    rows2 = slice(2 * C + ct * 8, 2 * C + ct * 8 + 8)
                    a1, a2 = harmonics(q, half, rows, b, False)
                    h = hup[t, q, rows, lanes]
                    h1 = rad[t, q, rows1, lanes] * h
                    h2 = rad[t, q, rows2, lanes] * h
                    slope = (
                        drad[t, q, rows, lanes] * gmom[b, 0, rows, :]
                        + drad[t, q, rows1, lanes] * a1
                        + drad[t, q, rows2, lanes] * a2
                    )
                    sums[8] = sums[8] + slope * h
                    for m in range(3):
                        sums[m] = sums[m] + gmom[b, 1 + m, rows, :] * h1
                    for m in range(3, 8):
                        sums[m] = sums[m] + gmom[b, 1 + m, rows, :] * h2
                k = (q - b * 8) * 2 + half
                for m in range(9):
                    total = jnp.sum(sums[m], axis=0, keepdims=True)
                    edge[b, m, pl.ds(k, 1), :] = edge[b, m, pl.ds(k, 1), :] + total
            return carry

        lax.fori_loop(0, Q, block, 0)

    position_block(1)
    for group in (to_left, to_right):
        group[0].wait_recv()
        group[1].wait_recv()
    rgrad[4] = rgrad[4] + gx_in[0, 0] + gx_in[1, 0]
    rgrad[7] = rgrad[7] + gx_in[0, 3] + gx_in[1, 3]
    row_copies = [
        remote(22, rgrad.at[4], gy_in.at[0], (gx, down)),
        remote(23, rgrad.at[7], gy_in.at[1], (gx, up)),
    ]
    for copy in row_copies:
        copy.start()
    reduced = reduce_send(1, reduce_wait(0, reduced))
    to_left[2].wait_recv()
    to_right[2].wait_recv()
    own_low = rgrad[5] + gx_in[0, 1] + gx_in[1, 1]
    own_high = rgrad[6] + gx_in[0, 2] + gx_in[1, 2]
    direct = jnp.concatenate([read_column(0)] * 2, axis=1) + exact(self_ref[1], grad1)
    for copy in row_copies:
        copy.wait_recv()
    returned = jnp.concatenate([own_low + gy_in[1], own_high + gy_in[0]], axis=1)
    grad0 = (direct + exact(up_ref[1], returned)) * filled

    moment_grads(0, grad0)
    reduced = reduce_send(2, reduce_wait(1, reduced))
    position_block(0)
    reduced = reduce_send(3, reduce_wait(2, reduced))

    direct_force = []
    for b in range(2):
        distance, ux, uy, uz, which, slot = unit[b]
        dy = [edge[b, m] for m in range(9)]
        gux = R3 * dy[0] + R15 * (uy * dy[3] + uz * dy[6] + ux * dy[7]) - R5 * ux * dy[5]
        guy = R3 * dy[1] + R15 * (ux * dy[3] + uz * dy[4] - uy * dy[7]) - R5 * uy * dy[5]
        guz = R3 * dy[2] + R15 * (uy * dy[4] + ux * dy[6]) + (2.0 * R5) * uz * dy[5]
        along = ux * gux + uy * guy + uz * guz
        grads = [
            (g - u * along) / distance + u * dy[8]
            for g, u in ((gux, ux), (guy, uy), (guz, uz))
        ]
        direct_force.append([jnp.sum(g, axis=0, keepdims=True) for g in grads])
        total = jnp.zeros((9 * K, S), F32)
        for k in range(K):
            bins = jnp.broadcast_to(which[k : k + 1, :], (K, S))
            here = rows_iota(K, S) == bins
            values = []
            for g in grads:
                values.append(
                    jnp.where(here, jnp.broadcast_to(g[k : k + 1, :], (K, S)), 0.0)
                )
            stack = jnp.concatenate(values, axis=0)
            stack = jnp.concatenate(pieces(stack, 3), axis=0).astype(BF16)
            place = jnp.where(
                rows_iota(S, S) == jnp.broadcast_to(slot[k : k + 1, :], (S, S)), 1.0, 0.0
            ).astype(BF16)
            total = total + nt(stack, place)
        total = total[0 : 3 * K] + total[3 * K : 6 * K] + total[6 * K :]
        for c in range(9):
            source = (c // 3) * 4 + b + c % 3
            for d in range(3):
                row = total[d * K + c : d * K + c + 1, :]
                if b == 0 or c % 3 == 2:
                    pgrad[source, d : d + 1, :] = row
                else:
                    pgrad[source, d : d + 1, :] = pgrad[source, d : d + 1, :] + row
    for source in range(12):
        pgrad[source, 3:8, :] = jnp.zeros((5, S), F32)
    back_copies = [
        remote(24, pgrad.at[pl.ds(1, 2)], pg_in.at[pl.ds(0, 2)], (left, gy)),
        remote(25, pgrad.at[pl.ds(9, 2)], pg_in.at[pl.ds(2, 2)], (right, gy)),
        remote(26, pgrad.at[4], pg_in.at[4], (gx, down)),
        remote(27, pgrad.at[7], pg_in.at[5], (gx, up)),
        remote(28, pgrad.at[0], pg_in.at[6], (left, down)),
        remote(29, pgrad.at[3], pg_in.at[7], (left, up)),
        remote(30, pgrad.at[8], pg_in.at[8], (right, down)),
        remote(31, pgrad.at[11], pg_in.at[9], (right, up)),
    ]
    for copy in back_copies:
        copy.start()
    total_ref[...] = reduce_wait(3, reduced)
    for copy in back_copies:
        copy.wait_recv()
    low_grad = pgrad[5] + pg_in[0] + pg_in[2] + pg_in[5] + pg_in[7] + pg_in[9]
    high_grad = pgrad[6] + pg_in[1] + pg_in[3] + pg_in[4] + pg_in[6] + pg_in[8]
    for b, returned in enumerate((low_grad, high_grad)):
        for d in range(3):
            force_ref[d, 0, b : b + 1, :] = direct_force[b][d] - returned[d : d + 1, :]
    for copy in pos_copies + up_copies + far_copies + to_left + to_right:
        copy.wait_send()
    for copy in row_copies + back_copies:
        copy.wait_send()


def on_device(shape, *arguments):
    vmem = pl.BlockSpec(memory_space=pltpu.VMEM)
    scratch = [
        ((12, 8, S), F32),
        ((9 * S, 2 * K * S), BF16),
        ((Q, 12, 8, W), F32),
        ((2, 2, Q, 3 * HR, W), BF16),
        ((2, Q, 3 * C, W), F32),
        ((2, Q, 3 * C, W), F32),
        ((2, Q, C, W), F32),
        ((2, 2, 9, C, S), F32),
        ((2, 9, C, S), F32),
        ((12, C, S), F32),
        ((2, 2 * C, 9 * S), BF16),
        ((2 * C, 2 * K * S), BF16),
        ((12, C, S), F32),
        ((2, 4, C, S), F32),
        ((2, C, S), F32),
        ((2, 9, K, S), F32),
        ((12, 8, S), F32),
        ((10, 8, S), F32),
        ((2, 3 * C, 3 * HR), BF16),
        ((2 * HR, 6 * NB), BF16),
        ((2 * C, S), BF16),
        ((3 * C, S), BF16),
        ((S, S), F32),
        ((2, C, 2 * S), F32),
        ((4, 8, S), F32),
        ((4, 4, 8, S), F32),
    ]
    forces, energy, total = pl.pallas_call(
        functools.partial(kernel, shape),
        out_shape=(
            jax.ShapeDtypeStruct((3, 1, 2, S), F32),
            jax.ShapeDtypeStruct((1, 2, S), F32),
            jax.ShapeDtypeStruct((8, S), F32),
        ),
        in_specs=[vmem] * 10,
        out_specs=(vmem, vmem, vmem),
        scratch_shapes=[pltpu.VMEM(dims, kind) for dims, kind in scratch]
        + [pltpu.SemaphoreType.DMA((44,)), pltpu.SemaphoreType.DMA((44,))],
        compiler_params=pltpu.CompilerParams(
            collective_id=0, has_side_effects=True, vmem_limit_bytes=60 * 1024 * 1024
        ),
    )(*arguments)
    return forces, energy, total[0, 0]


def solution(mesh):
    placed = (
        P(None, "gx", "gy", None),
        P("gx", "gy", None),
        P("gx", "gy", None, None),
        P(),
        P(),
        P(),
        P(),
        P(),
        P(),
        P(),
    )
    return jax.shard_map(
        functools.partial(on_device, (mesh.shape["gx"], mesh.shape["gy"])),
        mesh=mesh,
        in_specs=placed,
        out_specs=(P(None, "gx", "gy", None), P("gx", "gy", None), P()),
        check_vma=False,
    )
```

```python
import functools
import math

import jax
import jax.numpy as jnp
from jax import lax
from jax.experimental import pallas as pl
from jax.experimental.pallas import tpu as pltpu
from jax.sharding import PartitionSpec as P

bin_width = 6.0
slab_height = 12.0
cutoff = 6.0
softening = 0.25
spread_width = 0.75
message_scale = 1.5

S = 128
C = 128
K = 16
HR = 64
NB = 8
NSPEC = 89
Q = 16
W = 256
MESH = pl.DeviceIdType.MESH
F32 = jnp.float32
BF16 = jnp.bfloat16
HIGH = lax.Precision.HIGHEST
R3 = math.sqrt(3.0)
R5 = math.sqrt(5.0)
R15 = math.sqrt(15.0)


def exact(a, b):
    return jnp.dot(a, b, precision=HIGH, preferred_element_type=F32)


def pieces(x, count):
    parts = []
    for _ in range(count):
        part = x.astype(BF16).astype(F32)
        parts.append(part)
        x = x - part
    return parts


def wide(weight):
    high, low = pieces(weight, 2)
    return jnp.concatenate([high, high, low], axis=1).astype(BF16)


def tall(value):
    high, low = pieces(value, 2)
    return jnp.concatenate([high, low, high], axis=0).astype(BF16)


def product(weight, value):
    return jnp.dot(weight, tall(value), preferred_element_type=F32)


def blocks(count, unroll, step):
    def several(i, carry):
        for u in range(unroll):
            step(i * unroll + u)
        return carry

    if unroll == count:
        several(0, 0)
    else:
        lax.fori_loop(0, count // unroll, several, 0)


def nt(a, b):
    return lax.dot_general(a, b, (((1,), (1,)), ((), ())), preferred_element_type=F32)


def rows_iota(rows, cols):
    return lax.broadcasted_iota(jnp.int32, (rows, cols), 0)


def kernel(
    shape,
    frac_ref,
    spec_ref,
    nbr_ref,
    emb_ref,
    up_ref,
    rin_ref,
    rout_ref,
    self_ref,
    prod_ref,
    read_ref,
    force_ref,
    energy_ref,
    total_ref,
    pos,
    hot,
    yb,
    xs,
    rad,
    drad,
    hup,
    mom,
    gmom,
    rim,
    hl,
    dhl,
    rgrad,
    gx_in,
    gy_in,
    edge,
    pgrad,
    pg_in,
    wst,
    lin,
    tab,
    mix_w,
    back_w,
    up_w,
    base,
    emb_t,
    pad,
    feat,
    ar_out,
    ar_in,
    send_sem,
    recv_sem,
):
    gxn, gyn = shape
    gx = lax.axis_index("gx")
    gy = lax.axis_index("gy")
    left = lax.rem(gx + gxn - 1, gxn)
    right = lax.rem(gx + 1, gxn)
    down = lax.rem(gy + gyn - 1, gyn)
    up = lax.rem(gy + 1, gyn)
    around = [
        (left, gy),
        (right, gy),
        (gx, down),
        (gx, up),
        (left, down),
        (left, up),
        (right, down),
        (right, up),
    ]
    digits = [
        gy,
        lax.rem(gx, 4),
        lax.rem(gx // 4, 4),
        gx // 16,
    ]

    def partner(phase, step):
        other = lax.rem(digits[phase] + step, 4)
        if phase == 0:
            return (gx, other)
        return (gx + (other - digits[phase]) * 4 ** (phase - 1), gy)

    barrier = pltpu.get_barrier_semaphore()
    greeted = around + [partner(phase, step) for phase in range(4) for step in (1, 2, 3)]
    for device in greeted:
        pl.semaphore_signal(barrier, inc=1, device_id=device, device_id_type=MESH)

    def remote(number, source, target, device):
        return pltpu.make_async_remote_copy(
            src_ref=source,
            dst_ref=target,
            send_sem=send_sem.at[number],
            recv_sem=recv_sem.at[number],
            device_id=device,
            device_id_type=MESH,
        )

    pos[5:7] = jnp.zeros((2, 8, S), F32)
    for b in range(2):
        for d in range(3):
            pos[5 + b, d : d + 1, :] = frac_ref[d, 0, b : b + 1, :]
        pos[5 + b, 3:4, :] = spec_ref[0, b : b + 1, :].astype(F32)

    def radial_weights(t):
        w1, w2 = pieces(rout_ref[t], 2)
        wst[t] = jnp.concatenate([w1, w1, w2], axis=0).T.astype(BF16)

    def mix_weights(t):
        mix_w[t] = wide(jnp.concatenate([self_ref[t].T, prod_ref[t].T], axis=1))

    def back_weights(t):
        back_w[t] = wide(jnp.concatenate([prod_ref[t], self_ref[t]], axis=0))

    for t in range(2):
        w1, w2, w3 = pieces(rin_ref[t], 3)
        stack = jnp.concatenate([w1, w1, w2, w1, w2, w3], axis=0)
        pad[...] = jnp.zeros_like(pad)
        pad[0 : 6 * NB, 0:HR] = stack
        lin[t * HR : (t + 1) * HR, :] = pad[...].T[0:HR, 0 : 6 * NB].astype(BF16)
    pad[...] = jnp.zeros_like(pad)
    pad[0:NSPEC, :] = emb_ref[...]
    table = exact(pad[...], up_ref[0])
    parts = pieces(table.T, 2)
    tab[...] = jnp.concatenate(parts, axis=1).astype(BF16)
    radial_weights(0)
    pl.semaphore_wait(barrier, len(greeted))

    pos_copies = [
        remote(0, pos.at[pl.ds(5, 2)], pos.at[pl.ds(9, 2)], (left, gy)),
        remote(1, pos.at[pl.ds(5, 2)], pos.at[pl.ds(1, 2)], (right, gy)),
        remote(2, pos.at[5], pos.at[7], (gx, down)),
        remote(3, pos.at[6], pos.at[4], (gx, up)),
        remote(4, pos.at[5], pos.at[11], (left, down)),
        remote(5, pos.at[6], pos.at[8], (left, up)),
        remote(6, pos.at[5], pos.at[3], (right, down)),
        remote(7, pos.at[6], pos.at[0], (right, up)),
    ]
    for copy in pos_copies:
        copy.start()

    parts = pieces(pad[...].T, 3)
    emb_t[...] = jnp.concatenate(parts, axis=0).astype(BF16)
    mix_weights(0)
    up_w[0] = wide(up_ref[1].T)

    for b in range(2):

        def hot_block(k, carry, b=b):
            code = nbr_ref[0, b, pl.ds(k, 1), :]
            lanes = pl.ds(pl.multiple_of((b * K + k) * S, S), S)
            for c in range(9):
                match = rows_iota(S, S) == jnp.broadcast_to(code - c * S, (S, S))
                hot[c * S : (c + 1) * S, lanes] = jnp.where(match, 1.0, 0.0).astype(BF16)
            return carry

        lax.fori_loop(0, K, hot_block, 0)

    mom[...] = jnp.zeros_like(mom)
    edge[...] = jnp.zeros_like(edge)

    for copy in pos_copies:
        copy.wait_recv()

    unit = []
    for b in range(2):
        codes = nbr_ref[0, b]
        which = lax.shift_right_logical(codes, 7)
        slot = lax.bitwise_and(codes, S - 1)
        step_x = lax.shift_right_logical(which * 11, 5)
        step_y = which - 3 * step_x
        far = [jnp.zeros((K, S), F32)] * 4
        for c in range(9):
            source = (c // 3) * 4 + b + c % 3
            chosen = which == c
            for d in range(4):
                row = jnp.broadcast_to(pos[source, d : d + 1, :], (K, S))
                taken = jnp.take_along_axis(row, slot, axis=1, mode="promise_in_bounds")
                far[d] = jnp.where(chosen, taken, far[d])
        near = [pos[5 + b, d : d + 1, :] for d in range(3)]
        delta_x = ((step_x - 1).astype(F32) + far[0] - near[0]) * bin_width
        delta_y = ((step_y - 1).astype(F32) + far[1] - near[1]) * bin_width
        delta_z = (far[2] - near[2]) * slab_height
        distance = jnp.sqrt(delta_x * delta_x + delta_y * delta_y + delta_z * delta_z + softening)
        ux = delta_x / distance
        uy = delta_y / distance
        uz = delta_z / distance
        unit.append((distance, ux, uy, uz, which, slot))
        q1 = distance * (1.0 / cutoff)
        q2 = q1 * q1
        q4 = q2 * q2
        inside = q1 < 1.0
        env = jnp.where(inside, 1.0 + q4 * q1 * (-21.0 + q1 * (35.0 - 15.0 * q1)), 0.0)
        denv = jnp.where(
            inside, q4 * (-105.0 + q1 * (210.0 - 105.0 * q1)) * (1.0 / cutoff), 0.0
        )
        values = [
            R3 * ux,
            R3 * uy,
            R3 * uz,
            R15 * ux * uy,
            R15 * uy * uz,
            0.5 * R5 * (2.0 * uz * uz - ux * ux - uy * uy),
            R15 * ux * uz,
            0.5 * R15 * (ux * ux - uy * uy),
            distance,
            env,
            denv,
            far[3],
        ]
        for m, value in enumerate(values):
            for k in range(K):
                yb[b * 8 + k // 2, m, :, (k % 2) * S : (k % 2 + 1) * S] = jnp.broadcast_to(
                    value[k : k + 1, :], (8, S)
                )

    centers = rows_iota(NB, W).astype(F32) * (cutoff / (NB - 1))

    def stacked(value):
        b1, b2, b3 = pieces(value, 3)
        return jnp.concatenate([b1, b2, b1, b3, b2, b1], axis=0).astype(BF16)

    def hidden_blocks(t):
        def block(q):
            if t == 0:
                offset = yb[q, 8] - centers
                scaled = offset * (1.0 / spread_width)
                basis = jnp.exp(-(scaled * scaled))
                slope = basis * (offset * (-2.0 / (spread_width * spread_width)))
                flat = stacked(basis)
                steep = stacked(slope)
                base[0, q] = flat
                base[1, q] = steep
            else:
                flat = base[0, q]
                steep = base[1, q]
            weight = lin[t * HR : (t + 1) * HR, :]
            pre = jnp.dot(weight, flat, preferred_element_type=F32)
            dpre = jnp.dot(weight, steep, preferred_element_type=F32)
            env16 = jnp.concatenate([yb[q, 9], yb[q, 9]], axis=0)
            denv16 = jnp.concatenate([yb[q, 10], yb[q, 10]], axis=0)
            for r in range(HR // 16):
                rows = slice(r * 16, (r + 1) * 16)
                x = pre[rows]
                sig = 1.0 / (1.0 + jnp.exp(-x))
                h = x * sig
                dh = (sig + h * (1.0 - sig)) * dpre[rows]
                for v, value in enumerate((env16 * h, denv16 * h + env16 * dh)):
                    high, low = pieces(value, 2)
                    high = high.astype(BF16)
                    xs[t, v, q, r * 16 : (r + 1) * 16, :] = high
                    xs[t, v, q, HR + r * 16 : HR + (r + 1) * 16, :] = low.astype(BF16)
                    xs[t, v, q, 2 * HR + r * 16 : 2 * HR + (r + 1) * 16, :] = high

        blocks(Q, 4, block)

    def radial_blocks(t, v, target):
        def block(q):
            target[t, q] = jnp.dot(wst[t], xs[t, v, q], preferred_element_type=F32)

        blocks(Q, Q, block)

    def gather_blocks(t):
        def block(q):
            if t == 0:
                element = yb[q, 11].astype(jnp.int32) - 1
                element = jnp.concatenate([element] * (S // 8), axis=0)
                choice = jnp.where(rows_iota(S, W) == element, 1.0, 0.0).astype(BF16)
                choice = jnp.concatenate([choice, choice], axis=0)
                hup[t, q] = jnp.dot(tab[...], choice, preferred_element_type=F32)
            else:
                lanes = pl.ds(pl.multiple_of(q * W, W), W)
                both = jnp.dot(hl[q // 8], hot[:, lanes], preferred_element_type=F32)
                hup[t, q] = both[0:C] + both[C:]

        blocks(Q, 8 if t else Q, block)

    def moments(t):
        def block(q, carry):
            b = q // 8
            for ct in range(C // 8):
                rows = slice(ct * 8, ct * 8 + 8)
                sums = [mom[t, b, m, rows, :] for m in range(9)]
                for half in range(2):
                    lanes = slice(half * S, half * S + S)
                    h = hup[t, q, rows, lanes]
                    sums[0] = sums[0] + rad[t, q, rows, lanes] * h
                    h1 = rad[t, q, C + ct * 8 : C + ct * 8 + 8, lanes] * h
                    h2 = rad[t, q, 2 * C + ct * 8 : 2 * C + ct * 8 + 8, lanes] * h
                    for m in range(3):
                        sums[1 + m] = sums[1 + m] + yb[q, m, :, lanes] * h1
                    for m in range(3, 8):
                        sums[1 + m] = sums[1 + m] + yb[q, m, :, lanes] * h2
                for m in range(9):
                    mom[t, b, m, rows, :] = sums[m]
            return carry

        lax.fori_loop(0, Q, block, 0)

    filled = jnp.concatenate(
        [jnp.where(pos[5 + b, 3:4, :] > 0.0, 1.0, 0.0) for b in range(2)], axis=1
    )

    def features(t, own):
        inv0 = jnp.concatenate([mom[t, b, 0] for b in range(2)], axis=1) * message_scale
        inv1 = jnp.concatenate(
            [sum(mom[t, b, m] * mom[t, b, m] for m in range(1, 4)) for b in range(2)], axis=1
        )
        inv2 = jnp.concatenate(
            [sum(mom[t, b, m] * mom[t, b, m] for m in range(4, 9)) for b in range(2)], axis=1
        )
        scale = message_scale * message_scale
        inv = jnp.concatenate([inv0, inv1 * scale, inv2 * scale], axis=0)
        return product(mix_w[t], jnp.concatenate([own, inv], axis=0)) * filled

    def read_column(t):
        return jnp.broadcast_to(read_ref[t : t + 1, :], (C, C)).T

    def energies(t, values):
        column = read_column(t)
        return jnp.concatenate(
            [
                jnp.sum(values[:, b * S : (b + 1) * S] * column, axis=0, keepdims=True)
                for b in range(2)
            ],
            axis=1,
        )

    def moment_grads(t, inner):
        for b in range(2):
            lanes = slice(b * S, (b + 1) * S)
            gmom[b, 0] = inner[0:C, lanes] * message_scale
            scale = 2.0 * message_scale * message_scale
            for m in range(1, 9):
                rows = slice(C, 2 * C) if m < 4 else slice(2 * C, 3 * C)
                gmom[b, m] = inner[rows, lanes] * mom[t, b, m] * scale

    hidden_blocks(0)
    radial_blocks(0, 0, rad)
    gather_blocks(0)
    moments(0)
    own_element = jnp.concatenate([pos[5 + b, 3:4, :] for b in range(2)], axis=1)
    own_hot = jnp.where(
        rows_iota(S, 2 * S) == jnp.broadcast_to(own_element.astype(jnp.int32) - 1, (S, 2 * S)),
        1.0,
        0.0,
    ).astype(BF16)
    start = jnp.dot(emb_t[...], own_hot, preferred_element_type=F32)
    start = start[0:C] + start[C : 2 * C] + start[2 * C :]
    first = features(0, start)
    feat[0] = first
    own_up = product(up_w[0], first)
    rim[5] = own_up[:, 0:S]
    rim[6] = own_up[:, S:]
    up_copies = [
        remote(8, rim.at[5], rim.at[7], (gx, down)),
        remote(9, rim.at[6], rim.at[4], (gx, up)),
        remote(10, rim.at[pl.ds(5, 2)], rim.at[pl.ds(9, 2)], (left, gy)),
        remote(11, rim.at[pl.ds(5, 2)], rim.at[pl.ds(1, 2)], (right, gy)),
    ]
    for copy in up_copies:
        copy.start()
    first_energy = energies(0, first)

    hidden_blocks(1)
    radial_weights(1)
    radial_blocks(1, 0, rad)
    up_copies[0].wait_recv()
    up_copies[1].wait_recv()
    far_copies = [
        remote(12, rim.at[4], rim.at[8], (left, gy)),
        remote(13, rim.at[4], rim.at[0], (right, gy)),
        remote(14, rim.at[7], rim.at[11], (left, gy)),
        remote(15, rim.at[7], rim.at[3], (right, gy)),
    ]
    for copy in far_copies:
        copy.start()
    radial_blocks(0, 1, drad)
    mix_weights(1)
    back_weights(0)
    back_weights(1)
    up_w[1] = wide(up_ref[1])
    radial_blocks(1, 1, drad)
    for copy in up_copies[2:] + far_copies:
        copy.wait_recv()

    for a in range(3):
        for r in range(4):
            high, low = pieces(rim[a * 4 + r], 2)
            value = jnp.concatenate([high, low], axis=0).astype(BF16)
            for b in range(2):
                if 0 <= r - b < 3:
                    c = a * 3 + r - b
                    hl[b, :, c * S : (c + 1) * S] = value

    gather_blocks(1)
    moments(1)
    second = features(1, feat[0])
    atom_energy = first_energy + energies(1, second)
    for b in range(2):
        energy_ref[0, b : b + 1, :] = atom_energy[:, b * S : (b + 1) * S]

    def reduce_send(phase, value):
        ar_out[phase] = value
        ar_in[phase, digits[phase]] = value
        copies = [
            remote(
                32 + phase * 3 + step - 1,
                ar_out.at[phase],
                ar_in.at[phase, digits[phase]],
                partner(phase, step),
            )
            for step in (1, 2, 3)
        ]
        for copy in copies:
            copy.start()
        return copies

    def reduce_wait(phase, copies):
        for copy in copies:
            copy.wait()
        return (ar_in[phase, 0] + ar_in[phase, 1]) + (ar_in[phase, 2] + ar_in[phase, 3])

    pair = atom_energy[:, 0:S] + atom_energy[:, S:]
    reduced = reduce_send(0, jnp.broadcast_to(jnp.sum(pair, axis=1, keepdims=True), (8, S)))

    grad1 = jnp.concatenate([read_column(1)] * 2, axis=1) * filled
    inner1 = product(back_w[1], grad1)
    moment_grads(1, inner1)

    def harmonics(q, half, rows, b, twice):
        lanes = slice(half * S, half * S + S)

        def spread(m):
            value = yb[q, m, :, lanes]
            return jnp.concatenate([value, value], axis=0) if twice else value

        a1 = sum(spread(m) * gmom[b, 1 + m, rows, :] for m in range(3))
        a2 = sum(spread(m) * gmom[b, 1 + m, rows, :] for m in range(3, 8))
        return a1, a2

    def feature_block(q, carry):
        b = q // 8
        for half in range(2):
            lanes = slice(half * S, half * S + S)
            for ct in range(C // 16):
                rows = slice(ct * 16, ct * 16 + 16)
                a1, a2 = harmonics(q, half, rows, b, True)
                value = (
                    rad[1, q, rows, lanes] * gmom[b, 0, rows, :]
                    + rad[1, q, C + ct * 16 : C + ct * 16 + 16, lanes] * a1
                    + rad[1, q, 2 * C + ct * 16 : 2 * C + ct * 16 + 16, lanes] * a2
                )
                high, low = pieces(value, 2)
                target = pl.ds(pl.multiple_of(q * W + half * S, S), S)
                dhl[rows, target] = high.astype(BF16)
                dhl[C + ct * 16 : C + ct * 16 + 16, target] = low.astype(BF16)
        return carry

    lax.fori_loop(0, Q, feature_block, 0)

    def scatter(a):
        half = []
        for b in range(2):
            lanes = slice(b * K * S, (b + 1) * K * S)
            both = nt(dhl[:, lanes], hot[a * 3 * S : (a + 1) * 3 * S, lanes])
            half.append(both[0:C] + both[C:])
        rgrad[a * 4] = half[0][:, 0:S]
        rgrad[a * 4 + 1] = half[0][:, S : 2 * S] + half[1][:, 0:S]
        rgrad[a * 4 + 2] = half[0][:, 2 * S :] + half[1][:, S : 2 * S]
        rgrad[a * 4 + 3] = half[1][:, 2 * S :]

    def column_copies(a, number, target, device):
        return [
            remote(number, rgrad.at[a * 4], gx_in.at[target, 0], device),
            remote(number + 1, rgrad.at[a * 4 + 3], gx_in.at[target, 3], device),
            remote(
                number + 2,
                rgrad.at[pl.ds(a * 4 + 1, 2)],
                gx_in.at[target, pl.ds(1, 2)],
                device,
            ),
        ]

    scatter(0)
    to_left = column_copies(0, 16, 0, (left, gy))
    for copy in to_left:
        copy.start()
    scatter(2)
    to_right = column_copies(2, 19, 1, (right, gy))
    for copy in to_right:
        copy.start()
    scatter(1)

    def position_block(t):
        def block(q, carry):
            b = q // 8
            for half in range(2):
                lanes = slice(half * S, half * S + S)
                sums = [jnp.zeros((8, S), F32)] * 9
                for ct in range(C // 8):
                    rows = slice(ct * 8, ct * 8 + 8)
                    rows1 = slice(C + ct * 8, C + ct * 8 + 8)
                    rows2 = slice(2 * C + ct * 8, 2 * C + ct * 8 + 8)
                    a1, a2 = harmonics(q, half, rows, b, False)
                    h = hup[t, q, rows, lanes]
                    h1 = rad[t, q, rows1, lanes] * h
                    h2 = rad[t, q, rows2, lanes] * h
                    slope = (
                        drad[t, q, rows, lanes] * gmom[b, 0, rows, :]
                        + drad[t, q, rows1, lanes] * a1
                        + drad[t, q, rows2, lanes] * a2
                    )
                    sums[8] = sums[8] + slope * h
                    for m in range(3):
                        sums[m] = sums[m] + gmom[b, 1 + m, rows, :] * h1
                    for m in range(3, 8):
                        sums[m] = sums[m] + gmom[b, 1 + m, rows, :] * h2
                k = (q - b * 8) * 2 + half
                for m in range(9):
                    total = jnp.sum(sums[m], axis=0, keepdims=True)
                    edge[b, m, pl.ds(k, 1), :] = edge[b, m, pl.ds(k, 1), :] + total
            return carry

        lax.fori_loop(0, Q, block, 0)

    position_block(1)
    for group in (to_left, to_right):
        group[0].wait_recv()
        group[1].wait_recv()
    rgrad[4] = rgrad[4] + gx_in[0, 0] + gx_in[1, 0]
    rgrad[7] = rgrad[7] + gx_in[0, 3] + gx_in[1, 3]
    row_copies = [
        remote(22, rgrad.at[4], gy_in.at[0], (gx, down)),
        remote(23, rgrad.at[7], gy_in.at[1], (gx, up)),
    ]
    for copy in row_copies:
        copy.start()
    reduced = reduce_send(1, reduce_wait(0, reduced))
    to_left[2].wait_recv()
    to_right[2].wait_recv()
    own_low = rgrad[5] + gx_in[0, 1] + gx_in[1, 1]
    own_high = rgrad[6] + gx_in[0, 2] + gx_in[1, 2]
    direct = jnp.concatenate([read_column(0)] * 2, axis=1) + inner1[3 * C :]
    for copy in row_copies:
        copy.wait_recv()
    returned = jnp.concatenate([own_low + gy_in[1], own_high + gy_in[0]], axis=1)
    grad0 = (direct + product(up_w[1], returned)) * filled

    moment_grads(0, product(back_w[0, 0 : 3 * C], grad0))
    reduced = reduce_send(2, reduce_wait(1, reduced))
    position_block(0)
    reduced = reduce_send(3, reduce_wait(2, reduced))

    direct_force = []
    for b in range(2):
        distance, ux, uy, uz, which, slot = unit[b]
        dy = [edge[b, m] for m in range(9)]
        gux = R3 * dy[0] + R15 * (uy * dy[3] + uz * dy[6] + ux * dy[7]) - R5 * ux * dy[5]
        guy = R3 * dy[1] + R15 * (ux * dy[3] + uz * dy[4] - uy * dy[7]) - R5 * uy * dy[5]
        guz = R3 * dy[2] + R15 * (uy * dy[4] + ux * dy[6]) + (2.0 * R5) * uz * dy[5]
        along = ux * gux + uy * guy + uz * guz
        grads = [
            (g - u * along) / distance + u * dy[8]
            for g, u in ((gux, ux), (guy, uy), (guz, uz))
        ]
        direct_force.append([jnp.sum(g, axis=0, keepdims=True) for g in grads])
        total = jnp.zeros((9 * K, S), F32)
        for k in range(K):
            bins = jnp.broadcast_to(which[k : k + 1, :], (K, S))
            here = rows_iota(K, S) == bins
            values = []
            for g in grads:
                values.append(
                    jnp.where(here, jnp.broadcast_to(g[k : k + 1, :], (K, S)), 0.0)
                )
            stack = jnp.concatenate(values, axis=0)
            stack = jnp.concatenate(pieces(stack, 3), axis=0).astype(BF16)
            place = jnp.where(
                rows_iota(S, S) == jnp.broadcast_to(slot[k : k + 1, :], (S, S)), 1.0, 0.0
            ).astype(BF16)
            total = total + nt(stack, place)
        total = total[0 : 3 * K] + total[3 * K : 6 * K] + total[6 * K :]
        for c in range(9):
            source = (c // 3) * 4 + b + c % 3
            for d in range(3):
                row = total[d * K + c : d * K + c + 1, :]
                if b == 0 or c % 3 == 2:
                    pgrad[source, d : d + 1, :] = row
                else:
                    pgrad[source, d : d + 1, :] = pgrad[source, d : d + 1, :] + row
    for source in range(12):
        pgrad[source, 3:8, :] = jnp.zeros((5, S), F32)
    back_copies = [
        remote(24, pgrad.at[pl.ds(1, 2)], pg_in.at[pl.ds(0, 2)], (left, gy)),
        remote(25, pgrad.at[pl.ds(9, 2)], pg_in.at[pl.ds(2, 2)], (right, gy)),
        remote(26, pgrad.at[4], pg_in.at[4], (gx, down)),
        remote(27, pgrad.at[7], pg_in.at[5], (gx, up)),
        remote(28, pgrad.at[0], pg_in.at[6], (left, down)),
        remote(29, pgrad.at[3], pg_in.at[7], (left, up)),
        remote(30, pgrad.at[8], pg_in.at[8], (right, down)),
        remote(31, pgrad.at[11], pg_in.at[9], (right, up)),
    ]
    for copy in back_copies:
        copy.start()
    total_ref[...] = reduce_wait(3, reduced)[0:1, 0:1]
    for copy in back_copies:
        copy.wait_recv()
    low_grad = pgrad[5] + pg_in[0] + pg_in[2] + pg_in[5] + pg_in[7] + pg_in[9]
    high_grad = pgrad[6] + pg_in[1] + pg_in[3] + pg_in[4] + pg_in[6] + pg_in[8]
    for b, returned in enumerate((low_grad, high_grad)):
        for d in range(3):
            force_ref[d, 0, b : b + 1, :] = direct_force[b][d] - returned[d : d + 1, :]
    for copy in pos_copies + up_copies + far_copies + to_left + to_right:
        copy.wait_send()
    for copy in row_copies + back_copies:
        copy.wait_send()


def on_device(shape, *arguments):
    vmem = pl.BlockSpec(memory_space=pltpu.VMEM)
    scratch = [
        ((12, 8, S), F32),
        ((9 * S, 2 * K * S), BF16),
        ((Q, 12, 8, W), F32),
        ((2, 2, Q, 3 * HR, W), BF16),
        ((2, Q, 3 * C, W), F32),
        ((2, Q, 3 * C, W), F32),
        ((2, Q, C, W), F32),
        ((2, 2, 9, C, S), F32),
        ((2, 9, C, S), F32),
        ((12, C, S), F32),
        ((2, 2 * C, 9 * S), BF16),
        ((2 * C, 2 * K * S), BF16),
        ((12, C, S), F32),
        ((2, 4, C, S), F32),
        ((2, C, S), F32),
        ((2, 9, K, S), F32),
        ((12, 8, S), F32),
        ((10, 8, S), F32),
        ((2, 3 * C, 3 * HR), BF16),
        ((2 * HR, 6 * NB), BF16),
        ((C, 2 * S), BF16),
        ((2, C, 12 * C), BF16),
        ((2, 4 * C, 3 * C), BF16),
        ((2, C, 3 * C), BF16),
        ((2, Q, 6 * NB, W), BF16),
        ((3 * C, S), BF16),
        ((S, S), F32),
        ((2, C, 2 * S), F32),
        ((4, 8, S), F32),
        ((4, 4, 8, S), F32),
    ]
    forces, energy, total = pl.pallas_call(
        functools.partial(kernel, shape),
        out_shape=(
            jax.ShapeDtypeStruct((3, 1, 2, S), F32),
            jax.ShapeDtypeStruct((1, 2, S), F32),
            jax.ShapeDtypeStruct((1, 1), F32),
        ),
        in_specs=[vmem] * 10,
        out_specs=(vmem, vmem, vmem),
        scratch_shapes=[pltpu.VMEM(dims, kind) for dims, kind in scratch]
        + [pltpu.SemaphoreType.DMA((44,)), pltpu.SemaphoreType.DMA((44,))],
        compiler_params=pltpu.CompilerParams(
            collective_id=0, has_side_effects=True, vmem_limit_bytes=60 * 1024 * 1024
        ),
    )(*arguments)
    return forces, energy, total.reshape(())


def solution(mesh):
    placed = (
        P(None, "gx", "gy", None),
        P("gx", "gy", None),
        P("gx", "gy", None, None),
        P(),
        P(),
        P(),
        P(),
        P(),
        P(),
        P(),
    )
    return jax.shard_map(
        functools.partial(on_device, (mesh.shape["gx"], mesh.shape["gy"])),
        mesh=mesh,
        in_specs=placed,
        out_specs=(P(None, "gx", "gy", None), P("gx", "gy", None), P()),
        check_vma=False,
    )
```

```python
import functools
import math

import jax
import jax.numpy as jnp
from jax import lax
from jax.experimental import pallas as pl
from jax.experimental.pallas import tpu as pltpu
from jax.sharding import PartitionSpec as P

bin_width = 6.0
slab_height = 12.0
cutoff = 6.0
softening = 0.25
spread_width = 0.75
message_scale = 1.5

S = 128
C = 128
K = 16
HR = 64
NB = 8
NSPEC = 89
ORDER = ((3, 4, 5, 1, 2, 7, 8, 0, 6), (3, 4, 5, 0, 1, 6, 7, 2, 8))
Q = 16
W = 256
MESH = pl.DeviceIdType.MESH
F32 = jnp.float32
BF16 = jnp.bfloat16
HIGH = lax.Precision.HIGHEST
R3 = math.sqrt(3.0)
R5 = math.sqrt(5.0)
R15 = math.sqrt(15.0)


def exact(a, b):
    return jnp.dot(a, b, precision=HIGH, preferred_element_type=F32)


def pieces(x, count):
    parts = []
    for _ in range(count):
        part = x.astype(BF16).astype(F32)
        parts.append(part)
        x = x - part
    return parts


def wide(weight):
    high, low = pieces(weight, 2)
    return jnp.concatenate([high, high, low], axis=1).astype(BF16)


def tall(value):
    high, low = pieces(value, 2)
    return jnp.concatenate([high, low, high], axis=0).astype(BF16)


def product(weight, value):
    return jnp.dot(weight, tall(value), preferred_element_type=F32)


def blocks(count, unroll, step):
    def several(i, carry):
        for u in range(unroll):
            step(i * unroll + u)
        return carry

    if unroll == count:
        several(0, 0)
    else:
        lax.fori_loop(0, count // unroll, several, 0)


def nt(a, b):
    return lax.dot_general(a, b, (((1,), (1,)), ((), ())), preferred_element_type=F32)


def rows_iota(rows, cols):
    return lax.broadcasted_iota(jnp.int32, (rows, cols), 0)


SCRATCH = (
    ("pos", (12, 8, S), F32),
    ("hot", (9 * S, 2 * K * S), BF16),
    ("place", (S, 2 * K * S), BF16),
    ("mask", (2, K, K * S), F32),
    ("yb", (Q, 12, 8, W), F32),
    ("base", (2, Q, 6 * NB, W), BF16),
    ("xs", (2, Q, 3 * HR, W), BF16),
    ("rad", (2, Q, 3 * C, W), F32),
    ("drad", (2, Q, 3 * C, W), F32),
    ("hup", (2, Q, C, W), F32),
    ("mom", (2, 2, 9, C, S), F32),
    ("gmom", (2, 9, C, S), F32),
    ("comb", (2, 6, C, S), F32),
    ("rim", (12, C, S), F32),
    ("hl", (2, 2 * C, 9 * S), BF16),
    ("dhl", (2 * C, 2 * K * S), BF16),
    ("rgrad", (12, C, S), F32),
    ("gx_in", (2, 4, C, S), F32),
    ("gy_in", (2, C, S), F32),
    ("edge", (2, 9, K, S), F32),
    ("pgrad", (12, 8, S), F32),
    ("pg_in", (10, 8, S), F32),
    ("wst", (2, 3 * C, 3 * HR), BF16),
    ("lin", (2 * HR, 6 * NB), BF16),
    ("tab", (C, 2 * S), BF16),
    ("mix_w", (2, C, 12 * C), BF16),
    ("back_w", (2, 4 * C, 3 * C), BF16),
    ("up_w", (2, C, 3 * C), BF16),
    ("emb_t", (3 * C, S), BF16),
    ("pad", (S, S), F32),
    ("first", (C, 2 * S), F32),
    ("begin", (C, 2 * S), F32),
    ("inner1", (4 * C, 2 * S), F32),
    ("ar_out", (4, 8, S), F32),
    ("ar_in", (4, 4, 8, S), F32),
    ("emb_ref", (NSPEC, C), F32),
    ("up_ref", (2, C, C), F32),
    ("rin_ref", (2, NB, HR), F32),
    ("rout_ref", (2, HR, 3 * C), F32),
    ("self_ref", (2, C, C), F32),
    ("prod_ref", (2, 3 * C, C), F32),
    ("read_ref", (2, C), F32),
)
WEIGHTS = ("emb_ref", "up_ref", "rin_ref", "rout_ref", "self_ref", "prod_ref", "read_ref")
COPIES = 72


def kernel(shape, frac_ref, spec_ref, nbr_ref, *refs):
    weights_in, refs = refs[:7], refs[7:]
    force_ref, energy_ref, total_ref = refs[:3]
    send_sem, recv_sem, load_sem = refs[-3:]
    scr = dict(zip([name for name, _, _ in SCRATCH], refs[3:-3]))
    (
        pos, hot, place, mask, yb, base, xs, rad, drad, hup, mom, gmom, comb, rim, hl, dhl, rgrad,
        gx_in, gy_in, edge, pgrad, pg_in, wst, lin, tab, mix_w, back_w, up_w, emb_t, pad, first_ref,
        begin, inner1_ref, ar_out, ar_in, emb_ref, up_ref, rin_ref, rout_ref, self_ref, prod_ref,
        read_ref,
    ) = [scr[name] for name, _, _ in SCRATCH]
    gxn, gyn = shape
    gx = lax.axis_index("gx")
    gy = lax.axis_index("gy")
    left = (lax.rem(gx + gxn - 1, gxn), gy)
    right = (lax.rem(gx + 1, gxn), gy)
    down = (gx, lax.rem(gy + gyn - 1, gyn))
    up = (gx, lax.rem(gy + 1, gyn))
    left_down, left_up = (left[0], down[1]), (left[0], up[1])
    right_down, right_up = (right[0], down[1]), (right[0], up[1])
    around = [left, right, down, up, left_down, left_up, right_down, right_up]
    digits = [gy, lax.rem(gx, 4), lax.rem(gx // 4, 4), gx // 16]

    def partner(phase, step):
        other = lax.rem(digits[phase] + step, 4)
        if phase == 0:
            return (gx, other)
        return (gx + (other - digits[phase]) * 4 ** (phase - 1), gy)

    barrier = pltpu.get_barrier_semaphore()
    greeted = around + [partner(phase, step) for phase in range(4) for step in (1, 2, 3)]
    for device in greeted:
        pl.semaphore_signal(barrier, inc=1, device_id=device, device_id_type=MESH)
    loads = [
        pltpu.make_async_copy(source, scr[name], load_sem.at[n])
        for n, (source, name) in enumerate(zip(weights_in, WEIGHTS))
    ]
    for load in loads:
        load.start()

    made = []

    def remote(source, target, device):
        number = len(made)
        copy = pltpu.make_async_remote_copy(
            src_ref=source,
            dst_ref=target,
            send_sem=send_sem.at[number],
            recv_sem=recv_sem.at[number],
            device_id=device,
            device_id_type=MESH,
        )
        made.append(copy)
        copy.start()
        return copy

    def arrived(copies):
        for copy in copies:
            copy.wait_recv()

    pos[5:7] = jnp.zeros((2, 8, S), F32)
    for b in range(2):
        for d in range(3):
            pos[5 + b, d : d + 1, :] = frac_ref[d, 0, b : b + 1, :]
        pos[5 + b, 3:4, :] = spec_ref[0, b : b + 1, :].astype(F32)

    def hot_rows(b):
        def block(k, carry):
            code = nbr_ref[0, b, pl.ds(k, 1), :]
            lanes = pl.ds(pl.multiple_of((b * K + k) * S, S), S)
            for n, c in enumerate(ORDER[b]):
                match = rows_iota(S, S) == jnp.broadcast_to(code - c * S, (S, S))
                hot[n * S : (n + 1) * S, lanes] = jnp.where(match, 1.0, 0.0).astype(BF16)
            return carry

        lax.fori_loop(0, K, block, 0)

    hot_rows(0)

    for load in loads:
        load.wait()

    def radial_weights(t):
        w1, w2 = pieces(rout_ref[t], 2)
        wst[t] = jnp.concatenate([w1, w1, w2], axis=0).T.astype(BF16)

    def mix_weights(t):
        mix_w[t] = wide(jnp.concatenate([self_ref[t].T, prod_ref[t].T], axis=1))

    def back_weights(t):
        back_w[t] = wide(jnp.concatenate([prod_ref[t], self_ref[t]], axis=0))

    def read_column(t):
        return jnp.broadcast_to(read_ref[t : t + 1, :], (C, C)).T

    pl.semaphore_wait(barrier, len(greeted))
    pos_copies = [
        remote(pos.at[5], pos.at[11], left_down),
        remote(pos.at[6], pos.at[8], left_up),
        remote(pos.at[5], pos.at[3], right_down),
        remote(pos.at[6], pos.at[0], right_up),
        remote(pos.at[pl.ds(5, 2)], pos.at[pl.ds(9, 2)], left),
        remote(pos.at[pl.ds(5, 2)], pos.at[pl.ds(1, 2)], right),
        remote(pos.at[5], pos.at[7], down),
        remote(pos.at[6], pos.at[4], up),
    ]

    hot_rows(1)
    for t in range(2):
        w1, w2, w3 = pieces(rin_ref[t], 3)
        stack = jnp.concatenate([w1, w1, w2, w1, w2, w3], axis=0)
        pad[...] = jnp.zeros_like(pad)
        pad[0 : 6 * NB, 0:HR] = stack
        lin[t * HR : (t + 1) * HR, :] = pad[...].T[0:HR, 0 : 6 * NB].astype(BF16)
    pad[...] = jnp.zeros_like(pad)
    pad[0:NSPEC, :] = emb_ref[...]
    table = exact(pad[...], up_ref[0])
    tab[...] = jnp.concatenate(pieces(table.T, 2), axis=1).astype(BF16)
    radial_weights(0)
    mix_weights(0)
    up_w[0] = wide(up_ref[1].T)
    emb_t[...] = jnp.concatenate(pieces(pad[...].T, 3), axis=0).astype(BF16)
    own_element = jnp.concatenate([pos[5 + b, 3:4, :] for b in range(2)], axis=1)
    own_hot = jnp.where(
        rows_iota(S, 2 * S) == jnp.broadcast_to(own_element.astype(jnp.int32) - 1, (S, 2 * S)),
        1.0,
        0.0,
    ).astype(BF16)
    value = jnp.dot(emb_t[...], own_hot, preferred_element_type=F32)
    begin[...] = value[0:C] + value[C : 2 * C] + value[2 * C :]
    mom[...] = jnp.zeros_like(mom)
    edge[...] = jnp.zeros_like(edge)
    for b in range(2):
        for k in range(K):
            lanes = slice(k * S, (k + 1) * S)
            code = jnp.broadcast_to(nbr_ref[0, b, k : k + 1, :], (S, S))
            slots = lax.bitwise_and(code, S - 1)
            both = slice((b * K + k) * S, (b * K + k + 1) * S)
            place[:, both] = jnp.where(rows_iota(S, S) == slots, 1.0, 0.0).astype(BF16)
            bins = lax.shift_right_logical(code[0:K], 7)
            mask[b, :, lanes] = jnp.where(rows_iota(K, S) == bins, 1.0, 0.0)

    arrived(pos_copies)

    unit = []
    for b in range(2):
        codes = nbr_ref[0, b]
        which = lax.shift_right_logical(codes, 7)
        slot = lax.bitwise_and(codes, S - 1)
        step_x = lax.shift_right_logical(which * 11, 5)
        step_y = which - 3 * step_x
        far = [jnp.zeros((K, S), F32)] * 4
        for c in range(9):
            source = (c // 3) * 4 + b + c % 3
            chosen = which == c
            for d in range(4):
                row = jnp.broadcast_to(pos[source, d : d + 1, :], (K, S))
                taken = jnp.take_along_axis(row, slot, axis=1, mode="promise_in_bounds")
                far[d] = jnp.where(chosen, taken, far[d])
        near = [pos[5 + b, d : d + 1, :] for d in range(3)]
        delta_x = ((step_x - 1).astype(F32) + far[0] - near[0]) * bin_width
        delta_y = ((step_y - 1).astype(F32) + far[1] - near[1]) * bin_width
        delta_z = (far[2] - near[2]) * slab_height
        distance = jnp.sqrt(delta_x * delta_x + delta_y * delta_y + delta_z * delta_z + softening)
        ux = delta_x / distance
        uy = delta_y / distance
        uz = delta_z / distance
        unit.append((distance, ux, uy, uz))
        q1 = distance * (1.0 / cutoff)
        q2 = q1 * q1
        q4 = q2 * q2
        inside = q1 < 1.0
        env = jnp.where(inside, 1.0 + q4 * q1 * (-21.0 + q1 * (35.0 - 15.0 * q1)), 0.0)
        denv = jnp.where(
            inside, q4 * (-105.0 + q1 * (210.0 - 105.0 * q1)) * (1.0 / cutoff), 0.0
        )
        values = [
            R3 * ux,
            R3 * uy,
            R3 * uz,
            R15 * ux * uy,
            R15 * uy * uz,
            0.5 * R5 * (2.0 * uz * uz - ux * ux - uy * uy),
            R15 * ux * uz,
            0.5 * R15 * (ux * ux - uy * uy),
            distance,
            env,
            denv,
            far[3],
        ]
        for m, value in enumerate(values):
            for k in range(K):
                yb[b * 8 + k // 2, m, :, (k % 2) * S : (k % 2 + 1) * S] = jnp.broadcast_to(
                    value[k : k + 1, :], (8, S)
                )

    centers = rows_iota(NB, W).astype(F32) * (cutoff / (NB - 1))

    def stacked(value):
        b1, b2, b3 = pieces(value, 3)
        return jnp.concatenate([b1, b2, b1, b3, b2, b1], axis=0).astype(BF16)

    def hidden_blocks(t, want_value, want_slope):
        def block(q):
            weight = lin[t * HR : (t + 1) * HR, :]
            if t == 0:
                offset = yb[q, 8] - centers
                scaled = offset * (1.0 / spread_width)
                basis = jnp.exp(-(scaled * scaled))
                if want_value:
                    base[0, q] = stacked(basis)
                if want_slope:
                    base[1, q] = stacked(basis * (offset * (-2.0 / (spread_width * spread_width))))
            pre = jnp.dot(weight, base[0, q], preferred_element_type=F32)
            if want_slope:
                dpre = jnp.dot(weight, base[1, q], preferred_element_type=F32)
            env16 = jnp.concatenate([yb[q, 9], yb[q, 9]], axis=0)
            denv16 = jnp.concatenate([yb[q, 10], yb[q, 10]], axis=0)
            for r in range(HR // 16):
                rows = slice(r * 16, (r + 1) * 16)
                x = pre[rows]
                sig = 1.0 / (1.0 + jnp.exp(-x))
                h = x * sig
                found = []
                if want_value:
                    found.append((0, env16 * h))
                if want_slope:
                    dh = (sig + h * (1.0 - sig)) * dpre[rows]
                    found.append((1, denv16 * h + env16 * dh))
                for v, value in found:
                    high, low = pieces(value, 2)
                    high = high.astype(BF16)
                    xs[v, q, r * 16 : (r + 1) * 16, :] = high
                    xs[v, q, HR + r * 16 : HR + (r + 1) * 16, :] = low.astype(BF16)
                    xs[v, q, 2 * HR + r * 16 : 2 * HR + (r + 1) * 16, :] = high

        blocks(Q, 4, block)

    def radial_blocks(t, v, target):
        def block(q):
            target[t, q] = jnp.dot(wst[t], xs[v, q], preferred_element_type=F32)

        blocks(Q, Q, block)

    def element_blocks():
        def block(q):
            element = yb[q, 11].astype(jnp.int32) - 1
            element = jnp.concatenate([element] * (S // 8), axis=0)
            choice = jnp.where(rows_iota(S, W) == element, 1.0, 0.0).astype(BF16)
            choice = jnp.concatenate([choice, choice], axis=0)
            hup[0, q] = jnp.dot(tab[...], choice, preferred_element_type=F32)

        blocks(Q, Q, block)

    def gather_blocks(begin_bin, end_bin):
        part = slice(begin_bin * S, end_bin * S)

        def block(q):
            lanes = pl.ds(pl.multiple_of(q * W, W), W)
            both = jnp.dot(hl[q // 8, :, part], hot[part, lanes], preferred_element_type=F32)
            value = both[0:C] + both[C:]
            hup[1, q] = value if begin_bin == 0 else hup[1, q] + value

        blocks(Q, 8, block)

    def split_rim(begin_bin, end_bin):
        seen = {}
        for b in range(2):
            for n in range(begin_bin, end_bin):
                c = ORDER[b][n]
                source = (c // 3) * 4 + b + c % 3
                if source not in seen:
                    high, low = pieces(rim[source], 2)
                    seen[source] = jnp.concatenate([high, low], axis=0).astype(BF16)
                hl[b, :, n * S : (n + 1) * S] = seen[source]

    def moments(t):
        def block(i, carry):
            b = i // 4
            for ct in range(C // 8):
                rows = slice(ct * 8, ct * 8 + 8)
                rows1 = slice(C + ct * 8, C + ct * 8 + 8)
                rows2 = slice(2 * C + ct * 8, 2 * C + ct * 8 + 8)
                sums = [mom[t, b, m, rows, :] for m in range(9)]
                for part in range(4):
                    q = i * 2 + part // 2
                    lanes = slice(part % 2 * S, part % 2 * S + S)
                    h = hup[t, q, rows, lanes]
                    sums[0] = sums[0] + rad[t, q, rows, lanes] * h
                    h1 = rad[t, q, rows1, lanes] * h
                    h2 = rad[t, q, rows2, lanes] * h
                    for m in range(3):
                        sums[1 + m] = sums[1 + m] + yb[q, m, :, lanes] * h1
                    for m in range(3, 8):
                        sums[1 + m] = sums[1 + m] + yb[q, m, :, lanes] * h2
                for m in range(9):
                    mom[t, b, m, rows, :] = sums[m]
            return carry

        lax.fori_loop(0, Q // 2, block, 0)

    filled = jnp.concatenate(
        [jnp.where(pos[5 + b, 3:4, :] > 0.0, 1.0, 0.0) for b in range(2)], axis=1
    )

    def features(t, own):
        inv0 = jnp.concatenate([mom[t, b, 0] for b in range(2)], axis=1) * message_scale
        inv1 = jnp.concatenate(
            [sum(mom[t, b, m] * mom[t, b, m] for m in range(1, 4)) for b in range(2)], axis=1
        )
        inv2 = jnp.concatenate(
            [sum(mom[t, b, m] * mom[t, b, m] for m in range(4, 9)) for b in range(2)], axis=1
        )
        scale = message_scale * message_scale
        inv = jnp.concatenate([inv0, inv1 * scale, inv2 * scale], axis=0)
        return product(mix_w[t], jnp.concatenate([own, inv], axis=0)) * filled

    def energies(t, values):
        column = read_column(t)
        return jnp.concatenate(
            [
                jnp.sum(values[:, b * S : (b + 1) * S] * column, axis=0, keepdims=True)
                for b in range(2)
            ],
            axis=1,
        )

    hidden_blocks(0, True, False)
    radial_blocks(0, 0, rad)
    element_blocks()
    moments(0)
    first = features(0, begin[...])
    own_up = product(up_w[0], first)
    rim[5] = own_up[:, 0:S]
    rim[6] = own_up[:, S:]
    halves = [pl.ds(0, C // 2), pl.ds(C // 2, C // 2)]
    y_copies = [
        [
            remote(rim.at[5, half], rim.at[7, half], down),
            remote(rim.at[6, half], rim.at[4, half], up),
        ]
        for half in halves
    ]
    x_copies = [
        remote(rim.at[pl.ds(5, 2)], rim.at[pl.ds(9, 2)], left),
        remote(rim.at[pl.ds(5, 2)], rim.at[pl.ds(1, 2)], right),
    ]
    first_ref[...] = first

    first_energy = energies(0, first)
    hidden_blocks(0, False, True)
    radial_blocks(0, 1, drad)
    radial_weights(1)
    back_weights(1)
    grad1 = jnp.concatenate([read_column(1)] * 2, axis=1) * filled
    inner1_ref[...] = product(back_w[1], grad1)
    far_copies = []
    for half, group in zip(halves, y_copies):
        arrived(group)
        far_copies += [
            remote(rim.at[4, half], rim.at[8, half], left),
            remote(rim.at[4, half], rim.at[0, half], right),
            remote(rim.at[7, half], rim.at[11, half], left),
            remote(rim.at[7, half], rim.at[3, half], right),
        ]
    split_rim(0, 3)
    gather_blocks(0, 3)
    hidden_blocks(1, True, True)
    radial_blocks(1, 0, rad)
    arrived(x_copies)
    split_rim(3, 7)
    gather_blocks(3, 7)
    arrived(far_copies)

    split_rim(7, 9)
    gather_blocks(7, 9)
    moments(1)
    for b in range(2):
        lanes = slice(b * S, (b + 1) * S)
        gmom[b, 0] = inner1_ref[0:C, lanes] * message_scale
        scale = 2.0 * message_scale * message_scale
        for m in range(1, 9):
            rows = slice(C, 2 * C) if m < 4 else slice(2 * C, 3 * C)
            gmom[b, m] = inner1_ref[rows, lanes] * mom[1, b, m] * scale

    def feature_block(q, carry):
        b = q // 8
        for ct in range(C // 16):
            rows = slice(ct * 16, ct * 16 + 16)
            rows1 = slice(C + ct * 16, C + ct * 16 + 16)
            rows2 = slice(2 * C + ct * 16, 2 * C + ct * 16 + 16)
            grads = [gmom[b, m, rows, :] for m in range(9)]
            for half in range(2):
                lanes = slice(half * S, half * S + S)
                spread = [jnp.concatenate([yb[q, m, :, lanes]] * 2, axis=0) for m in range(8)]
                a1 = sum(spread[m] * grads[1 + m] for m in range(3))
                a2 = sum(spread[m] * grads[1 + m] for m in range(3, 8))
                value = (
                    rad[1, q, rows, lanes] * grads[0]
                    + rad[1, q, rows1, lanes] * a1
                    + rad[1, q, rows2, lanes] * a2
                )
                high, low = pieces(value, 2)
                target = pl.ds(pl.multiple_of(q * W + half * S, S), S)
                dhl[rows, target] = high.astype(BF16)
                dhl[C + ct * 16 : C + ct * 16 + 16, target] = low.astype(BF16)
        return carry

    lax.fori_loop(0, Q, feature_block, 0)

    def scatter(begin_bin, end_bin):
        found = {}
        for b in range(2):
            lanes = slice(b * K * S, (b + 1) * K * S)
            both = nt(dhl[:, lanes], hot[begin_bin * S : end_bin * S, lanes])
            value = both[0:C] + both[C:]
            for n in range(begin_bin, end_bin):
                c = ORDER[b][n]
                source = (c // 3) * 4 + b + c % 3
                piece = value[:, (n - begin_bin) * S : (n - begin_bin + 1) * S]
                found[source] = found[source] + piece if source in found else piece
        for source, value in found.items():
            rgrad[source] = value

    scatter(7, 9)
    corner_copies = [
        [
            remote(rgrad.at[0, half], gx_in.at[0, 0, half], left),
            remote(rgrad.at[8, half], gx_in.at[1, 0, half], right),
            remote(rgrad.at[3, half], gx_in.at[0, 3, half], left),
            remote(rgrad.at[11, half], gx_in.at[1, 3, half], right),
        ]
        for half in halves
    ]
    scatter(3, 7)
    side_copies = [
        remote(rgrad.at[pl.ds(1, 2)], gx_in.at[0, pl.ds(1, 2)], left),
        remote(rgrad.at[pl.ds(9, 2)], gx_in.at[1, pl.ds(1, 2)], right),
    ]
    scatter(0, 3)

    def reduce_send(phase, value):
        ar_out[phase] = value
        ar_in[phase, digits[phase]] = value
        return [
            remote(ar_out.at[phase], ar_in.at[phase, digits[phase]], partner(phase, step))
            for step in (1, 2, 3)
        ]

    def reduce_wait(phase, copies):
        arrived(copies)
        return (ar_in[phase, 0] + ar_in[phase, 1]) + (ar_in[phase, 2] + ar_in[phase, 3])

    mix_weights(1)
    second = features(1, first_ref[...])
    atom_energy = first_energy + energies(1, second)
    for b in range(2):
        energy_ref[0, b : b + 1, :] = atom_energy[:, b * S : (b + 1) * S]
    pair = atom_energy[:, 0:S] + atom_energy[:, S:]
    reduced = reduce_send(0, jnp.broadcast_to(jnp.sum(pair, axis=1, keepdims=True), (8, S)))
    radial_blocks(1, 1, drad)

    row_copies = []
    for half, group in zip((slice(0, C // 2), slice(C // 2, C)), corner_copies):
        arrived(group)
        rgrad[4, half] = rgrad[4, half] + gx_in[0, 0, half] + gx_in[1, 0, half]
        rgrad[7, half] = rgrad[7, half] + gx_in[0, 3, half] + gx_in[1, 3, half]
        window = pl.ds(half.start, C // 2)
        row_copies += [
            remote(rgrad.at[4, window], gy_in.at[0, window], down),
            remote(rgrad.at[7, window], gy_in.at[1, window], up),
        ]

    def position_block(q, carry):
        b = q // 8
        sums = [[jnp.zeros((8, S), F32)] * 9 for _ in range(2)]
        for ct in range(C // 8):
            rows = slice(ct * 8, ct * 8 + 8)
            rows1 = slice(C + ct * 8, C + ct * 8 + 8)
            rows2 = slice(2 * C + ct * 8, 2 * C + ct * 8 + 8)
            grads = [gmom[b, m, rows, :] for m in range(9)]
            for half in range(2):
                lanes = slice(half * S, half * S + S)
                a1 = sum(yb[q, m, :, lanes] * grads[1 + m] for m in range(3))
                a2 = sum(yb[q, m, :, lanes] * grads[1 + m] for m in range(3, 8))
                h = hup[1, q, rows, lanes]
                h1 = rad[1, q, rows1, lanes] * h
                h2 = rad[1, q, rows2, lanes] * h
                slope = (
                    drad[1, q, rows, lanes] * grads[0]
                    + drad[1, q, rows1, lanes] * a1
                    + drad[1, q, rows2, lanes] * a2
                )
                now = sums[half]
                now[8] = now[8] + slope * h
                for m in range(3):
                    now[m] = now[m] + grads[1 + m] * h1
                for m in range(3, 8):
                    now[m] = now[m] + grads[1 + m] * h2
        for half in range(2):
            k = (q - b * 8) * 2 + half
            for m in range(9):
                edge[b, m, pl.ds(k, 1), :] = jnp.sum(sums[half][m], axis=0, keepdims=True)
        return carry

    lax.fori_loop(0, Q, position_block, 0)
    reduced = reduce_send(1, reduce_wait(0, reduced))

    for b in range(2):
        m2 = [mom[0, b, 4 + m] for m in range(5)]
        comb[b, 0] = R5 * m2[0]
        comb[b, 1] = R5 * m2[1]
        comb[b, 2] = R5 * m2[3]
        comb[b, 3] = R5 * m2[4] - (R5 / R3) * m2[2]
        comb[b, 4] = -R5 * m2[4] - (R5 / R3) * m2[2]
        comb[b, 5] = (2.0 * R5 / R3) * m2[2]

    def product_block(q, carry):
        b = q // 8
        for ct in range(C // 8):
            rows = slice(ct * 8, ct * 8 + 8)
            rows1 = slice(C + ct * 8, C + ct * 8 + 8)
            rows2 = slice(2 * C + ct * 8, 2 * C + ct * 8 + 8)
            own = [mom[0, b, 1 + m, rows, :] for m in range(8)]
            mixed = [comb[b, m, rows, :] for m in range(6)]
            for half in range(2):
                lanes = slice(half * S, half * S + S)
                y = [yb[q, m, :, lanes] for m in range(8)]
                h = hup[0, q, rows, lanes]
                b1 = sum(y[m] * own[m] for m in range(3)) * h
                b2 = sum(y[m] * own[m] for m in range(3, 8)) * h
                h1 = rad[0, q, rows1, lanes] * h
                h2 = rad[0, q, rows2, lanes] * h
                drad[0, q, rows, lanes] = drad[0, q, rows, lanes] * h
                drad[0, q, rows1, lanes] = drad[0, q, rows1, lanes] * b1
                drad[0, q, rows2, lanes] = drad[0, q, rows2, lanes] * b2
                hup[0, q, rows, lanes] = h1
                rad[0, q, rows, lanes] = h2 * (y[1] * mixed[0] + y[2] * mixed[2] + y[0] * mixed[3])
                rad[0, q, rows1, lanes] = h2 * (y[0] * mixed[0] + y[2] * mixed[1] + y[1] * mixed[4])
                rad[0, q, rows2, lanes] = h2 * (y[1] * mixed[1] + y[0] * mixed[2] + y[2] * mixed[5])
        return carry

    lax.fori_loop(0, Q, product_block, 0)
    back_weights(0)
    up_w[1] = wide(up_ref[1])
    direct = jnp.concatenate([read_column(0)] * 2, axis=1) + inner1_ref[3 * C :]

    second_part = []
    for b in range(2):
        distance, ux, uy, uz = unit[b]
        dy = [edge[b, m] for m in range(9)]
        gux = R3 * dy[0] + R15 * (uy * dy[3] + uz * dy[6] + ux * dy[7]) - R5 * ux * dy[5]
        guy = R3 * dy[1] + R15 * (ux * dy[3] + uz * dy[4] - uy * dy[7]) - R5 * uy * dy[5]
        guz = R3 * dy[2] + R15 * (uy * dy[4] + ux * dy[6]) + (2.0 * R5) * uz * dy[5]
        second_part.append((gux, guy, guz, dy[8]))

    arrived(side_copies)
    own_low = rgrad[5] + gx_in[0, 1] + gx_in[1, 1]
    own_high = rgrad[6] + gx_in[0, 2] + gx_in[1, 2]
    arrived(row_copies)
    returned = jnp.concatenate([own_low + gy_in[1], own_high + gy_in[0]], axis=1)
    grad0 = (direct + product(up_w[1], returned)) * filled

    inner0 = product(back_w[0, 0 : 3 * C], grad0)
    scale = 2.0 * message_scale * message_scale
    for b in range(2):
        lanes = slice(b * S, (b + 1) * S)
        one = inner0[C : 2 * C, lanes] * scale
        comb[b, 0] = inner0[0:C, lanes] * message_scale
        comb[b, 1] = one
        comb[b, 2] = inner0[2 * C :, lanes] * scale
        for m in range(3):
            comb[b, 3 + m] = one * mom[0, b, 1 + m] * R3
    reduced = reduce_send(2, reduce_wait(1, reduced))

    def first_block(q, carry):
        b = q // 8
        sums = [[jnp.zeros((8, S), F32)] * 4 for _ in range(2)]
        for ct in range(C // 8):
            rows = slice(ct * 8, ct * 8 + 8)
            rows1 = slice(C + ct * 8, C + ct * 8 + 8)
            rows2 = slice(2 * C + ct * 8, 2 * C + ct * 8 + 8)
            grads = [comb[b, m, rows, :] for m in range(6)]
            for half in range(2):
                lanes = slice(half * S, half * S + S)
                now = sums[half]
                now[3] = (
                    now[3]
                    + drad[0, q, rows, lanes] * grads[0]
                    + drad[0, q, rows1, lanes] * grads[1]
                    + drad[0, q, rows2, lanes] * grads[2]
                )
                h1 = hup[0, q, rows, lanes]
                for d, part in enumerate((rows, rows1, rows2)):
                    now[d] = now[d] + grads[3 + d] * h1 + grads[2] * rad[0, q, part, lanes]
        for half in range(2):
            k = (q - b * 8) * 2 + half
            for m in range(4):
                edge[b, m, pl.ds(k, 1), :] = jnp.sum(sums[half][m], axis=0, keepdims=True)
        return carry

    lax.fori_loop(0, Q, first_block, 0)
    reduced = reduce_send(3, reduce_wait(2, reduced))

    direct_force = []
    for b in range(2):
        distance, ux, uy, uz = unit[b]
        gux, guy, guz, slope = [edge[b, m] + second_part[b][m] for m in range(4)]
        along = ux * gux + uy * guy + uz * guz
        grads = [
            (g - u * along) / distance + u * slope for g, u in ((gux, ux), (guy, uy), (guz, uz))
        ]
        direct_force.append([jnp.sum(g, axis=0, keepdims=True) for g in grads])
        columns = []
        for k in range(K):
            here = mask[b, :, k * S : (k + 1) * S]
            stack = [here * jnp.broadcast_to(g[k : k + 1, :], (K, S)) for g in grads]
            stack = pieces(jnp.concatenate(stack, axis=0), 2)
            columns.append(jnp.concatenate(stack, axis=0).astype(BF16))
        total = nt(jnp.concatenate(columns, axis=1), place[:, b * K * S : (b + 1) * K * S])
        total = total[0 : 3 * K] + total[3 * K :]
        for c in range(9):
            source = (c // 3) * 4 + b + c % 3
            for d in range(3):
                row = total[d * K + c : d * K + c + 1, :]
                if b == 0 or c % 3 == 2:
                    pgrad[source, d : d + 1, :] = row
                else:
                    pgrad[source, d : d + 1, :] = pgrad[source, d : d + 1, :] + row
    for source in range(12):
        pgrad[source, 3:8, :] = jnp.zeros((5, S), F32)
    back_copies = [
        remote(pgrad.at[0], pg_in.at[6], left_down),
        remote(pgrad.at[3], pg_in.at[7], left_up),
        remote(pgrad.at[8], pg_in.at[8], right_down),
        remote(pgrad.at[11], pg_in.at[9], right_up),
        remote(pgrad.at[pl.ds(1, 2)], pg_in.at[pl.ds(0, 2)], left),
        remote(pgrad.at[pl.ds(9, 2)], pg_in.at[pl.ds(2, 2)], right),
        remote(pgrad.at[4], pg_in.at[4], down),
        remote(pgrad.at[7], pg_in.at[5], up),
    ]
    total_ref[...] = reduce_wait(3, reduced)[0:1, 0:1]
    arrived(back_copies)
    low_grad = pgrad[5] + pg_in[0] + pg_in[2] + pg_in[5] + pg_in[7] + pg_in[9]
    high_grad = pgrad[6] + pg_in[1] + pg_in[3] + pg_in[4] + pg_in[6] + pg_in[8]
    for b, returned in enumerate((low_grad, high_grad)):
        for d in range(3):
            force_ref[d, 0, b : b + 1, :] = direct_force[b][d] - returned[d : d + 1, :]
    for copy in made:
        copy.wait_send()


def on_device(shape, *arguments):
    vmem = pl.BlockSpec(memory_space=pltpu.VMEM)
    anywhere = pl.BlockSpec(memory_space=pl.ANY)
    forces, energy, total = pl.pallas_call(
        functools.partial(kernel, shape),
        out_shape=(
            jax.ShapeDtypeStruct((3, 1, 2, S), F32),
            jax.ShapeDtypeStruct((1, 2, S), F32),
            jax.ShapeDtypeStruct((1, 1), F32),
        ),
        in_specs=[vmem] * 3 + [anywhere] * 7,
        out_specs=(vmem, vmem, vmem),
        scratch_shapes=[pltpu.VMEM(dims, kind) for _, dims, kind in SCRATCH]
        + [
            pltpu.SemaphoreType.DMA((COPIES,)),
            pltpu.SemaphoreType.DMA((COPIES,)),
            pltpu.SemaphoreType.DMA((len(WEIGHTS),)),
        ],
        compiler_params=pltpu.CompilerParams(
            collective_id=0, has_side_effects=True, vmem_limit_bytes=62 * 1024 * 1024
        ),
    )(*arguments)
    return forces, energy, total.reshape(())


def solution(mesh):
    placed = (
        P(None, "gx", "gy", None),
        P("gx", "gy", None),
        P("gx", "gy", None, None),
        P(),
        P(),
        P(),
        P(),
        P(),
        P(),
        P(),
    )
    return jax.shard_map(
        functools.partial(on_device, (mesh.shape["gx"], mesh.shape["gy"])),
        mesh=mesh,
        in_specs=placed,
        out_specs=(P(None, "gx", "gy", None), P("gx", "gy", None), P()),
        check_vma=False,
    )
```

```python
import functools
import math

import jax
import jax.numpy as jnp
from jax import lax
from jax.experimental import pallas as pl
from jax.experimental.pallas import tpu as pltpu
from jax.sharding import PartitionSpec as P

bin_width = 6.0
slab_height = 12.0
cutoff = 6.0
softening = 0.25
spread_width = 0.75
message_scale = 1.5

S = 128
C = 128
K = 16
HR = 64
NB = 8
NSPEC = 89
ORDER = ((3, 4, 5, 1, 2, 7, 8, 0, 6), (3, 4, 5, 0, 1, 6, 7, 2, 8))
Q = 16
W = 256
MESH = pl.DeviceIdType.MESH
F32 = jnp.float32
BF16 = jnp.bfloat16
HIGH = lax.Precision.HIGHEST
R3 = math.sqrt(3.0)
R5 = math.sqrt(5.0)
R15 = math.sqrt(15.0)


def exact(a, b):
    return jnp.dot(a, b, precision=HIGH, preferred_element_type=F32)


def pieces(x, count):
    parts = []
    for _ in range(count):
        part = x.astype(BF16).astype(F32)
        parts.append(part)
        x = x - part
    return parts


def wide(weight):
    high, low = pieces(weight, 2)
    return jnp.concatenate([high, high, low], axis=1).astype(BF16)


def tall(value):
    high, low = pieces(value, 2)
    return jnp.concatenate([high, low, high], axis=0).astype(BF16)


def product(weight, value):
    return jnp.dot(weight, tall(value), preferred_element_type=F32)


def blocks(count, unroll, step):
    def several(i, carry):
        for u in range(unroll):
            step(i * unroll + u)
        return carry

    if unroll == count:
        several(0, 0)
    else:
        lax.fori_loop(0, count // unroll, several, 0)


def nt(a, b):
    return lax.dot_general(a, b, (((1,), (1,)), ((), ())), preferred_element_type=F32)


def rows_iota(rows, cols):
    return lax.broadcasted_iota(jnp.int32, (rows, cols), 0)


SCRATCH = (
    ("pos", (12, 8, S), F32),
    ("hot", (9 * S, 2 * K * S), BF16),
    ("place", (S, 2 * K * S), BF16),
    ("mask", (2, K, K * S), F32),
    ("yb", (Q, 12, 8, W), F32),
    ("base", (2, Q, 6 * NB, W), BF16),
    ("xs", (3, Q, 3 * HR, W), BF16),
    ("rad", (2, Q, 3 * C, W), F32),
    ("drad", (2, Q, 3 * C, W), F32),
    ("hup", (2, Q, C, W), F32),
    ("mom", (2, 2, 9, C, S), F32),
    ("gmom", (2, 9, C, S), F32),
    ("comb", (2, 6, C, S), F32),
    ("rim", (12, C, S), F32),
    ("hl", (2, 2 * C, 9 * S), BF16),
    ("dhl", (2 * C, 2 * K * S), BF16),
    ("rgrad", (12, C, S), F32),
    ("side_in", (2, 2, C, S), F32),
    ("near_in", (2, C, S), F32),
    ("far_in", (C, S), F32),
    ("corner_in", (C, S), F32),
    ("gy_in", (2, C, S), F32),
    ("edge", (2, 9, K, S), F32),
    ("pgrad", (12, 8, S), F32),
    ("pg_in", (10, 8, S), F32),
    ("wst", (2, 3 * C, 3 * HR), BF16),
    ("lin", (2 * HR, 6 * NB), BF16),
    ("tab", (C, 2 * S), BF16),
    ("mix_w", (2 * C, 12 * C), BF16),
    ("back_w", (2, 4 * C, 3 * C), BF16),
    ("up_w", (3 * C, 3 * C), BF16),
    ("emb_t", (3 * C, S), BF16),
    ("pad", (S, S), F32),
    ("first", (C, 2 * S), F32),
    ("begin", (C, 2 * S), F32),
    ("inner1", (4 * C, 2 * S), F32),
    ("ar_out", (4, 8, S), F32),
    ("ar_in", (4, 4, 8, S), F32),
    ("a2", (Q, C, W), F32),
    ("frac_ref", (3, 1, 2, S), F32),
    ("spec_ref", (1, 2, S), jnp.int32),
    ("nbr_ref", (1, 2, K, S), jnp.int32),
    ("emb_ref", (NSPEC, C), F32),
    ("up_ref", (2, C, C), F32),
    ("rin_ref", (2, NB, HR), F32),
    ("rout_ref", (2, HR, 3 * C), F32),
    ("self_ref", (2, C, C), F32),
    ("prod_ref", (2, 3 * C, C), F32),
    ("read_ref", (2, C), F32),
)
INPUTS = ("nbr_ref", "frac_ref", "spec_ref", "emb_ref", "up_ref", "rin_ref", "rout_ref", "self_ref", "prod_ref", "read_ref")
COPIES = 72


def kernel(shape, frac_in, spec_in, nbr_in, *refs):
    inputs, refs = (nbr_in, frac_in, spec_in) + refs[:7], refs[7:]
    force_ref, energy_ref, total_ref = refs[:3]
    send_sem, recv_sem, load_sem = refs[-3:]
    scr = dict(zip([name for name, _, _ in SCRATCH], refs[3:-3]))
    (
        pos, hot, place, mask, yb, base, xs, rad, drad, hup, mom, gmom, comb, rim, hl, dhl, rgrad,
        side_in, near_in, far_in, corner_in, gy_in, edge, pgrad, pg_in, wst, lin, tab, mix_w, back_w, up_w, emb_t, pad, first_ref,
        begin, inner1_ref, ar_out, ar_in, a2_ref, frac_ref, spec_ref, nbr_ref, emb_ref,
        up_ref, rin_ref, rout_ref, self_ref, prod_ref, read_ref,
    ) = [scr[name] for name, _, _ in SCRATCH]
    gxn, gyn = shape
    gx = lax.axis_index("gx")
    gy = lax.axis_index("gy")
    left = (lax.rem(gx + gxn - 1, gxn), gy)
    right = (lax.rem(gx + 1, gxn), gy)
    down = (gx, lax.rem(gy + gyn - 1, gyn))
    up = (gx, lax.rem(gy + 1, gyn))
    left_down, left_up = (left[0], down[1]), (left[0], up[1])
    right_down, right_up = (right[0], down[1]), (right[0], up[1])
    around = [left, right, down, up, left_down, left_up, right_down, right_up]
    core = lax.rem(gx, 2)
    odd = lax.rem(gx // 2, 2)
    near_dev = (gx + 1 - 2 * core, gy)
    far_dev = (lax.rem(gx + gxn - 1 + 2 * core, gxn), gy)
    corner_dev = (far_dev[0], lax.rem(gy + gyn - 1 + 2 * odd, gyn))
    near_base = 8 * core
    far_base = 8 - near_base
    digits = [gy, lax.rem(gx, 4), lax.rem(gx // 4, 4), gx // 16]

    def partner(phase, step):
        other = lax.rem(digits[phase] + step, 4)
        if phase == 0:
            return (gx, other)
        return (gx + (other - digits[phase]) * 4 ** (phase - 1), gy)

    barrier = pltpu.get_barrier_semaphore()
    greeted = around + [partner(phase, step) for phase in range(4) for step in (1, 2, 3)]
    for device in greeted:
        pl.semaphore_signal(barrier, inc=1, device_id=device, device_id_type=MESH)
    loads = [
        pltpu.make_async_copy(source, scr[name], load_sem.at[n])
        for n, (source, name) in enumerate(zip(inputs, INPUTS))
    ]
    for load in loads:
        load.start()

    made = []

    def remote(source, target, device):
        number = len(made)
        copy = pltpu.make_async_remote_copy(
            src_ref=source,
            dst_ref=target,
            send_sem=send_sem.at[number],
            recv_sem=recv_sem.at[number],
            device_id=device,
            device_id_type=MESH,
        )
        made.append(copy)
        copy.start()
        return copy

    def arrived(copies):
        for copy in copies:
            copy.wait_recv()

    for load in loads[:3]:
        load.wait()

    pos[5:7] = jnp.zeros((2, 8, S), F32)
    for b in range(2):
        for d in range(3):
            pos[5 + b, d : d + 1, :] = frac_ref[d, 0, b : b + 1, :]
        pos[5 + b, 3:4, :] = spec_ref[0, b : b + 1, :].astype(F32)

    def hot_rows(b):
        def block(k, carry):
            code = nbr_ref[0, b, pl.ds(k, 1), :]
            lanes = pl.ds(pl.multiple_of((b * K + k) * S, S), S)
            for n, c in enumerate(ORDER[b]):
                match = rows_iota(S, S) == jnp.broadcast_to(code - c * S, (S, S))
                hot[n * S : (n + 1) * S, lanes] = jnp.where(match, 1.0, 0.0).astype(BF16)
            return carry

        lax.fori_loop(0, K, block, 0)

    hot_rows(0)

    for load in loads[3:]:
        load.wait()

    def radial_weights(t):
        w1, w2 = pieces(rout_ref[t], 2)
        wst[t] = jnp.concatenate([w1, w1, w2], axis=0).T.astype(BF16)

    def back_weights(t):
        back_w[t] = wide(jnp.concatenate([prod_ref[t], self_ref[t]], axis=0))

    def read_column(t):
        return jnp.broadcast_to(read_ref[t : t + 1, :], (C, C)).T

    pl.semaphore_wait(barrier, len(greeted))
    pos_copies = [
        remote(pos.at[5], pos.at[11], left_down),
        remote(pos.at[6], pos.at[8], left_up),
        remote(pos.at[5], pos.at[3], right_down),
        remote(pos.at[6], pos.at[0], right_up),
        remote(pos.at[pl.ds(5, 2)], pos.at[pl.ds(9, 2)], left),
        remote(pos.at[pl.ds(5, 2)], pos.at[pl.ds(1, 2)], right),
        remote(pos.at[5], pos.at[7], down),
        remote(pos.at[6], pos.at[4], up),
    ]

    hot_rows(1)
    for t in range(2):
        w1, w2, w3 = pieces(rin_ref[t], 3)
        stack = jnp.concatenate([w1, w1, w2, w1, w2, w3], axis=0)
        pad[...] = jnp.zeros_like(pad)
        pad[0 : 6 * NB, 0:HR] = stack
        lin[t * HR : (t + 1) * HR, :] = pad[...].T[0:HR, 0 : 6 * NB].astype(BF16)
    pad[...] = jnp.zeros_like(pad)
    pad[0:NSPEC, :] = emb_ref[...]
    table = exact(pad[...], up_ref[0])
    tab[...] = jnp.concatenate(pieces(table.T, 2), axis=1).astype(BF16)
    for t in range(2):
        radial_weights(t)
        back_weights(t)
    mix = jnp.concatenate([self_ref[0], prod_ref[0]], axis=0)
    mix_up = exact(mix, up_ref[1])
    mix_w[0:C] = wide(mix.T)
    mix_w[C:] = wide(mix_up.T)
    up_w[...] = wide(mix_up[C:])
    filled = jnp.where(
        jnp.concatenate([pos[5 + b, 3:4, :] for b in range(2)], axis=1) > 0.0, 1.0, 0.0
    )
    inner1_ref[...] = product(back_w[1], jnp.concatenate([read_column(1)] * 2, axis=1) * filled)
    emb_t[...] = jnp.concatenate(pieces(pad[...].T, 3), axis=0).astype(BF16)
    own_element = jnp.concatenate([pos[5 + b, 3:4, :] for b in range(2)], axis=1)
    own_hot = jnp.where(
        rows_iota(S, 2 * S) == jnp.broadcast_to(own_element.astype(jnp.int32) - 1, (S, 2 * S)),
        1.0,
        0.0,
    ).astype(BF16)
    value = jnp.dot(emb_t[...], own_hot, preferred_element_type=F32)
    begin[...] = value[0:C] + value[C : 2 * C] + value[2 * C :]
    mom[...] = jnp.zeros_like(mom)
    edge[...] = jnp.zeros_like(edge)
    for b in range(2):
        for k in range(K):
            lanes = slice(k * S, (k + 1) * S)
            code = jnp.broadcast_to(nbr_ref[0, b, k : k + 1, :], (S, S))
            slots = lax.bitwise_and(code, S - 1)
            both = slice((b * K + k) * S, (b * K + k + 1) * S)
            place[:, both] = jnp.where(rows_iota(S, S) == slots, 1.0, 0.0).astype(BF16)
            bins = lax.shift_right_logical(code[0:K], 7)
            mask[b, :, lanes] = jnp.where(rows_iota(K, S) == bins, 1.0, 0.0)

    arrived(pos_copies)

    unit = []
    for b in range(2):
        codes = nbr_ref[0, b]
        which = lax.shift_right_logical(codes, 7)
        slot = lax.bitwise_and(codes, S - 1)
        step_x = lax.shift_right_logical(which * 11, 5)
        step_y = which - 3 * step_x
        far = [jnp.zeros((K, S), F32)] * 4
        for c in range(9):
            source = (c // 3) * 4 + b + c % 3
            chosen = which == c
            for d in range(4):
                row = jnp.broadcast_to(pos[source, d : d + 1, :], (K, S))
                taken = jnp.take_along_axis(row, slot, axis=1, mode="promise_in_bounds")
                far[d] = jnp.where(chosen, taken, far[d])
        near = [pos[5 + b, d : d + 1, :] for d in range(3)]
        delta_x = ((step_x - 1).astype(F32) + far[0] - near[0]) * bin_width
        delta_y = ((step_y - 1).astype(F32) + far[1] - near[1]) * bin_width
        delta_z = (far[2] - near[2]) * slab_height
        distance = jnp.sqrt(delta_x * delta_x + delta_y * delta_y + delta_z * delta_z + softening)
        ux = delta_x / distance
        uy = delta_y / distance
        uz = delta_z / distance
        unit.append((distance, ux, uy, uz))
        q1 = distance * (1.0 / cutoff)
        q2 = q1 * q1
        q4 = q2 * q2
        inside = q1 < 1.0
        env = jnp.where(inside, 1.0 + q4 * q1 * (-21.0 + q1 * (35.0 - 15.0 * q1)), 0.0)
        denv = jnp.where(
            inside, q4 * (-105.0 + q1 * (210.0 - 105.0 * q1)) * (1.0 / cutoff), 0.0
        )
        values = [
            R3 * ux,
            R3 * uy,
            R3 * uz,
            R15 * ux * uy,
            R15 * uy * uz,
            0.5 * R5 * (2.0 * uz * uz - ux * ux - uy * uy),
            R15 * ux * uz,
            0.5 * R15 * (ux * ux - uy * uy),
            distance,
            env,
            denv,
            far[3],
        ]
        for m, value in enumerate(values):
            for k in range(K):
                yb[b * 8 + k // 2, m, :, (k % 2) * S : (k % 2 + 1) * S] = jnp.broadcast_to(
                    value[k : k + 1, :], (8, S)
                )

    centers = rows_iota(NB, W).astype(F32) * (cutoff / (NB - 1))

    def stacked(value):
        b1, b2, b3 = pieces(value, 3)
        return jnp.concatenate([b1, b2, b1, b3, b2, b1], axis=0).astype(BF16)

    def hidden_blocks(t, want_value, want_slope, beside):
        def block(q):
            beside(q)
            weight = lin[t * HR : (t + 1) * HR, :]
            if t == 0:
                offset = yb[q, 8] - centers
                scaled = offset * (1.0 / spread_width)
                basis = jnp.exp(-(scaled * scaled))
                if want_value:
                    base[0, q] = stacked(basis)
                if want_slope:
                    base[1, q] = stacked(basis * (offset * (-2.0 / (spread_width * spread_width))))
            pre = jnp.dot(weight, base[0, q], preferred_element_type=F32)
            if want_slope:
                dpre = jnp.dot(weight, base[1, q], preferred_element_type=F32)
            env16 = jnp.concatenate([yb[q, 9], yb[q, 9]], axis=0)
            denv16 = jnp.concatenate([yb[q, 10], yb[q, 10]], axis=0)
            for r in range(HR // 16):
                rows = slice(r * 16, (r + 1) * 16)
                x = pre[rows]
                sig = 1.0 / (1.0 + jnp.exp(-x))
                h = x * sig
                found = []
                if want_value:
                    found.append((0, env16 * h))
                if want_slope:
                    dh = (sig + h * (1.0 - sig)) * dpre[rows]
                    found.append((1, denv16 * h + env16 * dh))
                for v, value in found:
                    v = v * 2 if t else v
                    high, low = pieces(value, 2)
                    high = high.astype(BF16)
                    xs[v, q, r * 16 : (r + 1) * 16, :] = high
                    xs[v, q, HR + r * 16 : HR + (r + 1) * 16, :] = low.astype(BF16)
                    xs[v, q, 2 * HR + r * 16 : 2 * HR + (r + 1) * 16, :] = high

        blocks(Q, 4, block)

    def radial_block(t, units, target):
        def block(q):
            target[t, q] = jnp.dot(wst[t], xs[units, q], preferred_element_type=F32)

        return block

    def element_block(q):
        element = yb[q, 11].astype(jnp.int32) - 1
        element = jnp.concatenate([element] * (S // 8), axis=0)
        choice = jnp.where(rows_iota(S, W) == element, 1.0, 0.0).astype(BF16)
        choice = jnp.concatenate([choice, choice], axis=0)
        hup[0, q] = jnp.dot(tab[...], choice, preferred_element_type=F32)

    def gather_blocks(begin_bin, end_bin):
        part = slice(begin_bin * S, end_bin * S)

        def block(q):
            lanes = pl.ds(pl.multiple_of(q * W, W), W)
            both = jnp.dot(hl[q // 8, :, part], hot[part, lanes], preferred_element_type=F32)
            value = both[0:C] + both[C:]
            hup[1, q] = value if begin_bin == 0 else hup[1, q] + value

        blocks(Q, 8, block)

    def split_rim(begin_bin, end_bin):
        seen = {}
        for b in range(2):
            for n in range(begin_bin, end_bin):
                c = ORDER[b][n]
                source = (c // 3) * 4 + b + c % 3
                if source not in seen:
                    high, low = pieces(rim[source], 2)
                    seen[source] = jnp.concatenate([high, low], axis=0).astype(BF16)
                hl[b, :, n * S : (n + 1) * S] = seen[source]

    def moments(t):
        def block(i, carry):
            b = i // 4
            for ct in range(C // 8):
                rows = slice(ct * 8, ct * 8 + 8)
                rows1 = slice(C + ct * 8, C + ct * 8 + 8)
                rows2 = slice(2 * C + ct * 8, 2 * C + ct * 8 + 8)
                sums = [mom[t, b, m, rows, :] for m in range(9)]
                for part in range(4):
                    q = i * 2 + part // 2
                    lanes = slice(part % 2 * S, part % 2 * S + S)
                    h = hup[t, q, rows, lanes]
                    sums[0] = sums[0] + rad[t, q, rows, lanes] * h
                    h1 = rad[t, q, rows1, lanes] * h
                    h2 = rad[t, q, rows2, lanes] * h
                    for m in range(3):
                        sums[1 + m] = sums[1 + m] + yb[q, m, :, lanes] * h1
                    for m in range(3, 8):
                        sums[1 + m] = sums[1 + m] + yb[q, m, :, lanes] * h2
                for m in range(9):
                    mom[t, b, m, rows, :] = sums[m]
            return carry

        lax.fori_loop(0, Q // 2, block, 0)

    def invariants(t):
        inv0 = jnp.concatenate([mom[t, b, 0] for b in range(2)], axis=1) * message_scale
        inv1 = jnp.concatenate(
            [sum(mom[t, b, m] * mom[t, b, m] for m in range(1, 4)) for b in range(2)], axis=1
        )
        inv2 = jnp.concatenate(
            [sum(mom[t, b, m] * mom[t, b, m] for m in range(4, 9)) for b in range(2)], axis=1
        )
        scale = message_scale * message_scale
        return jnp.concatenate([inv0, inv1 * scale, inv2 * scale], axis=0)

    def energies(t, values):
        column = read_column(t)
        return jnp.concatenate(
            [
                jnp.sum(values[:, b * S : (b + 1) * S] * column, axis=0, keepdims=True)
                for b in range(2)
            ],
            axis=1,
        )

    hidden_blocks(0, True, False, element_block)
    blocks(Q, Q, radial_block(0, 0, rad))
    moments(0)
    mixed = product(mix_w[...], jnp.concatenate([begin[...], invariants(0)], axis=0))
    first = mixed[0:C] * filled
    own_up = mixed[C:] * filled
    rim[5] = own_up[:, 0:S]
    rim[6] = own_up[:, S:]
    halves = [pl.ds(0, C // 2), pl.ds(C // 2, C // 2)]
    y_copies = [
        [
            remote(rim.at[5, half], rim.at[7, half], down),
            remote(rim.at[6, half], rim.at[4, half], up),
        ]
        for half in halves
    ]
    straight = [remote(rim.at[5 + odd], rim.at[far_base + 3 - 3 * odd], corner_dev)]
    x_copies = [
        remote(rim.at[pl.ds(5, 2)], rim.at[pl.ds(far_base + 1, 2)], far_dev),
        remote(rim.at[pl.ds(5, 2)], rim.at[pl.ds(near_base + 1, 2)], near_dev),
    ]
    first_ref[...] = first

    first_energy = energies(0, first)
    hidden_blocks(0, False, True, lambda q: None)
    hidden_blocks(1, True, True, radial_block(0, 1, drad))
    far_copies = []
    for half, group in zip(halves, y_copies):
        arrived(group)
        far_copies += [
            remote(rim.at[4 + 3 * odd, half], rim.at[far_base + 3 * odd, half], far_dev),
            remote(rim.at[4, half], rim.at[near_base, half], near_dev),
            remote(rim.at[7, half], rim.at[near_base + 3, half], near_dev),
        ]
    split_rim(0, 3)
    gather_blocks(0, 3)
    blocks(Q, Q, radial_block(1, 0, rad))
    blocks(Q, Q, radial_block(1, 2, drad))
    arrived(x_copies)
    split_rim(3, 7)
    gather_blocks(3, 7)
    arrived(straight + far_copies)

    split_rim(7, 9)

    gather_blocks(7, 9)
    moments(1)
    for b in range(2):
        lanes = slice(b * S, (b + 1) * S)
        gmom[b, 0] = inner1_ref[0:C, lanes] * message_scale
        scale = 2.0 * message_scale * message_scale
        for m in range(1, 9):
            rows = slice(C, 2 * C) if m < 4 else slice(2 * C, 3 * C)
            gmom[b, m] = inner1_ref[rows, lanes] * mom[1, b, m] * scale

    def feature_block(q, carry):
        b = q // 8
        for ct in range(C // 16):
            rows = slice(ct * 16, ct * 16 + 16)
            rows1 = slice(C + ct * 16, C + ct * 16 + 16)
            rows2 = slice(2 * C + ct * 16, 2 * C + ct * 16 + 16)
            grads = [gmom[b, m, rows, :] for m in range(9)]
            for half in range(2):
                lanes = slice(half * S, half * S + S)
                spread = [jnp.concatenate([yb[q, m, :, lanes]] * 2, axis=0) for m in range(8)]
                a1 = sum(spread[m] * grads[1 + m] for m in range(3))
                a2 = sum(spread[m] * grads[1 + m] for m in range(3, 8))
                value = (
                    rad[1, q, rows, lanes] * grads[0]
                    + rad[1, q, rows1, lanes] * a1
                    + rad[1, q, rows2, lanes] * a2
                )
                rad[1, q, rows, lanes] = a1
                a2_ref[q, rows, lanes] = a2
                high, low = pieces(value, 2)
                target = pl.ds(pl.multiple_of(q * W + half * S, S), S)
                dhl[rows, target] = high.astype(BF16)
                dhl[C + ct * 16 : C + ct * 16 + 16, target] = low.astype(BF16)
        return carry

    lax.fori_loop(0, Q, feature_block, 0)

    def scatter(begin_bin, end_bin):
        found = {}
        for b in range(2):
            lanes = slice(b * K * S, (b + 1) * K * S)
            both = nt(dhl[:, lanes], hot[begin_bin * S : end_bin * S, lanes])
            value = both[0:C] + both[C:]
            for n in range(begin_bin, end_bin):
                c = ORDER[b][n]
                source = (c // 3) * 4 + b + c % 3
                piece = value[:, (n - begin_bin) * S : (n - begin_bin + 1) * S]
                found[source] = found[source] + piece if source in found else piece
        for source, value in found.items():
            rgrad[source] = value

    scatter(7, 9)
    corner_copies = [
        [
            remote(rgrad.at[near_base + 3 - 3 * odd, half], far_in.at[half], far_dev),
            remote(rgrad.at[far_base, half], near_in.at[0, half], near_dev),
            remote(rgrad.at[far_base + 3, half], near_in.at[1, half], near_dev),
        ]
        for half in halves
    ]
    back_straight = [remote(rgrad.at[near_base + 3 * odd], corner_in, corner_dev)]
    scatter(3, 7)
    side_copies = [
        remote(rgrad.at[pl.ds(near_base + 1, 2)], side_in.at[0], far_dev),
        remote(rgrad.at[pl.ds(far_base + 1, 2)], side_in.at[1], near_dev),
    ]
    scatter(0, 3)

    def reduce_send(phase, value):
        ar_out[phase] = value
        ar_in[phase, digits[phase]] = value
        return [
            remote(ar_out.at[phase], ar_in.at[phase, digits[phase]], partner(phase, step))
            for step in (1, 2, 3)
        ]

    def reduce_wait(phase, copies):
        arrived(copies)
        return (ar_in[phase, 0] + ar_in[phase, 1]) + (ar_in[phase, 2] + ar_in[phase, 3])

    second_inputs = jnp.concatenate([invariants(1), first_ref[...]], axis=0)
    atom_energy = first_energy + jnp.sum(inner1_ref[...] * second_inputs, axis=0, keepdims=True)
    for b in range(2):
        energy_ref[0, b : b + 1, :] = atom_energy[:, b * S : (b + 1) * S]
    pair = atom_energy[:, 0:S] + atom_energy[:, S:]
    reduced = reduce_send(0, jnp.broadcast_to(jnp.sum(pair, axis=1, keepdims=True), (8, S)))

    def position_block(q, carry):
        b = q // 8
        sums = [[jnp.zeros((8, S), F32)] * 9 for _ in range(2)]
        for ct in range(C // 8):
            rows = slice(ct * 8, ct * 8 + 8)
            rows1 = slice(C + ct * 8, C + ct * 8 + 8)
            rows2 = slice(2 * C + ct * 8, 2 * C + ct * 8 + 8)
            grads = [gmom[b, m, rows, :] for m in range(9)]
            for half in range(2):
                lanes = slice(half * S, half * S + S)
                a1 = rad[1, q, rows, lanes]
                a2 = a2_ref[q, rows, lanes]
                h = hup[1, q, rows, lanes]
                h1 = rad[1, q, rows1, lanes] * h
                h2 = rad[1, q, rows2, lanes] * h
                slope = (
                    drad[1, q, rows, lanes] * grads[0]
                    + drad[1, q, rows1, lanes] * a1
                    + drad[1, q, rows2, lanes] * a2
                )
                now = sums[half]
                now[8] = now[8] + slope * h
                for m in range(3):
                    now[m] = now[m] + grads[1 + m] * h1
                for m in range(3, 8):
                    now[m] = now[m] + grads[1 + m] * h2
        for half in range(2):
            k = (q - b * 8) * 2 + half
            for m in range(9):
                edge[b, m, pl.ds(k, 1), :] = jnp.sum(sums[half][m], axis=0, keepdims=True)
        return carry

    lax.fori_loop(0, Q // 2, position_block, 0)
    row_copies = []
    for half, group in zip((slice(0, C // 2), slice(C // 2, C)), corner_copies):
        arrived(group)
        rgrad[4, half] = rgrad[4, half] + near_in[0, half]
        rgrad[7, half] = rgrad[7, half] + near_in[1, half]
        rgrad[4 + 3 * odd, half] = rgrad[4 + 3 * odd, half] + far_in[half]
        window = pl.ds(half.start, C // 2)
        row_copies += [
            remote(rgrad.at[4, window], gy_in.at[0, window], down),
            remote(rgrad.at[7, window], gy_in.at[1, window], up),
        ]

    lax.fori_loop(Q // 2, Q, position_block, 0)
    reduced = reduce_send(1, reduce_wait(0, reduced))

    for b in range(2):
        m2 = [mom[0, b, 4 + m] for m in range(5)]
        comb[b, 0] = R5 * m2[0]
        comb[b, 1] = R5 * m2[1]
        comb[b, 2] = R5 * m2[3]
        comb[b, 3] = R5 * m2[4] - (R5 / R3) * m2[2]
        comb[b, 4] = -R5 * m2[4] - (R5 / R3) * m2[2]
        comb[b, 5] = (2.0 * R5 / R3) * m2[2]

    def product_block(q):
        b = q // 8
        for ct in range(C // 8):
            rows = slice(ct * 8, ct * 8 + 8)
            rows1 = slice(C + ct * 8, C + ct * 8 + 8)
            rows2 = slice(2 * C + ct * 8, 2 * C + ct * 8 + 8)
            own = [mom[0, b, 1 + m, rows, :] for m in range(8)]
            mixed = [comb[b, m, rows, :] for m in range(6)]
            for half in range(2):
                lanes = slice(half * S, half * S + S)
                y = [yb[q, m, :, lanes] for m in range(8)]
                h = hup[0, q, rows, lanes]
                b1 = sum(y[m] * own[m] for m in range(3)) * h
                b2 = sum(y[m] * own[m] for m in range(3, 8)) * h
                h1 = rad[0, q, rows1, lanes] * h
                h2 = rad[0, q, rows2, lanes] * h
                drad[0, q, rows, lanes] = drad[0, q, rows, lanes] * h
                drad[0, q, rows1, lanes] = drad[0, q, rows1, lanes] * b1
                drad[0, q, rows2, lanes] = drad[0, q, rows2, lanes] * b2
                hup[0, q, rows, lanes] = h1
                rad[0, q, rows, lanes] = h2 * (y[1] * mixed[0] + y[2] * mixed[2] + y[0] * mixed[3])
                rad[0, q, rows1, lanes] = h2 * (y[0] * mixed[0] + y[2] * mixed[1] + y[1] * mixed[4])
                rad[0, q, rows2, lanes] = h2 * (y[1] * mixed[1] + y[0] * mixed[2] + y[2] * mixed[5])

    blocks(Q, 1, product_block)

    direct = jnp.concatenate([read_column(0)] * 2, axis=1) + inner1_ref[3 * C :]
    inner1_ref[0 : 3 * C] = product(back_w[0, 0 : 3 * C], direct * filled)

    second_part = []
    for b in range(2):
        distance, ux, uy, uz = unit[b]
        dy = [edge[b, m] for m in range(9)]
        gux = R3 * dy[0] + R15 * (uy * dy[3] + uz * dy[6] + ux * dy[7]) - R5 * ux * dy[5]
        guy = R3 * dy[1] + R15 * (ux * dy[3] + uz * dy[4] - uy * dy[7]) - R5 * uy * dy[5]
        guz = R3 * dy[2] + R15 * (uy * dy[4] + ux * dy[6]) + (2.0 * R5) * uz * dy[5]
        second_part.append((gux, guy, guz, dy[8]))

    arrived(back_straight + side_copies)
    rgrad[5 + odd] = rgrad[5 + odd] + corner_in[...]
    own_low = rgrad[5] + side_in[0, 0] + side_in[1, 0]
    own_high = rgrad[6] + side_in[0, 1] + side_in[1, 1]
    arrived(row_copies)
    returned = jnp.concatenate([own_low + gy_in[1], own_high + gy_in[0]], axis=1)

    inner0 = inner1_ref[0 : 3 * C] + product(up_w[...], returned) * filled
    scale = 2.0 * message_scale * message_scale
    for b in range(2):
        lanes = slice(b * S, (b + 1) * S)
        one = inner0[C : 2 * C, lanes] * scale
        comb[b, 0] = inner0[0:C, lanes] * message_scale
        comb[b, 1] = one
        comb[b, 2] = inner0[2 * C :, lanes] * scale
        for m in range(3):
            comb[b, 3 + m] = one * mom[0, b, 1 + m] * R3
    reduced = reduce_send(2, reduce_wait(1, reduced))

    def first_block(q, carry):
        b = q // 8
        sums = [[jnp.zeros((8, S), F32)] * 4 for _ in range(2)]
        for ct in range(C // 8):
            rows = slice(ct * 8, ct * 8 + 8)
            rows1 = slice(C + ct * 8, C + ct * 8 + 8)
            rows2 = slice(2 * C + ct * 8, 2 * C + ct * 8 + 8)
            grads = [comb[b, m, rows, :] for m in range(6)]
            for half in range(2):
                lanes = slice(half * S, half * S + S)
                now = sums[half]
                now[3] = (
                    now[3]
                    + drad[0, q, rows, lanes] * grads[0]
                    + drad[0, q, rows1, lanes] * grads[1]
                    + drad[0, q, rows2, lanes] * grads[2]
                )
                h1 = hup[0, q, rows, lanes]
                for d, part in enumerate((rows, rows1, rows2)):
                    now[d] = now[d] + grads[3 + d] * h1 + grads[2] * rad[0, q, part, lanes]
        for half in range(2):
            k = (q - b * 8) * 2 + half
            for m in range(4):
                edge[b, m, pl.ds(k, 1), :] = jnp.sum(sums[half][m], axis=0, keepdims=True)
        return carry

    lax.fori_loop(0, Q, first_block, 0)
    reduced = reduce_send(3, reduce_wait(2, reduced))

    direct_force = []
    for b in range(2):
        distance, ux, uy, uz = unit[b]
        gux, guy, guz, slope = [edge[b, m] + second_part[b][m] for m in range(4)]
        along = ux * gux + uy * guy + uz * guz
        grads = [
            (g - u * along) / distance + u * slope for g, u in ((gux, ux), (guy, uy), (guz, uz))
        ]
        direct_force.append([jnp.sum(g, axis=0, keepdims=True) for g in grads])
        columns = []
        for k in range(K):
            here = mask[b, :, k * S : (k + 1) * S]
            stack = [here * jnp.broadcast_to(g[k : k + 1, :], (K, S)) for g in grads]
            stack = pieces(jnp.concatenate(stack, axis=0), 2)
            columns.append(jnp.concatenate(stack, axis=0).astype(BF16))
        total = nt(jnp.concatenate(columns, axis=1), place[:, b * K * S : (b + 1) * K * S])
        total = total[0 : 3 * K] + total[3 * K :]
        for c in range(9):
            source = (c // 3) * 4 + b + c % 3
            for d in range(3):
                row = total[d * K + c : d * K + c + 1, :]
                if b == 0 or c % 3 == 2:
                    pgrad[source, d : d + 1, :] = row
                else:
                    pgrad[source, d : d + 1, :] = pgrad[source, d : d + 1, :] + row
    for source in range(12):
        pgrad[source, 3:8, :] = jnp.zeros((5, S), F32)
    back_copies = [
        remote(pgrad.at[0], pg_in.at[6], left_down),
        remote(pgrad.at[3], pg_in.at[7], left_up),
        remote(pgrad.at[8], pg_in.at[8], right_down),
        remote(pgrad.at[11], pg_in.at[9], right_up),
        remote(pgrad.at[pl.ds(1, 2)], pg_in.at[pl.ds(0, 2)], left),
        remote(pgrad.at[pl.ds(9, 2)], pg_in.at[pl.ds(2, 2)], right),
        remote(pgrad.at[4], pg_in.at[4], down),
        remote(pgrad.at[7], pg_in.at[5], up),
    ]
    total_ref[...] = reduce_wait(3, reduced)[0:1, 0:1]
    arrived(back_copies)
    low_grad = pgrad[5] + pg_in[0] + pg_in[2] + pg_in[5] + pg_in[7] + pg_in[9]
    high_grad = pgrad[6] + pg_in[1] + pg_in[3] + pg_in[4] + pg_in[6] + pg_in[8]
    for b, returned in enumerate((low_grad, high_grad)):
        for d in range(3):
            force_ref[d, 0, b : b + 1, :] = direct_force[b][d] - returned[d : d + 1, :]
    for copy in made:
        copy.wait_send()


def finish(*refs):
    for source, target in zip(refs[:3], refs[3:]):
        target[...] = source[...]


def on_device(shape, *arguments):
    vmem = pl.BlockSpec(memory_space=pltpu.VMEM)
    anywhere = pl.BlockSpec(memory_space=pl.ANY)
    forces, energy, total = pl.pallas_call(
        functools.partial(kernel, shape),
        out_shape=(
            jax.ShapeDtypeStruct((3, 1, 2, S), F32),
            jax.ShapeDtypeStruct((1, 2, S), F32),
            jax.ShapeDtypeStruct((1, 1), F32),
        ),
        in_specs=[anywhere] * 10,
        out_specs=(vmem, vmem, vmem),
        scratch_shapes=[pltpu.VMEM(dims, kind) for _, dims, kind in SCRATCH]
        + [
            pltpu.SemaphoreType.DMA((COPIES,)),
            pltpu.SemaphoreType.DMA((COPIES,)),
            pltpu.SemaphoreType.DMA((len(INPUTS),)),
        ],
        compiler_params=pltpu.CompilerParams(
            collective_id=0, has_side_effects=True, vmem_limit_bytes=62 * 1024 * 1024
        ),
    )(*arguments)
    outputs = pl.pallas_call(
        finish,
        out_shape=[jax.ShapeDtypeStruct(x.shape, F32) for x in (forces, energy, total)],
        in_specs=[vmem] * 3,
        out_specs=[vmem] * 3,
    )(forces, energy, total)
    return outputs[0], outputs[1], outputs[2].reshape(())


def solution(mesh):
    placed = (
        P(None, "gx", "gy", None),
        P("gx", "gy", None),
        P("gx", "gy", None, None),
        P(),
        P(),
        P(),
        P(),
        P(),
        P(),
        P(),
    )
    return jax.shard_map(
        functools.partial(on_device, (mesh.shape["gx"], mesh.shape["gy"])),
        mesh=mesh,
        in_specs=placed,
        out_specs=(P(None, "gx", "gy", None), P("gx", "gy", None), P()),
        check_vma=False,
    )
```

```python
import functools
import math

import jax
import jax.numpy as jnp
from jax import lax
from jax.experimental import pallas as pl
from jax.experimental.pallas import tpu as pltpu
from jax.sharding import PartitionSpec as P

bin_width = 6.0
slab_height = 12.0
cutoff = 6.0
softening = 0.25
spread_width = 0.75
message_scale = 1.5

S = 128
C = 128
K = 16
HR = 64
NB = 8
NSPEC = 89
ORDER = ((3, 4, 5, 1, 2, 7, 8, 0, 6), (3, 4, 5, 0, 1, 6, 7, 2, 8))
Q = 16
W = 256
MESH = pl.DeviceIdType.MESH
F32 = jnp.float32
BF16 = jnp.bfloat16
HIGH = lax.Precision.HIGHEST
R3 = math.sqrt(3.0)
R5 = math.sqrt(5.0)
R15 = math.sqrt(15.0)


def exact(a, b):
    return jnp.dot(a, b, precision=HIGH, preferred_element_type=F32)


def pieces(x, count):
    parts = []
    for _ in range(count):
        part = x.astype(BF16).astype(F32)
        parts.append(part)
        x = x - part
    return parts


def wide(weight):
    high, low = pieces(weight, 2)
    return jnp.concatenate([high, high, low], axis=1).astype(BF16)


def tall(value):
    high, low = pieces(value, 2)
    return jnp.concatenate([high, low, high], axis=0).astype(BF16)


def product(weight, value):
    return jnp.dot(weight, tall(value), preferred_element_type=F32)


def blocks(count, unroll, step, start=0):
    def several(i, carry):
        for u in range(unroll):
            step(start + i * unroll + u)
        return carry

    if unroll == count:
        several(0, 0)
    else:
        lax.fori_loop(0, count // unroll, several, 0)


def nt(a, b):
    return lax.dot_general(a, b, (((1,), (1,)), ((), ())), preferred_element_type=F32)


def rows_iota(rows, cols):
    return lax.broadcasted_iota(jnp.int32, (rows, cols), 0)


SCRATCH = (
    ("pos", (12, 8, S), F32),
    ("hot", (9 * S, 2 * K * S), BF16),
    ("place", (S, 2 * K * S), BF16),
    ("mask", (2, K, K * S), F32),
    ("yb", (Q, 12, 8, W), F32),
    ("base", (2, Q, 6 * NB, W), BF16),
    ("xs", (3, Q, 3 * HR, W), BF16),
    ("rad0", (Q, 3 * C, W), F32),
    ("rad1", (Q, 3 * C, W), F32),
    ("drad0", (Q, 3 * C, W), F32),
    ("drad1", (Q, 3 * C, W), F32),
    ("hup0", (Q, C, W), F32),
    ("hup1", (Q, C, W), F32),
    ("mom", (2, 2, 9, C, S), F32),
    ("gmom", (2, 9, C, S), F32),
    ("comb", (2, 3, C, S), F32),
    ("rim", (12, C, S), F32),
    ("hl", (2, 2 * C, 9 * S), BF16),
    ("dhl", (2 * C, 2 * K * S), BF16),
    ("rgrad", (12, C, S), F32),
    ("side_in", (2, 2, C, S), F32),
    ("near_in", (2, C, S), F32),
    ("far_in", (C, S), F32),
    ("corner_in", (C, S), F32),
    ("gy_in", (2, C, S), F32),
    ("edge", (2, 9, K, S), F32),
    ("pgrad", (12, 8, S), F32),
    ("pg_in", (10, 8, S), F32),
    ("wst", (2, 3 * C, 3 * HR), BF16),
    ("lin", (2 * HR, 6 * NB), BF16),
    ("tab", (C, 2 * S), BF16),
    ("mix_w", (2 * C, 12 * C), BF16),
    ("back_w", (2, 4 * C, 3 * C), BF16),
    ("up_w", (3 * C, 3 * C), BF16),
    ("emb_t", (3 * C, S), BF16),
    ("pad", (S, S), F32),
    ("first", (C, 2 * S), F32),
    ("begin", (C, 2 * S), F32),
    ("inner1", (4 * C, 2 * S), F32),
    ("ar_out", (4, 8, S), F32),
    ("ar_in", (4, 4, 8, S), F32),
    ("a2", (Q, C, W), F32),
    ("frac_ref", (3, 1, 2, S), F32),
    ("spec_ref", (1, 2, S), jnp.int32),
    ("nbr_ref", (1, 2, K, S), jnp.int32),
    ("emb_ref", (NSPEC, C), F32),
    ("up_ref", (2, C, C), F32),
    ("rin_ref", (2, NB, HR), F32),
    ("rout_ref", (2, HR, 3 * C), F32),
    ("self_ref", (2, C, C), F32),
    ("prod_ref", (2, 3 * C, C), F32),
    ("read_ref", (2, C), F32),
)
INPUTS = ("nbr_ref", "frac_ref", "spec_ref", "emb_ref", "up_ref", "rin_ref", "rout_ref", "self_ref", "prod_ref", "read_ref")
COPIES = 72


def kernel(shape, frac_in, spec_in, nbr_in, *refs):
    inputs, refs = (nbr_in, frac_in, spec_in) + refs[:7], refs[7:]
    force_ref, energy_ref, total_ref = refs[:3]
    send_sem, recv_sem, load_sem = refs[-3:]
    scr = dict(zip([name for name, _, _ in SCRATCH], refs[3:-3]))
    (
        pos, hot, place, mask, yb, base, xs, rad0, rad1, drad0, drad1, hup0, hup1, mom, gmom, comb, rim, hl, dhl, rgrad,
        side_in, near_in, far_in, corner_in, gy_in, edge, pgrad, pg_in, wst, lin, tab, mix_w, back_w, up_w, emb_t, pad, first_ref,
        begin, inner1_ref, ar_out, ar_in, a2_ref, frac_ref, spec_ref, nbr_ref, emb_ref,
        up_ref, rin_ref, rout_ref, self_ref, prod_ref, read_ref,
    ) = [scr[name] for name, _, _ in SCRATCH]
    rad = (rad0, rad1)
    hup = (hup0, hup1)
    gxn, gyn = shape
    gx = lax.axis_index("gx")
    gy = lax.axis_index("gy")
    left = (lax.rem(gx + gxn - 1, gxn), gy)
    right = (lax.rem(gx + 1, gxn), gy)
    down = (gx, lax.rem(gy + gyn - 1, gyn))
    up = (gx, lax.rem(gy + 1, gyn))
    left_down, left_up = (left[0], down[1]), (left[0], up[1])
    right_down, right_up = (right[0], down[1]), (right[0], up[1])
    around = [left, right, down, up, left_down, left_up, right_down, right_up]
    core = lax.rem(gx, 2)
    odd = lax.rem(gx // 2, 2)
    near_dev = (gx + 1 - 2 * core, gy)
    far_dev = (lax.rem(gx + gxn - 1 + 2 * core, gxn), gy)
    corner_dev = (far_dev[0], lax.rem(gy + gyn - 1 + 2 * odd, gyn))
    near_base = 8 * core
    far_base = 8 - near_base
    digits = [gy, lax.rem(gx, 4), lax.rem(gx // 4, 4), gx // 16]

    def partner(phase, step):
        other = lax.rem(digits[phase] + step, 4)
        if phase == 0:
            return (gx, other)
        return (gx + (other - digits[phase]) * 4 ** (phase - 1), gy)

    barrier = pltpu.get_barrier_semaphore()
    greeted = around + [partner(phase, step) for phase in range(4) for step in (1, 2, 3)]
    for device in greeted:
        pl.semaphore_signal(barrier, inc=1, device_id=device, device_id_type=MESH)
    loads = [
        pltpu.make_async_copy(source, scr[name], load_sem.at[n])
        for n, (source, name) in enumerate(zip(inputs, INPUTS))
    ]
    for load in loads:
        load.start()

    made = []

    def remote(source, target, device):
        number = len(made)
        copy = pltpu.make_async_remote_copy(
            src_ref=source,
            dst_ref=target,
            send_sem=send_sem.at[number],
            recv_sem=recv_sem.at[number],
            device_id=device,
            device_id_type=MESH,
        )
        made.append(copy)
        copy.start()
        return copy

    def arrived(copies):
        for copy in copies:
            copy.wait_recv()

    for load in loads[:3]:
        load.wait()

    pos[5:7] = jnp.zeros((2, 8, S), F32)
    for b in range(2):
        for d in range(3):
            pos[5 + b, d : d + 1, :] = frac_ref[d, 0, b : b + 1, :]
        pos[5 + b, 3:4, :] = spec_ref[0, b : b + 1, :].astype(F32)

    def hot_rows(b):
        def block(k, carry):
            code = nbr_ref[0, b, pl.ds(k, 1), :]
            lanes = pl.ds(pl.multiple_of((b * K + k) * S, S), S)
            for n, c in enumerate(ORDER[b]):
                match = rows_iota(S, S) == jnp.broadcast_to(code - c * S, (S, S))
                hot[n * S : (n + 1) * S, lanes] = jnp.where(match, 1.0, 0.0).astype(BF16)
            return carry

        lax.fori_loop(0, K, block, 0)

    hot_rows(0)

    for load in loads[3:]:
        load.wait()

    def radial_weights(t):
        w1, w2 = pieces(rout_ref[t], 2)
        wst[t] = jnp.concatenate([w1, w1, w2], axis=0).T.astype(BF16)

    def back_weights(t):
        back_w[t] = wide(jnp.concatenate([prod_ref[t], self_ref[t]], axis=0))

    def read_column(t):
        return jnp.broadcast_to(read_ref[t : t + 1, :], (C, C)).T

    pl.semaphore_wait(barrier, len(greeted))
    pos_copies = [
        remote(pos.at[5], pos.at[11], left_down),
        remote(pos.at[6], pos.at[8], left_up),
        remote(pos.at[5], pos.at[3], right_down),
        remote(pos.at[6], pos.at[0], right_up),
        remote(pos.at[pl.ds(5, 2)], pos.at[pl.ds(9, 2)], left),
        remote(pos.at[pl.ds(5, 2)], pos.at[pl.ds(1, 2)], right),
        remote(pos.at[5], pos.at[7], down),
        remote(pos.at[6], pos.at[4], up),
    ]

    hot_rows(1)
    for t in range(2):
        w1, w2, w3 = pieces(rin_ref[t], 3)
        stack = jnp.concatenate([w1, w1, w2, w1, w2, w3], axis=0)
        pad[...] = jnp.zeros_like(pad)
        pad[0 : 6 * NB, 0:HR] = stack
        lin[t * HR : (t + 1) * HR, :] = pad[...].T[0:HR, 0 : 6 * NB].astype(BF16)
    pad[...] = jnp.zeros_like(pad)
    pad[0:NSPEC, :] = emb_ref[...]
    table = exact(pad[...], up_ref[0])
    tab[...] = jnp.concatenate(pieces(table.T, 2), axis=1).astype(BF16)
    for t in range(2):
        radial_weights(t)
        back_weights(t)
    mix = jnp.concatenate([self_ref[0], prod_ref[0]], axis=0)
    mix_up = exact(mix, up_ref[1])
    mix_w[0:C] = wide(mix.T)
    mix_w[C:] = wide(mix_up.T)
    up_w[...] = wide(mix_up[C:])
    filled = jnp.where(
        jnp.concatenate([pos[5 + b, 3:4, :] for b in range(2)], axis=1) > 0.0, 1.0, 0.0
    )
    inner1_ref[...] = product(back_w[1], jnp.concatenate([read_column(1)] * 2, axis=1) * filled)
    emb_t[...] = jnp.concatenate(pieces(pad[...].T, 3), axis=0).astype(BF16)
    own_element = jnp.concatenate([pos[5 + b, 3:4, :] for b in range(2)], axis=1)
    own_hot = jnp.where(
        rows_iota(S, 2 * S) == jnp.broadcast_to(own_element.astype(jnp.int32) - 1, (S, 2 * S)),
        1.0,
        0.0,
    ).astype(BF16)
    value = jnp.dot(emb_t[...], own_hot, preferred_element_type=F32)
    begin[...] = value[0:C] + value[C : 2 * C] + value[2 * C :]
    mom[...] = jnp.zeros_like(mom)
    edge[...] = jnp.zeros_like(edge)
    for b in range(2):
        for k in range(K):
            lanes = slice(k * S, (k + 1) * S)
            code = jnp.broadcast_to(nbr_ref[0, b, k : k + 1, :], (S, S))
            slots = lax.bitwise_and(code, S - 1)
            both = slice((b * K + k) * S, (b * K + k + 1) * S)
            place[:, both] = jnp.where(rows_iota(S, S) == slots, 1.0, 0.0).astype(BF16)
            bins = lax.shift_right_logical(code[0:K], 7)
            mask[b, :, lanes] = jnp.where(rows_iota(K, S) == bins, 1.0, 0.0)

    arrived(pos_copies)

    unit = []
    for b in range(2):
        codes = nbr_ref[0, b]
        which = lax.shift_right_logical(codes, 7)
        slot = lax.bitwise_and(codes, S - 1)
        step_x = lax.shift_right_logical(which * 11, 5)
        step_y = which - 3 * step_x
        far = [jnp.zeros((K, S), F32)] * 4
        for c in range(9):
            source = (c // 3) * 4 + b + c % 3
            chosen = which == c
            for d in range(4):
                row = jnp.broadcast_to(pos[source, d : d + 1, :], (K, S))
                taken = jnp.take_along_axis(row, slot, axis=1, mode="promise_in_bounds")
                far[d] = jnp.where(chosen, taken, far[d])
        near = [pos[5 + b, d : d + 1, :] for d in range(3)]
        delta_x = ((step_x - 1).astype(F32) + far[0] - near[0]) * bin_width
        delta_y = ((step_y - 1).astype(F32) + far[1] - near[1]) * bin_width
        delta_z = (far[2] - near[2]) * slab_height
        distance = jnp.sqrt(delta_x * delta_x + delta_y * delta_y + delta_z * delta_z + softening)
        ux = delta_x / distance
        uy = delta_y / distance
        uz = delta_z / distance
        unit.append((distance, ux, uy, uz))
        q1 = distance * (1.0 / cutoff)
        q2 = q1 * q1
        q4 = q2 * q2
        inside = q1 < 1.0
        env = jnp.where(inside, 1.0 + q4 * q1 * (-21.0 + q1 * (35.0 - 15.0 * q1)), 0.0)
        denv = jnp.where(
            inside, q4 * (-105.0 + q1 * (210.0 - 105.0 * q1)) * (1.0 / cutoff), 0.0
        )
        values = [
            R3 * ux,
            R3 * uy,
            R3 * uz,
            R15 * ux * uy,
            R15 * uy * uz,
            0.5 * R5 * (2.0 * uz * uz - ux * ux - uy * uy),
            R15 * ux * uz,
            0.5 * R15 * (ux * ux - uy * uy),
            distance,
            env,
            denv,
            far[3],
        ]
        for m, value in enumerate(values):
            for k in range(K):
                yb[b * 8 + k // 2, m, :, (k % 2) * S : (k % 2 + 1) * S] = jnp.broadcast_to(
                    value[k : k + 1, :], (8, S)
                )

    centers = rows_iota(NB, W).astype(F32) * (cutoff / (NB - 1))

    def stacked(value):
        b1, b2, b3 = pieces(value, 3)
        return jnp.concatenate([b1, b2, b1, b3, b2, b1], axis=0).astype(BF16)

    def hidden_blocks(t, want_value, want_slope, beside):
        def block(q):
            beside(q)
            weight = lin[t * HR : (t + 1) * HR, :]
            if t == 0:
                offset = yb[q, 8] - centers
                scaled = offset * (1.0 / spread_width)
                basis = jnp.exp(-(scaled * scaled))
                if want_value:
                    base[0, q] = stacked(basis)
                if want_slope:
                    base[1, q] = stacked(basis * (offset * (-2.0 / (spread_width * spread_width))))
            pre = jnp.dot(weight, base[0, q], preferred_element_type=F32)
            if want_slope:
                dpre = jnp.dot(weight, base[1, q], preferred_element_type=F32)
            env16 = jnp.concatenate([yb[q, 9], yb[q, 9]], axis=0)
            denv16 = jnp.concatenate([yb[q, 10], yb[q, 10]], axis=0)
            for r in range(HR // 16):
                rows = slice(r * 16, (r + 1) * 16)
                x = pre[rows]
                sig = 1.0 / (1.0 + jnp.exp(-x))
                h = x * sig
                found = []
                if want_value:
                    found.append((0, env16 * h))
                if want_slope:
                    dh = (sig + h * (1.0 - sig)) * dpre[rows]
                    found.append((1, denv16 * h + env16 * dh))
                for v, value in found:
                    v = v * 2 if t else v
                    high, low = pieces(value, 2)
                    high = high.astype(BF16)
                    xs[v, q, r * 16 : (r + 1) * 16, :] = high
                    xs[v, q, HR + r * 16 : HR + (r + 1) * 16, :] = low.astype(BF16)
                    xs[v, q, 2 * HR + r * 16 : 2 * HR + (r + 1) * 16, :] = high

        blocks(Q, 4, block)

    def radial_block(t, units, target):
        def block(q):
            target[q] = jnp.dot(wst[t], xs[units, q], preferred_element_type=F32)

        return block

    def element_block(q):
        element = yb[q, 11].astype(jnp.int32) - 1
        element = jnp.concatenate([element] * (S // 8), axis=0)
        choice = jnp.where(rows_iota(S, W) == element, 1.0, 0.0).astype(BF16)
        choice = jnp.concatenate([choice, choice], axis=0)
        hup0[q] = jnp.dot(tab[...], choice, preferred_element_type=F32)

    def gather_block(begin_bin, end_bin):
        part = slice(begin_bin * S, end_bin * S)

        def block(q):
            lanes = slice(q * W, q * W + W)
            if not isinstance(q, int):
                lanes = pl.ds(pl.multiple_of(q * W, W), W)
            both = jnp.dot(hl[q // 8, :, part], hot[part, lanes], preferred_element_type=F32)
            value = both[0:C] + both[C:]
            hup1[q] = value if begin_bin == 0 else hup1[q] + value

        return block

    def split_rim(begin_bin, end_bin):
        seen = {}
        for b in range(2):
            for n in range(begin_bin, end_bin):
                c = ORDER[b][n]
                source = (c // 3) * 4 + b + c % 3
                if source not in seen:
                    high, low = pieces(rim[source], 2)
                    seen[source] = jnp.concatenate([high, low], axis=0).astype(BF16)
                hl[b, :, n * S : (n + 1) * S] = seen[source]

    def moment_block(t, q):
        b = q // 8
        for ct in range(C // 8):
            rows = slice(ct * 8, ct * 8 + 8)
            rows1 = slice(C + ct * 8, C + ct * 8 + 8)
            rows2 = slice(2 * C + ct * 8, 2 * C + ct * 8 + 8)
            sums = [mom[t, b, m, rows, :] for m in range(9)]
            for half in range(2):
                lanes = slice(half * S, half * S + S)
                h = hup[t][q, rows, lanes]
                sums[0] = sums[0] + rad[t][q, rows, lanes] * h
                h1 = rad[t][q, rows1, lanes] * h
                h2 = rad[t][q, rows2, lanes] * h
                for m in range(3):
                    sums[1 + m] = sums[1 + m] + yb[q, m, :, lanes] * h1
                for m in range(3, 8):
                    sums[1 + m] = sums[1 + m] + yb[q, m, :, lanes] * h2
            for m in range(9):
                mom[t, b, m, rows, :] = sums[m]

    def invariants(t):
        inv0 = jnp.concatenate([mom[t, b, 0] for b in range(2)], axis=1) * message_scale
        inv1 = jnp.concatenate(
            [sum(mom[t, b, m] * mom[t, b, m] for m in range(1, 4)) for b in range(2)], axis=1
        )
        inv2 = jnp.concatenate(
            [sum(mom[t, b, m] * mom[t, b, m] for m in range(4, 9)) for b in range(2)], axis=1
        )
        scale = message_scale * message_scale
        return jnp.concatenate([inv0, inv1 * scale, inv2 * scale], axis=0)

    def energies(t, values):
        column = read_column(t)
        return jnp.concatenate(
            [
                jnp.sum(values[:, b * S : (b + 1) * S] * column, axis=0, keepdims=True)
                for b in range(2)
            ],
            axis=1,
        )

    hidden_blocks(0, True, False, element_block)
    step = radial_block(0, 0, rad0)
    step(0)
    step(1)
    for q in range(Q):
        if q + 2 < Q:
            step(q + 2)
        moment_block(0, q)
    mixed = product(mix_w[...], jnp.concatenate([begin[...], invariants(0)], axis=0))
    first = mixed[0:C] * filled
    own_up = mixed[C:] * filled
    rim[5] = own_up[:, 0:S]
    rim[6] = own_up[:, S:]
    halves = [pl.ds(0, C // 2), pl.ds(C // 2, C // 2)]
    y_copies = [
        [
            remote(rim.at[5, half], rim.at[7, half], down),
            remote(rim.at[6, half], rim.at[4, half], up),
        ]
        for half in halves
    ]
    straight = [remote(rim.at[5 + odd], rim.at[far_base + 3 - 3 * odd], corner_dev)]
    x_copies = [
        remote(rim.at[pl.ds(5, 2)], rim.at[pl.ds(far_base + 1, 2)], far_dev),
        remote(rim.at[pl.ds(5, 2)], rim.at[pl.ds(near_base + 1, 2)], near_dev),
    ]
    first_ref[...] = first

    first_energy = energies(0, first)
    hidden_blocks(0, False, True, lambda q: None)
    hidden_blocks(1, True, True, radial_block(0, 1, drad0))
    far_copies = []
    for half, group in zip(halves, y_copies):
        arrived(group)
        far_copies += [
            remote(rim.at[4 + 3 * odd, half], rim.at[far_base + 3 * odd, half], far_dev),
            remote(rim.at[4, half], rim.at[near_base, half], near_dev),
            remote(rim.at[7, half], rim.at[near_base + 3, half], near_dev),
        ]
    split_rim(0, 3)
    blocks(Q, 8, gather_block(0, 3))
    def product_block(q):
        b = q // 8
        for ct in range(C // 8):
            rows = slice(ct * 8, ct * 8 + 8)
            rows1 = slice(C + ct * 8, C + ct * 8 + 8)
            rows2 = slice(2 * C + ct * 8, 2 * C + ct * 8 + 8)
            own = [mom[0, b, 1 + m, rows, :] for m in range(8)]
            for half in range(2):
                lanes = slice(half * S, half * S + S)
                y = [yb[q, m, :, lanes] for m in range(8)]
                h = hup0[q, rows, lanes]
                b1 = sum(y[m] * own[m] for m in range(3)) * h
                b2 = sum(y[m] * own[m] for m in range(3, 8)) * h
                h1 = rad0[q, rows1, lanes] * h
                h2 = rad0[q, rows2, lanes] * h
                drad0[q, rows, lanes] = drad0[q, rows, lanes] * h
                drad0[q, rows1, lanes] = drad0[q, rows1, lanes] * b1
                drad0[q, rows2, lanes] = drad0[q, rows2, lanes] * b2
                hup0[q, rows, lanes] = h1
                rad0[q, rows, lanes] = h2

    def second_radial(q):
        rad1[q] = jnp.dot(wst[1], xs[0, q], preferred_element_type=F32)
        drad1[q] = jnp.dot(wst[1], xs[2, q], preferred_element_type=F32)

    blocks(Q, Q, second_radial)
    arrived(x_copies)
    split_rim(3, 7)
    blocks(Q, 8, gather_block(3, 7))
    arrived(straight + far_copies)

    split_rim(7, 9)

    step = gather_block(7, 9)
    step(0)
    step(1)
    for q in range(Q):
        if q + 2 < Q:
            step(q + 2)
        moment_block(1, q)
    for b in range(2):
        lanes = slice(b * S, (b + 1) * S)
        gmom[b, 0] = inner1_ref[0:C, lanes] * message_scale
        scale = 2.0 * message_scale * message_scale
        for m in range(1, 9):
            rows = slice(C, 2 * C) if m < 4 else slice(2 * C, 3 * C)
            gmom[b, m] = inner1_ref[rows, lanes] * mom[1, b, m] * scale

    def feature_block(q):
        b = q // 8
        for ct in range(C // 16):
            rows = slice(ct * 16, ct * 16 + 16)
            rows1 = slice(C + ct * 16, C + ct * 16 + 16)
            rows2 = slice(2 * C + ct * 16, 2 * C + ct * 16 + 16)
            grads = [gmom[b, m, rows, :] for m in range(9)]
            for half in range(2):
                lanes = slice(half * S, half * S + S)
                spread = [jnp.concatenate([yb[q, m, :, lanes]] * 2, axis=0) for m in range(8)]
                a1 = sum(spread[m] * grads[1 + m] for m in range(3))
                a2 = sum(spread[m] * grads[1 + m] for m in range(3, 8))
                value = (
                    rad1[q, rows, lanes] * grads[0]
                    + rad1[q, rows1, lanes] * a1
                    + rad1[q, rows2, lanes] * a2
                )
                rad1[q, rows, lanes] = a1
                a2_ref[q, rows, lanes] = a2
                high, low = pieces(value, 2)
                target = pl.ds(pl.multiple_of(q * W + half * S, S), S)
                dhl[rows, target] = high.astype(BF16)
                dhl[C + ct * 16 : C + ct * 16 + 16, target] = low.astype(BF16)

    blocks(Q, 2, feature_block)

    def scatter(begin_bin, end_bin):
        found = {}
        for b in range(2):
            lanes = slice(b * K * S, (b + 1) * K * S)
            both = nt(dhl[:, lanes], hot[begin_bin * S : end_bin * S, lanes])
            value = both[0:C] + both[C:]
            for n in range(begin_bin, end_bin):
                c = ORDER[b][n]
                source = (c // 3) * 4 + b + c % 3
                piece = value[:, (n - begin_bin) * S : (n - begin_bin + 1) * S]
                found[source] = found[source] + piece if source in found else piece
        for source, value in found.items():
            rgrad[source] = value

    scatter(7, 9)
    corner_copies = [
        [
            remote(rgrad.at[near_base + 3 - 3 * odd, half], far_in.at[half], far_dev),
            remote(rgrad.at[far_base, half], near_in.at[0, half], near_dev),
            remote(rgrad.at[far_base + 3, half], near_in.at[1, half], near_dev),
        ]
        for half in halves
    ]
    back_straight = [remote(rgrad.at[near_base + 3 * odd], corner_in, corner_dev)]
    scatter(3, 7)
    side_copies = [
        remote(rgrad.at[pl.ds(near_base + 1, 2)], side_in.at[0], far_dev),
        remote(rgrad.at[pl.ds(far_base + 1, 2)], side_in.at[1], near_dev),
    ]
    scatter(0, 3)

    def reduce_send(phase, value):
        ar_out[phase] = value
        ar_in[phase, digits[phase]] = value
        return [
            remote(ar_out.at[phase], ar_in.at[phase, digits[phase]], partner(phase, step))
            for step in (1, 2, 3)
        ]

    def reduce_wait(phase, copies):
        arrived(copies)
        return (ar_in[phase, 0] + ar_in[phase, 1]) + (ar_in[phase, 2] + ar_in[phase, 3])

    second_inputs = jnp.concatenate([invariants(1), first_ref[...]], axis=0)
    atom_energy = first_energy + jnp.sum(inner1_ref[...] * second_inputs, axis=0, keepdims=True)
    for b in range(2):
        energy_ref[0, b : b + 1, :] = atom_energy[:, b * S : (b + 1) * S]
    pair = atom_energy[:, 0:S] + atom_energy[:, S:]
    reduced = reduce_send(0, jnp.broadcast_to(jnp.sum(pair, axis=1, keepdims=True), (8, S)))

    def position_block(q):
        b = q // 8
        sums = [[jnp.zeros((8, S), F32)] * 9 for _ in range(2)]
        for ct in range(C // 8):
            rows = slice(ct * 8, ct * 8 + 8)
            rows1 = slice(C + ct * 8, C + ct * 8 + 8)
            rows2 = slice(2 * C + ct * 8, 2 * C + ct * 8 + 8)
            grads = [gmom[b, m, rows, :] for m in range(9)]
            for half in range(2):
                lanes = slice(half * S, half * S + S)
                a1 = rad1[q, rows, lanes]
                a2 = a2_ref[q, rows, lanes]
                h = hup1[q, rows, lanes]
                h1 = rad1[q, rows1, lanes] * h
                h2 = rad1[q, rows2, lanes] * h
                slope = (
                    drad1[q, rows, lanes] * grads[0]
                    + drad1[q, rows1, lanes] * a1
                    + drad1[q, rows2, lanes] * a2
                )
                now = sums[half]
                now[8] = now[8] + slope * h
                for m in range(3):
                    now[m] = now[m] + grads[1 + m] * h1
                for m in range(3, 8):
                    now[m] = now[m] + grads[1 + m] * h2
        for half in range(2):
            k = (q - b * 8) * 2 + half
            for m in range(9):
                edge[b, m, pl.ds(k, 1), :] = jnp.sum(sums[half][m], axis=0, keepdims=True)

    blocks(Q // 2, 2, position_block)
    row_copies = []
    for half, group in zip((slice(0, C // 2), slice(C // 2, C)), corner_copies):
        arrived(group)
        rgrad[4, half] = rgrad[4, half] + near_in[0, half]
        rgrad[7, half] = rgrad[7, half] + near_in[1, half]
        rgrad[4 + 3 * odd, half] = rgrad[4 + 3 * odd, half] + far_in[half]
        window = pl.ds(half.start, C // 2)
        row_copies += [
            remote(rgrad.at[4, window], gy_in.at[0, window], down),
            remote(rgrad.at[7, window], gy_in.at[1, window], up),
        ]

    blocks(Q // 2, 2, position_block, Q // 2)
    reduced = reduce_send(1, reduce_wait(0, reduced))


    blocks(Q, 1, product_block)
    direct = jnp.concatenate([read_column(0)] * 2, axis=1) + inner1_ref[3 * C :]
    inner1_ref[0 : 3 * C] = product(back_w[0, 0 : 3 * C], direct * filled)

    arrived(back_straight + side_copies)
    rgrad[5 + odd] = rgrad[5 + odd] + corner_in[...]
    own_low = rgrad[5] + side_in[0, 0] + side_in[1, 0]
    own_high = rgrad[6] + side_in[0, 1] + side_in[1, 1]
    arrived(row_copies)
    returned = jnp.concatenate([own_low + gy_in[1], own_high + gy_in[0]], axis=1)

    inner0 = inner1_ref[0 : 3 * C] + product(up_w[...], returned) * filled
    scale = 2.0 * message_scale * message_scale
    for b in range(2):
        lanes = slice(b * S, (b + 1) * S)
        one = inner0[C : 2 * C, lanes] * scale
        two = inner0[2 * C :, lanes] * scale
        comb[b, 0] = inner0[0:C, lanes] * message_scale
        comb[b, 1] = one
        comb[b, 2] = two
        for m in range(1, 9):
            gmom[b, m] = (one if m < 4 else two) * mom[0, b, m]
    reduced = reduce_send(2, reduce_wait(1, reduced))

    def first_block(q):
        b = q // 8
        sums = [[jnp.zeros((8, S), F32)] * 9 for _ in range(2)]
        for ct in range(C // 8):
            rows = slice(ct * 8, ct * 8 + 8)
            rows1 = slice(C + ct * 8, C + ct * 8 + 8)
            rows2 = slice(2 * C + ct * 8, 2 * C + ct * 8 + 8)
            grads = [gmom[b, 1 + m, rows, :] for m in range(8)]
            ends = [comb[b, m, rows, :] for m in range(3)]
            for half in range(2):
                lanes = slice(half * S, half * S + S)
                now = sums[half]
                now[8] = now[8] + (
                    drad0[q, rows, lanes] * ends[0]
                    + drad0[q, rows1, lanes] * ends[1]
                    + drad0[q, rows2, lanes] * ends[2]
                )
                h1 = hup0[q, rows, lanes]
                h2 = rad0[q, rows, lanes]
                for m in range(3):
                    now[m] = now[m] + grads[m] * h1
                for m in range(3, 8):
                    now[m] = now[m] + grads[m] * h2
        for half in range(2):
            k = (q - b * 8) * 2 + half
            for m in range(9):
                total = jnp.sum(sums[half][m], axis=0, keepdims=True)
                edge[b, m, pl.ds(k, 1), :] = edge[b, m, pl.ds(k, 1), :] + total

    blocks(Q, 4, first_block)
    reduced = reduce_send(3, reduce_wait(2, reduced))

    direct_force = []
    for b in range(2):
        distance, ux, uy, uz = unit[b]
        dy = [edge[b, m] for m in range(9)]
        gux = R3 * dy[0] + R15 * (uy * dy[3] + uz * dy[6] + ux * dy[7]) - R5 * ux * dy[5]
        guy = R3 * dy[1] + R15 * (ux * dy[3] + uz * dy[4] - uy * dy[7]) - R5 * uy * dy[5]
        guz = R3 * dy[2] + R15 * (uy * dy[4] + ux * dy[6]) + (2.0 * R5) * uz * dy[5]
        slope = dy[8]
        along = ux * gux + uy * guy + uz * guz
        grads = [
            (g - u * along) / distance + u * slope for g, u in ((gux, ux), (guy, uy), (guz, uz))
        ]
        direct_force.append([jnp.sum(g, axis=0, keepdims=True) for g in grads])
        columns = []
        for k in range(K):
            here = mask[b, :, k * S : (k + 1) * S]
            stack = [here * jnp.broadcast_to(g[k : k + 1, :], (K, S)) for g in grads]
            stack = pieces(jnp.concatenate(stack, axis=0), 2)
            columns.append(jnp.concatenate(stack, axis=0).astype(BF16))
        total = nt(jnp.concatenate(columns, axis=1), place[:, b * K * S : (b + 1) * K * S])
        total = total[0 : 3 * K] + total[3 * K :]
        for c in range(9):
            source = (c // 3) * 4 + b + c % 3
            for d in range(3):
                row = total[d * K + c : d * K + c + 1, :]
                if b == 0 or c % 3 == 2:
                    pgrad[source, d : d + 1, :] = row
                else:
                    pgrad[source, d : d + 1, :] = pgrad[source, d : d + 1, :] + row
    for source in range(12):
        pgrad[source, 3:8, :] = jnp.zeros((5, S), F32)
    back_copies = [
        remote(pgrad.at[0], pg_in.at[6], left_down),
        remote(pgrad.at[3], pg_in.at[7], left_up),
        remote(pgrad.at[8], pg_in.at[8], right_down),
        remote(pgrad.at[11], pg_in.at[9], right_up),
        remote(pgrad.at[pl.ds(1, 2)], pg_in.at[pl.ds(0, 2)], left),
        remote(pgrad.at[pl.ds(9, 2)], pg_in.at[pl.ds(2, 2)], right),
        remote(pgrad.at[4], pg_in.at[4], down),
        remote(pgrad.at[7], pg_in.at[5], up),
    ]
    for copy in made[: -len(back_copies)]:
        copy.wait_send()
    total_ref[...] = reduce_wait(3, reduced)[0:1, 0:1]
    arrived(back_copies)
    low_grad = pgrad[5] + pg_in[0] + pg_in[2] + pg_in[5] + pg_in[7] + pg_in[9]
    high_grad = pgrad[6] + pg_in[1] + pg_in[3] + pg_in[4] + pg_in[6] + pg_in[8]
    for b, returned in enumerate((low_grad, high_grad)):
        for d in range(3):
            force_ref[d, 0, b : b + 1, :] = direct_force[b][d] - returned[d : d + 1, :]
    for copy in back_copies:
        copy.wait_send()


def finish(*refs):
    copies = [pltpu.make_async_copy(refs[n], refs[n + 3], refs[6].at[n]) for n in range(3)]
    for copy in copies:
        copy.start()
    for copy in copies:
        copy.wait()


def on_device(shape, *arguments):
    vmem = pl.BlockSpec(memory_space=pltpu.VMEM)
    anywhere = pl.BlockSpec(memory_space=pl.ANY)
    forces, energy, total = pl.pallas_call(
        functools.partial(kernel, shape),
        out_shape=(
            jax.ShapeDtypeStruct((3, 1, 2, S), F32),
            jax.ShapeDtypeStruct((1, 2, S), F32),
            jax.ShapeDtypeStruct((1, 1), F32),
        ),
        in_specs=[anywhere] * 10,
        out_specs=(vmem, vmem, vmem),
        scratch_shapes=[pltpu.VMEM(dims, kind) for _, dims, kind in SCRATCH]
        + [
            pltpu.SemaphoreType.DMA((COPIES,)),
            pltpu.SemaphoreType.DMA((COPIES,)),
            pltpu.SemaphoreType.DMA((len(INPUTS),)),
        ],
        compiler_params=pltpu.CompilerParams(
            collective_id=0, has_side_effects=True, vmem_limit_bytes=62 * 1024 * 1024
        ),
    )(*arguments)
    outputs = pl.pallas_call(
        finish,
        out_shape=[jax.ShapeDtypeStruct(x.shape, F32) for x in (forces, energy, total)],
        in_specs=[anywhere] * 3,
        out_specs=[anywhere] * 3,
        scratch_shapes=[pltpu.SemaphoreType.DMA((3,))],
    )(forces, energy, total)
    return outputs[0], outputs[1], outputs[2].reshape(())


def solution(mesh):
    placed = (
        P(None, "gx", "gy", None),
        P("gx", "gy", None),
        P("gx", "gy", None, None),
        P(),
        P(),
        P(),
        P(),
        P(),
        P(),
        P(),
    )
    return jax.shard_map(
        functools.partial(on_device, (mesh.shape["gx"], mesh.shape["gy"])),
        mesh=mesh,
        in_specs=placed,
        out_specs=(P(None, "gx", "gy", None), P("gx", "gy", None), P()),
        check_vma=False,
    )
```

```python
import functools
import math

import jax
import jax.numpy as jnp
from jax import lax
from jax.experimental import pallas as pl
from jax.experimental.pallas import tpu as pltpu
from jax.sharding import PartitionSpec as P

bin_width = 6.0
slab_height = 12.0
cutoff = 6.0
softening = 0.25
spread_width = 0.75
message_scale = 1.5

S = 128
C = 128
K = 16
HR = 64
NB = 8
NSPEC = 89
ORDER = ((3, 4, 5, 1, 2, 7, 8, 0, 6), (3, 4, 5, 0, 1, 6, 7, 2, 8))
Q = 16
W = 256
MESH = pl.DeviceIdType.MESH
F32 = jnp.float32
BF16 = jnp.bfloat16
HIGH = lax.Precision.HIGHEST
R3 = math.sqrt(3.0)
R5 = math.sqrt(5.0)
R15 = math.sqrt(15.0)


def exact(a, b):
    return jnp.dot(a, b, precision=HIGH, preferred_element_type=F32)


def pieces(x, count):
    parts = []
    for _ in range(count):
        part = x.astype(BF16).astype(F32)
        parts.append(part)
        x = x - part
    return parts


def wide(weight):
    high, low = pieces(weight, 2)
    return jnp.concatenate([high, high, low], axis=1).astype(BF16)


def tall(value):
    high, low = pieces(value, 2)
    return jnp.concatenate([high, low, high], axis=0).astype(BF16)


def product(weight, value):
    return jnp.dot(weight, tall(value), preferred_element_type=F32)


def blocks(count, unroll, step, start=0):
    def several(i, carry):
        for u in range(unroll):
            step(start + i * unroll + u)
        return carry

    if unroll == count:
        several(0, 0)
    else:
        lax.fori_loop(0, count // unroll, several, 0)


def nt(a, b):
    return lax.dot_general(a, b, (((1,), (1,)), ((), ())), preferred_element_type=F32)


def rows_iota(rows, cols):
    return lax.broadcasted_iota(jnp.int32, (rows, cols), 0)


SCRATCH = (
    ("pos", (12, 8, S), F32),
    ("hot", (9 * S, 2 * K * S), BF16),
    ("place", (S, 2 * K * S), BF16),
    ("mask", (2, K, K * S), F32),
    ("yb", (Q, 12, 8, W), F32),
    ("base", (2, Q, 6 * NB, W), BF16),
    ("xs", (3, Q, 3 * HR, W), BF16),
    ("rad0", (Q, 3 * C, W), F32),
    ("rad1", (Q, 3 * C, W), F32),
    ("drad0", (Q, 3 * C, W), F32),
    ("drad1", (Q, 3 * C, W), F32),
    ("hup0", (Q, C, W), F32),
    ("hup1", (Q, C, W), F32),
    ("mom", (2, 2, 9, C, S), F32),
    ("gmom", (2, 9, C, S), F32),
    ("comb", (2, 3, C, S), F32),
    ("rim", (12, C, S), F32),
    ("hl", (2, 2 * C, 9 * S), BF16),
    ("dhl", (2 * C, 2 * K * S), BF16),
    ("rgrad", (12, C, S), F32),
    ("side_in", (2, 2, C, S), F32),
    ("near_in", (2, C, S), F32),
    ("far_in", (C, S), F32),
    ("corner_in", (C, S), F32),
    ("gy_in", (2, C, S), F32),
    ("edge", (2, 9, K, S), F32),
    ("pgrad", (12, 8, S), F32),
    ("pg_in", (10, 8, S), F32),
    ("wst", (2, 3 * C, 3 * HR), BF16),
    ("lin", (2 * HR, 6 * NB), BF16),
    ("tab", (C, 2 * S), BF16),
    ("mix_w", (2 * C, 12 * C), BF16),
    ("back_w", (2, 4 * C, 3 * C), BF16),
    ("up_w", (3 * C, 3 * C), BF16),
    ("emb_t", (3 * C, S), BF16),
    ("pad", (S, S), F32),
    ("first", (C, 2 * S), F32),
    ("begin", (C, 2 * S), F32),
    ("inner1", (4 * C, 2 * S), F32),
    ("ar_out", (4, 8, S), F32),
    ("ar_in", (4, 4, 8, S), F32),
    ("a2", (Q, C, W), F32),
    ("frac_ref", (3, 1, 2, S), F32),
    ("spec_ref", (1, 2, S), jnp.int32),
    ("nbr_ref", (1, 2, K, S), jnp.int32),
    ("emb_ref", (NSPEC, C), F32),
    ("up_ref", (2, C, C), F32),
    ("rin_ref", (2, NB, HR), F32),
    ("rout_ref", (2, HR, 3 * C), F32),
    ("self_ref", (2, C, C), F32),
    ("prod_ref", (2, 3 * C, C), F32),
    ("read_ref", (2, C), F32),
)
INPUTS = ("nbr_ref", "frac_ref", "spec_ref", "emb_ref", "up_ref", "rin_ref", "rout_ref", "self_ref", "prod_ref", "read_ref")
COPIES = 72


def kernel(shape, frac_in, spec_in, nbr_in, *refs):
    inputs, refs = (nbr_in, frac_in, spec_in) + refs[:7], refs[7:]
    force_ref, energy_ref, total_ref = refs[:3]
    send_sem, recv_sem, load_sem = refs[-3:]
    scr = dict(zip([name for name, _, _ in SCRATCH], refs[3:-3]))
    (
        pos, hot, place, mask, yb, base, xs, rad0, rad1, drad0, drad1, hup0, hup1, mom, gmom, comb, rim, hl, dhl, rgrad,
        side_in, near_in, far_in, corner_in, gy_in, edge, pgrad, pg_in, wst, lin, tab, mix_w, back_w, up_w, emb_t, pad, first_ref,
        begin, inner1_ref, ar_out, ar_in, a2_ref, frac_ref, spec_ref, nbr_ref, emb_ref,
        up_ref, rin_ref, rout_ref, self_ref, prod_ref, read_ref,
    ) = [scr[name] for name, _, _ in SCRATCH]
    rad = (rad0, rad1)
    hup = (hup0, hup1)
    gxn, gyn = shape
    gx = lax.axis_index("gx")
    gy = lax.axis_index("gy")
    left = (lax.rem(gx + gxn - 1, gxn), gy)
    right = (lax.rem(gx + 1, gxn), gy)
    down = (gx, lax.rem(gy + gyn - 1, gyn))
    up = (gx, lax.rem(gy + 1, gyn))
    left_down, left_up = (left[0], down[1]), (left[0], up[1])
    right_down, right_up = (right[0], down[1]), (right[0], up[1])
    around = [left, right, down, up, left_down, left_up, right_down, right_up]
    core = lax.rem(gx, 2)
    odd = lax.rem(gx // 2, 2)
    near_dev = (gx + 1 - 2 * core, gy)
    far_dev = (lax.rem(gx + gxn - 1 + 2 * core, gxn), gy)
    corner_dev = (far_dev[0], lax.rem(gy + gyn - 1 + 2 * odd, gyn))
    near_base = 8 * core
    far_base = 8 - near_base
    digits = [gy, lax.rem(gx, 4), lax.rem(gx // 4, 4), gx // 16]

    def partner(phase, step):
        other = lax.rem(digits[phase] + step, 4)
        if phase == 0:
            return (gx, other)
        return (gx + (other - digits[phase]) * 4 ** (phase - 1), gy)

    barrier = pltpu.get_barrier_semaphore()
    greeted = around + [partner(phase, step) for phase in range(4) for step in (1, 2, 3)]
    for device in greeted:
        pl.semaphore_signal(barrier, inc=1, device_id=device, device_id_type=MESH)
    loads = [
        pltpu.make_async_copy(source, scr[name], load_sem.at[n])
        for n, (source, name) in enumerate(zip(inputs, INPUTS))
    ]
    for load in loads:
        load.start()

    made = []

    def remote(source, target, device):
        number = len(made)
        copy = pltpu.make_async_remote_copy(
            src_ref=source,
            dst_ref=target,
            send_sem=send_sem.at[number],
            recv_sem=recv_sem.at[number],
            device_id=device,
            device_id_type=MESH,
        )
        made.append(copy)
        copy.start()
        return copy

    def arrived(copies):
        for copy in copies:
            copy.wait_recv()

    for load in loads[:3]:
        load.wait()

    pos[5:7] = jnp.zeros((2, 8, S), F32)
    for b in range(2):
        for d in range(3):
            pos[5 + b, d : d + 1, :] = frac_ref[d, 0, b : b + 1, :]
        pos[5 + b, 3:4, :] = spec_ref[0, b : b + 1, :].astype(F32)

    def hot_rows(b):
        def block(k, carry):
            code = nbr_ref[0, b, pl.ds(k, 1), :]
            lanes = pl.ds(pl.multiple_of((b * K + k) * S, S), S)
            for n, c in enumerate(ORDER[b]):
                match = rows_iota(S, S) == jnp.broadcast_to(code - c * S, (S, S))
                hot[n * S : (n + 1) * S, lanes] = jnp.where(match, 1.0, 0.0).astype(BF16)
            return carry

        lax.fori_loop(0, K, block, 0)

    hot_rows(0)

    for load in loads[3:]:
        load.wait()

    def radial_weights(t):
        w1, w2 = pieces(rout_ref[t], 2)
        wst[t] = jnp.concatenate([w1, w1, w2], axis=0).T.astype(BF16)

    def back_weights(t):
        back_w[t] = wide(jnp.concatenate([prod_ref[t], self_ref[t]], axis=0))

    def read_column(t):
        return jnp.broadcast_to(read_ref[t : t + 1, :], (C, C)).T

    pl.semaphore_wait(barrier, len(greeted))
    pos_copies = [
        remote(pos.at[5], pos.at[11], left_down),
        remote(pos.at[6], pos.at[8], left_up),
        remote(pos.at[5], pos.at[3], right_down),
        remote(pos.at[6], pos.at[0], right_up),
        remote(pos.at[pl.ds(5, 2)], pos.at[pl.ds(9, 2)], left),
        remote(pos.at[pl.ds(5, 2)], pos.at[pl.ds(1, 2)], right),
        remote(pos.at[5], pos.at[7], down),
        remote(pos.at[6], pos.at[4], up),
    ]

    hot_rows(1)
    for t in range(2):
        w1, w2, w3 = pieces(rin_ref[t], 3)
        stack = jnp.concatenate([w1, w1, w2, w1, w2, w3], axis=0)
        pad[...] = jnp.zeros_like(pad)
        pad[0 : 6 * NB, 0:HR] = stack
        lin[t * HR : (t + 1) * HR, :] = pad[...].T[0:HR, 0 : 6 * NB].astype(BF16)
    pad[...] = jnp.zeros_like(pad)
    pad[0:NSPEC, :] = emb_ref[...]
    table = exact(pad[...], up_ref[0])
    tab[...] = jnp.concatenate(pieces(table.T, 2), axis=1).astype(BF16)
    for t in range(2):
        radial_weights(t)
        back_weights(t)
    mix = jnp.concatenate([self_ref[0], prod_ref[0]], axis=0)
    mix_up = exact(mix, up_ref[1])
    mix_w[0:C] = wide(mix.T)
    mix_w[C:] = wide(mix_up.T)
    up_w[...] = wide(mix_up[C:])
    filled = jnp.where(
        jnp.concatenate([pos[5 + b, 3:4, :] for b in range(2)], axis=1) > 0.0, 1.0, 0.0
    )
    inner1_ref[...] = product(back_w[1], jnp.concatenate([read_column(1)] * 2, axis=1) * filled)
    emb_t[...] = jnp.concatenate(pieces(pad[...].T, 3), axis=0).astype(BF16)
    own_element = jnp.concatenate([pos[5 + b, 3:4, :] for b in range(2)], axis=1)
    own_hot = jnp.where(
        rows_iota(S, 2 * S) == jnp.broadcast_to(own_element.astype(jnp.int32) - 1, (S, 2 * S)),
        1.0,
        0.0,
    ).astype(BF16)
    value = jnp.dot(emb_t[...], own_hot, preferred_element_type=F32)
    begin[...] = value[0:C] + value[C : 2 * C] + value[2 * C :]
    mom[...] = jnp.zeros_like(mom)
    edge[...] = jnp.zeros_like(edge)
    for b in range(2):
        for k in range(K):
            lanes = slice(k * S, (k + 1) * S)
            code = jnp.broadcast_to(nbr_ref[0, b, k : k + 1, :], (S, S))
            slots = lax.bitwise_and(code, S - 1)
            both = slice((b * K + k) * S, (b * K + k + 1) * S)
            place[:, both] = jnp.where(rows_iota(S, S) == slots, 1.0, 0.0).astype(BF16)
            bins = lax.shift_right_logical(code[0:K], 7)
            mask[b, :, lanes] = jnp.where(rows_iota(K, S) == bins, 1.0, 0.0)

    arrived(pos_copies)

    unit = []
    for b in range(2):
        codes = nbr_ref[0, b]
        which = lax.shift_right_logical(codes, 7)
        slot = lax.bitwise_and(codes, S - 1)
        step_x = lax.shift_right_logical(which * 11, 5)
        step_y = which - 3 * step_x
        far = [jnp.zeros((K, S), F32)] * 4
        for c in range(9):
            source = (c // 3) * 4 + b + c % 3
            chosen = which == c
            for d in range(4):
                row = jnp.broadcast_to(pos[source, d : d + 1, :], (K, S))
                taken = jnp.take_along_axis(row, slot, axis=1, mode="promise_in_bounds")
                far[d] = jnp.where(chosen, taken, far[d])
        near = [pos[5 + b, d : d + 1, :] for d in range(3)]
        delta_x = ((step_x - 1).astype(F32) + far[0] - near[0]) * bin_width
        delta_y = ((step_y - 1).astype(F32) + far[1] - near[1]) * bin_width
        delta_z = (far[2] - near[2]) * slab_height
        distance = jnp.sqrt(delta_x * delta_x + delta_y * delta_y + delta_z * delta_z + softening)
        ux = delta_x / distance
        uy = delta_y / distance
        uz = delta_z / distance
        unit.append((distance, ux, uy, uz))
        q1 = distance * (1.0 / cutoff)
        q2 = q1 * q1
        q4 = q2 * q2
        inside = q1 < 1.0
        env = jnp.where(inside, 1.0 + q4 * q1 * (-21.0 + q1 * (35.0 - 15.0 * q1)), 0.0)
        denv = jnp.where(
            inside, q4 * (-105.0 + q1 * (210.0 - 105.0 * q1)) * (1.0 / cutoff), 0.0
        )
        values = [
            R3 * ux,
            R3 * uy,
            R3 * uz,
            R15 * ux * uy,
            R15 * uy * uz,
            0.5 * R5 * (2.0 * uz * uz - ux * ux - uy * uy),
            R15 * ux * uz,
            0.5 * R15 * (ux * ux - uy * uy),
            distance,
            env,
            denv,
            far[3],
        ]
        for m, value in enumerate(values):
            for k in range(K):
                yb[b * 8 + k // 2, m, :, (k % 2) * S : (k % 2 + 1) * S] = jnp.broadcast_to(
                    value[k : k + 1, :], (8, S)
                )

    centers = rows_iota(NB, W).astype(F32) * (cutoff / (NB - 1))

    def stacked(value):
        b1, b2, b3 = pieces(value, 3)
        return jnp.concatenate([b1, b2, b1, b3, b2, b1], axis=0).astype(BF16)

    def hidden_blocks(t, want_value, want_slope, beside):
        def block(q):
            beside(q)
            weight = lin[t * HR : (t + 1) * HR, :]
            if t == 0:
                offset = yb[q, 8] - centers
                scaled = offset * (1.0 / spread_width)
                basis = jnp.exp(-(scaled * scaled))
                if want_value:
                    base[0, q] = stacked(basis)
                if want_slope:
                    base[1, q] = stacked(basis * (offset * (-2.0 / (spread_width * spread_width))))
            pre = jnp.dot(weight, base[0, q], preferred_element_type=F32)
            if want_slope:
                dpre = jnp.dot(weight, base[1, q], preferred_element_type=F32)
            env16 = jnp.concatenate([yb[q, 9], yb[q, 9]], axis=0)
            denv16 = jnp.concatenate([yb[q, 10], yb[q, 10]], axis=0)
            for r in range(HR // 16):
                rows = slice(r * 16, (r + 1) * 16)
                x = pre[rows]
                sig = 1.0 / (1.0 + jnp.exp(-x))
                h = x * sig
                found = []
                if want_value:
                    found.append((0, env16 * h))
                if want_slope:
                    dh = (sig + h * (1.0 - sig)) * dpre[rows]
                    found.append((1, denv16 * h + env16 * dh))
                for v, value in found:
                    v = v * 2 if t else v
                    high, low = pieces(value, 2)
                    high = high.astype(BF16)
                    xs[v, q, r * 16 : (r + 1) * 16, :] = high
                    xs[v, q, HR + r * 16 : HR + (r + 1) * 16, :] = low.astype(BF16)
                    xs[v, q, 2 * HR + r * 16 : 2 * HR + (r + 1) * 16, :] = high

        blocks(Q, 8, block)

    def radial_block(t, units, target):
        def block(q):
            target[q] = jnp.dot(wst[t], xs[units, q], preferred_element_type=F32)

        return block

    def element_block(q):
        element = yb[q, 11].astype(jnp.int32) - 1
        element = jnp.concatenate([element] * (S // 8), axis=0)
        choice = jnp.where(rows_iota(S, W) == element, 1.0, 0.0).astype(BF16)
        choice = jnp.concatenate([choice, choice], axis=0)
        hup0[q] = jnp.dot(tab[...], choice, preferred_element_type=F32)

    def gather_block(begin_bin, end_bin):
        part = slice(begin_bin * S, end_bin * S)

        def block(q):
            lanes = slice(q * W, q * W + W)
            if not isinstance(q, int):
                lanes = pl.ds(pl.multiple_of(q * W, W), W)
            both = jnp.dot(hl[q // 8, :, part], hot[part, lanes], preferred_element_type=F32)
            value = both[0:C] + both[C:]
            hup1[q] = value if begin_bin == 0 else hup1[q] + value

        return block

    def split_rim(begin_bin, end_bin):
        seen = {}
        for b in range(2):
            for n in range(begin_bin, end_bin):
                c = ORDER[b][n]
                source = (c // 3) * 4 + b + c % 3
                if source not in seen:
                    high, low = pieces(rim[source], 2)
                    seen[source] = jnp.concatenate([high, low], axis=0).astype(BF16)
                hl[b, :, n * S : (n + 1) * S] = seen[source]

    def moment_block(t, q):
        b = q // 8
        for ct in range(C // 8):
            rows = slice(ct * 8, ct * 8 + 8)
            rows1 = slice(C + ct * 8, C + ct * 8 + 8)
            rows2 = slice(2 * C + ct * 8, 2 * C + ct * 8 + 8)
            sums = [mom[t, b, m, rows, :] for m in range(9)]
            for half in range(2):
                lanes = slice(half * S, half * S + S)
                h = hup[t][q, rows, lanes]
                sums[0] = sums[0] + rad[t][q, rows, lanes] * h
                h1 = rad[t][q, rows1, lanes] * h
                h2 = rad[t][q, rows2, lanes] * h
                for m in range(3):
                    sums[1 + m] = sums[1 + m] + yb[q, m, :, lanes] * h1
                for m in range(3, 8):
                    sums[1 + m] = sums[1 + m] + yb[q, m, :, lanes] * h2
            for m in range(9):
                mom[t, b, m, rows, :] = sums[m]

    def invariants(t):
        inv0 = jnp.concatenate([mom[t, b, 0] for b in range(2)], axis=1) * message_scale
        inv1 = jnp.concatenate(
            [sum(mom[t, b, m] * mom[t, b, m] for m in range(1, 4)) for b in range(2)], axis=1
        )
        inv2 = jnp.concatenate(
            [sum(mom[t, b, m] * mom[t, b, m] for m in range(4, 9)) for b in range(2)], axis=1
        )
        scale = message_scale * message_scale
        return jnp.concatenate([inv0, inv1 * scale, inv2 * scale], axis=0)

    def energies(t, values):
        column = read_column(t)
        return jnp.concatenate(
            [
                jnp.sum(values[:, b * S : (b + 1) * S] * column, axis=0, keepdims=True)
                for b in range(2)
            ],
            axis=1,
        )

    hidden_blocks(0, True, False, element_block)
    step = radial_block(0, 0, rad0)
    step(0)
    step(1)
    for q in range(Q):
        if q + 2 < Q:
            step(q + 2)
        moment_block(0, q)
    mixed = product(mix_w[...], jnp.concatenate([begin[...], invariants(0)], axis=0))
    first = mixed[0:C] * filled
    own_up = mixed[C:] * filled
    rim[5] = own_up[:, 0:S]
    rim[6] = own_up[:, S:]
    halves = [pl.ds(0, C // 2), pl.ds(C // 2, C // 2)]
    y_copies = [
        [
            remote(rim.at[5, half], rim.at[7, half], down),
            remote(rim.at[6, half], rim.at[4, half], up),
        ]
        for half in halves
    ]
    straight = [remote(rim.at[5 + odd], rim.at[far_base + 3 - 3 * odd], corner_dev)]
    x_copies = [
        remote(rim.at[pl.ds(5, 2)], rim.at[pl.ds(far_base + 1, 2)], far_dev),
        remote(rim.at[pl.ds(5, 2)], rim.at[pl.ds(near_base + 1, 2)], near_dev),
    ]
    first_ref[...] = first

    first_energy = energies(0, first)
    hidden_blocks(0, False, True, lambda q: None)
    hidden_blocks(1, True, True, radial_block(0, 1, drad0))
    far_copies = []
    for half, group in zip(halves, y_copies):
        arrived(group)
        far_copies += [
            remote(rim.at[4 + 3 * odd, half], rim.at[far_base + 3 * odd, half], far_dev),
            remote(rim.at[4, half], rim.at[near_base, half], near_dev),
            remote(rim.at[7, half], rim.at[near_base + 3, half], near_dev),
        ]
    split_rim(0, 3)
    blocks(Q, Q, gather_block(0, 3))
    def product_block(q):
        b = q // 8
        for ct in range(C // 8):
            rows = slice(ct * 8, ct * 8 + 8)
            rows1 = slice(C + ct * 8, C + ct * 8 + 8)
            rows2 = slice(2 * C + ct * 8, 2 * C + ct * 8 + 8)
            own = [mom[0, b, 1 + m, rows, :] for m in range(8)]
            for half in range(2):
                lanes = slice(half * S, half * S + S)
                y = [yb[q, m, :, lanes] for m in range(8)]
                h = hup0[q, rows, lanes]
                b1 = sum(y[m] * own[m] for m in range(3)) * h
                b2 = sum(y[m] * own[m] for m in range(3, 8)) * h
                h1 = rad0[q, rows1, lanes] * h
                h2 = rad0[q, rows2, lanes] * h
                drad0[q, rows, lanes] = drad0[q, rows, lanes] * h
                drad0[q, rows1, lanes] = drad0[q, rows1, lanes] * b1
                drad0[q, rows2, lanes] = drad0[q, rows2, lanes] * b2
                hup0[q, rows, lanes] = h1
                rad0[q, rows, lanes] = h2

    def second_radial(q):
        rad1[q] = jnp.dot(wst[1], xs[0, q], preferred_element_type=F32)

    blocks(Q, Q, second_radial)
    arrived(x_copies)
    split_rim(3, 7)
    blocks(Q, Q, gather_block(3, 7))
    arrived(straight + far_copies)

    split_rim(7, 9)

    step = gather_block(7, 9)
    step(0)
    step(1)
    for q in range(Q):
        if q + 2 < Q:
            step(q + 2)
        moment_block(1, q)
    for b in range(2):
        lanes = slice(b * S, (b + 1) * S)
        gmom[b, 0] = inner1_ref[0:C, lanes] * message_scale
        scale = 2.0 * message_scale * message_scale
        for m in range(1, 9):
            rows = slice(C, 2 * C) if m < 4 else slice(2 * C, 3 * C)
            gmom[b, m] = inner1_ref[rows, lanes] * mom[1, b, m] * scale

    def feature_block(q):
        b = q // 8
        for ct in range(C // 16):
            rows = slice(ct * 16, ct * 16 + 16)
            rows1 = slice(C + ct * 16, C + ct * 16 + 16)
            rows2 = slice(2 * C + ct * 16, 2 * C + ct * 16 + 16)
            grads = [gmom[b, m, rows, :] for m in range(9)]
            for half in range(2):
                lanes = slice(half * S, half * S + S)
                spread = [jnp.concatenate([yb[q, m, :, lanes]] * 2, axis=0) for m in range(8)]
                a1 = sum(spread[m] * grads[1 + m] for m in range(3))
                a2 = sum(spread[m] * grads[1 + m] for m in range(3, 8))
                value = (
                    rad1[q, rows, lanes] * grads[0]
                    + rad1[q, rows1, lanes] * a1
                    + rad1[q, rows2, lanes] * a2
                )
                rad1[q, rows, lanes] = a1
                a2_ref[q, rows, lanes] = a2
                high, low = pieces(value, 2)
                target = pl.ds(pl.multiple_of(q * W + half * S, S), S)
                dhl[rows, target] = high.astype(BF16)
                dhl[C + ct * 16 : C + ct * 16 + 16, target] = low.astype(BF16)

    blocks(Q, 2, feature_block)

    def scatter(begin_bin, end_bin):
        found = {}
        for b in range(2):
            lanes = slice(b * K * S, (b + 1) * K * S)
            both = nt(dhl[:, lanes], hot[begin_bin * S : end_bin * S, lanes])
            value = both[0:C] + both[C:]
            for n in range(begin_bin, end_bin):
                c = ORDER[b][n]
                source = (c // 3) * 4 + b + c % 3
                piece = value[:, (n - begin_bin) * S : (n - begin_bin + 1) * S]
                found[source] = found[source] + piece if source in found else piece
        for source, value in found.items():
            rgrad[source] = value

    scatter(7, 9)
    corner_copies = [
        [
            remote(rgrad.at[near_base + 3 - 3 * odd, half], far_in.at[half], far_dev),
            remote(rgrad.at[far_base, half], near_in.at[0, half], near_dev),
            remote(rgrad.at[far_base + 3, half], near_in.at[1, half], near_dev),
        ]
        for half in halves
    ]
    back_straight = [remote(rgrad.at[near_base + 3 * odd], corner_in, corner_dev)]
    scatter(3, 7)
    side_copies = [
        remote(rgrad.at[pl.ds(near_base + 1, 2)], side_in.at[0], far_dev),
        remote(rgrad.at[pl.ds(far_base + 1, 2)], side_in.at[1], near_dev),
    ]
    scatter(0, 3)

    def reduce_send(phase, value):
        ar_out[phase] = value
        ar_in[phase, digits[phase]] = value
        return [
            remote(ar_out.at[phase], ar_in.at[phase, digits[phase]], partner(phase, step))
            for step in (1, 2, 3)
        ]

    def reduce_wait(phase, copies):
        arrived(copies)
        return (ar_in[phase, 0] + ar_in[phase, 1]) + (ar_in[phase, 2] + ar_in[phase, 3])

    second_inputs = jnp.concatenate([invariants(1), first_ref[...]], axis=0)
    atom_energy = first_energy + jnp.sum(inner1_ref[...] * second_inputs, axis=0, keepdims=True)
    for b in range(2):
        energy_ref[0, b : b + 1, :] = atom_energy[:, b * S : (b + 1) * S]
    pair = atom_energy[:, 0:S] + atom_energy[:, S:]
    reduced = reduce_send(0, jnp.broadcast_to(jnp.sum(pair, axis=1, keepdims=True), (8, S)))
    blocks(Q, Q, radial_block(1, 2, drad1))

    def position_block(q):
        b = q // 8
        sums = [[jnp.zeros((8, S), F32)] * 9 for _ in range(2)]
        for ct in range(C // 8):
            rows = slice(ct * 8, ct * 8 + 8)
            rows1 = slice(C + ct * 8, C + ct * 8 + 8)
            rows2 = slice(2 * C + ct * 8, 2 * C + ct * 8 + 8)
            grads = [gmom[b, m, rows, :] for m in range(9)]
            for half in range(2):
                lanes = slice(half * S, half * S + S)
                a1 = rad1[q, rows, lanes]
                a2 = a2_ref[q, rows, lanes]
                h = hup1[q, rows, lanes]
                h1 = rad1[q, rows1, lanes] * h
                h2 = rad1[q, rows2, lanes] * h
                slope = (
                    drad1[q, rows, lanes] * grads[0]
                    + drad1[q, rows1, lanes] * a1
                    + drad1[q, rows2, lanes] * a2
                )
                now = sums[half]
                now[8] = now[8] + slope * h
                for m in range(3):
                    now[m] = now[m] + grads[1 + m] * h1
                for m in range(3, 8):
                    now[m] = now[m] + grads[1 + m] * h2
        for half in range(2):
            k = (q - b * 8) * 2 + half
            for m in range(9):
                edge[b, m, pl.ds(k, 1), :] = jnp.sum(sums[half][m], axis=0, keepdims=True)

    blocks(Q // 2, 2, position_block)
    row_copies = []
    for half, group in zip((slice(0, C // 2), slice(C // 2, C)), corner_copies):
        arrived(group)
        rgrad[4, half] = rgrad[4, half] + near_in[0, half]
        rgrad[7, half] = rgrad[7, half] + near_in[1, half]
        rgrad[4 + 3 * odd, half] = rgrad[4 + 3 * odd, half] + far_in[half]
        window = pl.ds(half.start, C // 2)
        row_copies += [
            remote(rgrad.at[4, window], gy_in.at[0, window], down),
            remote(rgrad.at[7, window], gy_in.at[1, window], up),
        ]

    blocks(Q // 2, 2, position_block, Q // 2)
    reduced = reduce_send(1, reduce_wait(0, reduced))


    blocks(Q, 1, product_block)
    direct = jnp.concatenate([read_column(0)] * 2, axis=1) + inner1_ref[3 * C :]
    inner1_ref[0 : 3 * C] = product(back_w[0, 0 : 3 * C], direct * filled)

    arrived(back_straight + side_copies)
    rgrad[5 + odd] = rgrad[5 + odd] + corner_in[...]
    own_low = rgrad[5] + side_in[0, 0] + side_in[1, 0]
    own_high = rgrad[6] + side_in[0, 1] + side_in[1, 1]
    arrived(row_copies)
    returned = jnp.concatenate([own_low + gy_in[1], own_high + gy_in[0]], axis=1)

    inner0 = inner1_ref[0 : 3 * C] + product(up_w[...], returned) * filled
    scale = 2.0 * message_scale * message_scale
    for b in range(2):
        lanes = slice(b * S, (b + 1) * S)
        one = inner0[C : 2 * C, lanes] * scale
        two = inner0[2 * C :, lanes] * scale
        comb[b, 0] = inner0[0:C, lanes] * message_scale
        comb[b, 1] = one
        comb[b, 2] = two
        for m in range(1, 9):
            gmom[b, m] = (one if m < 4 else two) * mom[0, b, m]
    reduced = reduce_send(2, reduce_wait(1, reduced))

    def first_block(q):
        b = q // 8
        sums = [[jnp.zeros((8, S), F32)] * 9 for _ in range(2)]
        for ct in range(C // 8):
            rows = slice(ct * 8, ct * 8 + 8)
            rows1 = slice(C + ct * 8, C + ct * 8 + 8)
            rows2 = slice(2 * C + ct * 8, 2 * C + ct * 8 + 8)
            grads = [gmom[b, 1 + m, rows, :] for m in range(8)]
            ends = [comb[b, m, rows, :] for m in range(3)]
            for half in range(2):
                lanes = slice(half * S, half * S + S)
                now = sums[half]
                now[8] = now[8] + (
                    drad0[q, rows, lanes] * ends[0]
                    + drad0[q, rows1, lanes] * ends[1]
                    + drad0[q, rows2, lanes] * ends[2]
                )
                h1 = hup0[q, rows, lanes]
                h2 = rad0[q, rows, lanes]
                for m in range(3):
                    now[m] = now[m] + grads[m] * h1
                for m in range(3, 8):
                    now[m] = now[m] + grads[m] * h2
        for half in range(2):
            k = (q - b * 8) * 2 + half
            for m in range(9):
                total = jnp.sum(sums[half][m], axis=0, keepdims=True)
                edge[b, m, pl.ds(k, 1), :] = edge[b, m, pl.ds(k, 1), :] + total

    blocks(Q, 4, first_block)
    reduced = reduce_send(3, reduce_wait(2, reduced))

    direct_force = []
    for b in range(2):
        distance, ux, uy, uz = unit[b]
        dy = [edge[b, m] for m in range(9)]
        gux = R3 * dy[0] + R15 * (uy * dy[3] + uz * dy[6] + ux * dy[7]) - R5 * ux * dy[5]
        guy = R3 * dy[1] + R15 * (ux * dy[3] + uz * dy[4] - uy * dy[7]) - R5 * uy * dy[5]
        guz = R3 * dy[2] + R15 * (uy * dy[4] + ux * dy[6]) + (2.0 * R5) * uz * dy[5]
        slope = dy[8]
        along = ux * gux + uy * guy + uz * guz
        grads = [
            (g - u * along) / distance + u * slope for g, u in ((gux, ux), (guy, uy), (guz, uz))
        ]
        direct_force.append([jnp.sum(g, axis=0, keepdims=True) for g in grads])
        columns = []
        for k in range(K):
            here = mask[b, :, k * S : (k + 1) * S]
            stack = [here * jnp.broadcast_to(g[k : k + 1, :], (K, S)) for g in grads]
            stack = pieces(jnp.concatenate(stack, axis=0), 2)
            columns.append(jnp.concatenate(stack, axis=0).astype(BF16))
        total = nt(jnp.concatenate(columns, axis=1), place[:, b * K * S : (b + 1) * K * S])
        total = total[0 : 3 * K] + total[3 * K :]
        for c in range(9):
            source = (c // 3) * 4 + b + c % 3
            for d in range(3):
                row = total[d * K + c : d * K + c + 1, :]
                if b == 0 or c % 3 == 2:
                    pgrad[source, d : d + 1, :] = row
                else:
                    pgrad[source, d : d + 1, :] = pgrad[source, d : d + 1, :] + row
    for source in range(12):
        pgrad[source, 3:8, :] = jnp.zeros((5, S), F32)
    back_copies = [
        remote(pgrad.at[0], pg_in.at[6], left_down),
        remote(pgrad.at[3], pg_in.at[7], left_up),
        remote(pgrad.at[8], pg_in.at[8], right_down),
        remote(pgrad.at[11], pg_in.at[9], right_up),
        remote(pgrad.at[pl.ds(1, 2)], pg_in.at[pl.ds(0, 2)], left),
        remote(pgrad.at[pl.ds(9, 2)], pg_in.at[pl.ds(2, 2)], right),
        remote(pgrad.at[4], pg_in.at[4], down),
        remote(pgrad.at[7], pg_in.at[5], up),
    ]
    for copy in made[: -len(back_copies)]:
        copy.wait_send()
    total_ref[...] = reduce_wait(3, reduced)[0:1, 0:1]
    arrived(back_copies)
    low_grad = pgrad[5] + pg_in[0] + pg_in[2] + pg_in[5] + pg_in[7] + pg_in[9]
    high_grad = pgrad[6] + pg_in[1] + pg_in[3] + pg_in[4] + pg_in[6] + pg_in[8]
    for b, returned in enumerate((low_grad, high_grad)):
        for d in range(3):
            force_ref[d, 0, b : b + 1, :] = direct_force[b][d] - returned[d : d + 1, :]
    for copy in back_copies:
        copy.wait_send()


def finish(*refs):
    copies = [pltpu.make_async_copy(refs[n], refs[n + 3], refs[6].at[n]) for n in range(3)]
    for copy in copies:
        copy.start()
    for copy in copies:
        copy.wait()


def on_device(shape, *arguments):
    vmem = pl.BlockSpec(memory_space=pltpu.VMEM)
    anywhere = pl.BlockSpec(memory_space=pl.ANY)
    forces, energy, total = pl.pallas_call(
        functools.partial(kernel, shape),
        out_shape=(
            jax.ShapeDtypeStruct((3, 1, 2, S), F32),
            jax.ShapeDtypeStruct((1, 2, S), F32),
            jax.ShapeDtypeStruct((1, 1), F32),
        ),
        in_specs=[anywhere] * 10,
        out_specs=(vmem, vmem, vmem),
        scratch_shapes=[pltpu.VMEM(dims, kind) for _, dims, kind in SCRATCH]
        + [
            pltpu.SemaphoreType.DMA((COPIES,)),
            pltpu.SemaphoreType.DMA((COPIES,)),
            pltpu.SemaphoreType.DMA((len(INPUTS),)),
        ],
        compiler_params=pltpu.CompilerParams(
            collective_id=0, has_side_effects=True, vmem_limit_bytes=62 * 1024 * 1024
        ),
    )(*arguments)
    outputs = pl.pallas_call(
        finish,
        out_shape=[jax.ShapeDtypeStruct(x.shape, F32) for x in (forces, energy, total)],
        in_specs=[anywhere] * 3,
        out_specs=[anywhere] * 3,
        scratch_shapes=[pltpu.SemaphoreType.DMA((3,))],
    )(forces, energy, total)
    return outputs[0], outputs[1], outputs[2].reshape(())


def solution(mesh):
    placed = (
        P(None, "gx", "gy", None),
        P("gx", "gy", None),
        P("gx", "gy", None, None),
        P(),
        P(),
        P(),
        P(),
        P(),
        P(),
        P(),
    )
    return jax.shard_map(
        functools.partial(on_device, (mesh.shape["gx"], mesh.shape["gy"])),
        mesh=mesh,
        in_specs=placed,
        out_specs=(P(None, "gx", "gy", None), P("gx", "gy", None), P()),
        check_vma=False,
    )
```
